32 devices in a mesh: seq: 8 (over z, y), kvh: 4 (over x, core).
Axes of the slice: x: 2, y: 2, z: 4, core: 2. Of those that a mesh axis runs over, the one named last changes fastest.
Arguments:
- queries: bfloat16 [1024, 2560], P('seq', 'kvh'), may hold values from -7 to 7
- keys: bfloat16 [1024, 512], P(('seq', 'kvh')), may hold values from -6 to 6
- values: bfloat16 [1024, 512], P(('seq', 'kvh')), may hold values from -6 to 6
- d_out: bfloat16 [1024, 2560], P('seq', 'kvh'), may hold values from -6 to 6
- slab_order: int32 [16], replicated, may hold values from 0 to 15, as said below
Outputs:
- query_grads: bfloat16 [1024, 2560], P('seq', 'kvh')
- key_grads: bfloat16 [1024, 512], P(('seq', 'kvh'))
- value_grads: bfloat16 [1024, 512], P(('seq', 'kvh'))
The draws below stay inside these ranges and needn't reach their ends.
Inputs may be any that keep to these rules, and one draw needn't show every extreme that they name: `slab_order`: each number 0 to 15 appears once; slots 2 d and 2 d + 1 hold the slabs c and 15 - c for some c, in either order.
All inputs are finite; a program needn't handle non-finite values.
Results may differ from the reference program's by a relative error of at most 0.015.
Values may be sent and summed in bfloat16 or wider, within the bound.
No kernel may reach another device: no remote copies, remote signals or barrier semaphores. Data moves between devices by JAX's collectives and lax.ppermute only.
A program may use at most 64 MiB of HBM per device.

```python
import math
import jax
import jax.numpy as jnp
from jax import lax

HEADS = 20
KV_HEADS = 4
HEAD = 128
TOKENS = 1024
SLAB = 64
SLABS = 16


def order_of(base_key):
    half_count = SLABS // 2
    pair_ids = jax.random.permutation(jax.random.fold_in(base_key, 11), half_count).astype(jnp.int32)
    flip_bits = jax.random.randint(jax.random.fold_in(base_key, 12), (half_count,), 0, 2)
    lower = pair_ids
    upper = SLABS - 1 - pair_ids
    first_slab = jnp.where(flip_bits == 1, upper, lower)
    second_slab = jnp.where(flip_bits == 1, lower, upper)
    return jnp.stack([first_slab, second_slab], axis=1).reshape(SLABS).astype(jnp.int32)


def draw_slab_order(key, part):
    return order_of(key)


def draw_keys(key, part):
    result = jnp.clip(jax.random.normal(jax.random.fold_in(key, 33), (TOKENS, KV_HEADS * HEAD), jnp.float32), -4.0, 4.0)
    return result.astype(jnp.bfloat16)


def draw_queries(key, part):
    result = jnp.clip(jax.random.normal(jax.random.fold_in(key, 43), (TOKENS, HEADS * HEAD), jnp.float32), -4.0, 4.0)
    return result.astype(jnp.bfloat16)


def block_levels(stream_key, extent, shards, smallest, high):
    loudness = 1.0
    for axis_at, parts in shards:
        draws = jax.random.uniform(jax.random.fold_in(jax.random.fold_in(stream_key, 6), axis_at), (parts,), jnp.float32, smallest / len(shards), high / len(shards))
        loudness = loudness * jnp.repeat(jnp.exp(draws), extent[axis_at] // parts).reshape((-1,) + (1,) * (len(extent) - 1 - axis_at))
    return loudness


def bell_draw(key, shape, deviation, reach, pieces=(), kind=jnp.bfloat16):
    values = jax.random.normal(key, shape, jnp.float32) * deviation
    if len(pieces) > 0:
        values = block_levels(key, shape, pieces, -0.22, 0.18) * values
    return jnp.clip(values, min=-reach, max=reach).astype(kind)


def setup_inputs(seed: int = 0) -> dict:
    seeds = jax.random.split(jax.random.key(seed), 6)
    return {
        "queries": draw_queries(jax.random.fold_in(seeds[5], 71), 0),
        "keys": draw_keys(jax.random.fold_in(seeds[5], 71), 0),
        "values": bell_draw(seeds[2], (TOKENS, KV_HEADS * HEAD), 1.0, 6.0, ((0, 32),)),
        "d_out": bell_draw(seeds[3], (TOKENS, HEADS * HEAD), 1.0, 6.0, ((0, 8), (1, 4))),
        "slab_order": draw_slab_order(jax.random.fold_in(seeds[5], 71), 0),
    }


def rounded_result(array_in):
    return lax.optimization_barrier(array_in.astype(jnp.bfloat16)).astype(jnp.float32)


def reference(queries, keys, values, d_out, slab_order):
    group_size = HEADS // KV_HEADS
    softmax_scale = HEAD ** -0.5
    highest_position = lax.Precision.HIGHEST
    slab_ids = jnp.arange(SLABS, dtype=jnp.int32)
    slot_of_slab = jnp.sum(jnp.where(slab_order[None, :] == slab_ids[:, None], slab_ids[None, :], 0), axis=1).astype(jnp.int32)
    inside = jnp.arange(SLAB, dtype=jnp.int32)
    row_of_pos = (slot_of_slab[:, None] * SLAB + inside[None, :]).reshape(TOKENS).astype(jnp.int32)
    pos_of_row = (slab_order[:, None] * SLAB + inside[None, :]).reshape(TOKENS).astype(jnp.int32)
    query_sorted = jnp.take(queries, row_of_pos, axis=0).astype(jnp.float32).reshape(TOKENS, KV_HEADS, group_size, HEAD)
    grad_sorted = jnp.take(d_out, row_of_pos, axis=0).astype(jnp.float32).reshape(TOKENS, KV_HEADS, group_size, HEAD)
    key_sorted = jnp.take(keys, row_of_pos, axis=0).astype(jnp.float32).reshape(TOKENS, KV_HEADS, HEAD)
    value_sorted = jnp.take(values, row_of_pos, axis=0).astype(jnp.float32).reshape(TOKENS, KV_HEADS, HEAD)
    block_rows = math.gcd(512, TOKENS)
    key_gradient_total = jnp.zeros((TOKENS, KV_HEADS, HEAD), jnp.float32)
    value_gradient_total = jnp.zeros((TOKENS, KV_HEADS, HEAD), jnp.float32)
    query_portions = []
    for block_index in range(TOKENS // block_rows):
        first_row = block_index * block_rows
        key_upper_limit = first_row + block_rows
        query_block_slice = query_sorted[first_row:key_upper_limit]
        gradient_tile_block = grad_sorted[first_row:key_upper_limit]
        key_block_slice = key_sorted[:key_upper_limit]
        value_block_slice = value_sorted[:key_upper_limit]
        logit_scores = jnp.einsum("uiyh,mih->iyum", query_block_slice, key_block_slice, precision=highest_position) * softmax_scale
        allowed = jnp.arange(key_upper_limit)[None, :] <= (first_row + jnp.arange(block_rows))[:, None]
        logit_scores = jnp.where(allowed, logit_scores, -jnp.inf)
        row_max = jnp.max(logit_scores, axis=-1, keepdims=True)
        expon = jnp.exp(logit_scores - row_max)
        probs = expon / jnp.sum(expon, axis=-1, keepdims=True)
        probability_reduced = rounded_result(probs)
        attended_output = rounded_result(jnp.einsum("oiau,uoc->aoic", probability_reduced, value_block_slice, precision=highest_position))
        delta = jnp.transpose(jnp.sum(gradient_tile_block * attended_output, axis=-1), (1, 2, 0))
        probability_gradient = jnp.einsum("uiyh,mih->iyum", gradient_tile_block, value_block_slice, precision=highest_position)
        score_gradient = rounded_result(probs * (probability_gradient - delta[..., None]))
        query_portions.append(jnp.einsum("oiau,uoc->aoic", score_gradient, key_block_slice, precision=highest_position) * softmax_scale)
        key_gradient_total = key_gradient_total.at[:key_upper_limit].add(jnp.einsum("wrci,cwrx->iwx", score_gradient, query_block_slice, precision=highest_position) * softmax_scale)
        value_gradient_total = value_gradient_total.at[:key_upper_limit].add(jnp.einsum("wrci,cwrx->iwx", probability_reduced, gradient_tile_block, precision=highest_position))
    query_sorted_grads = jnp.concatenate(query_portions, axis=0).reshape(TOKENS, HEADS * HEAD)
    query_grads = jnp.take(query_sorted_grads, pos_of_row, axis=0).astype(jnp.bfloat16)
    key_grads = jnp.take(key_gradient_total.reshape(TOKENS, KV_HEADS * HEAD), pos_of_row, axis=0).astype(jnp.bfloat16)
    value_grads = jnp.take(value_gradient_total.reshape(TOKENS, KV_HEADS * HEAD), pos_of_row, axis=0).astype(jnp.bfloat16)
    return (query_grads, key_grads, value_grads)
```

```python
import functools
import math

import jax
import jax.numpy as jnp
from jax import lax
from jax.experimental import pallas as pl
from jax.experimental.pallas import tpu as pltpu
from jax.sharding import PartitionSpec as P

HEADS = 20
KV_HEADS = 4
HEAD = 128
VMEM_LIMIT = 56 * 1024 * 1024


def repeat(count, body):
    if count <= 8:
        for step in range(count):
            body(step)
    else:
        pl.loop(0, count)(body)


def pack_kernel(kvh, keys_ref, values_ref, out_ref):
    width = out_ref.shape[2] // 2
    for k in range(kvh):
        cols = slice(k * width, (k + 1) * width)
        key_part = keys_ref[:, cols]
        value_part = values_ref[:, cols]
        for s in range(out_ref.shape[0] // kvh):
            out_ref[s * kvh + k, :, :width] = key_part
            out_ref[s * kvh + k, :, width:] = value_part


def combine_kernel(kvh, terms_ref, key_ref, value_ref):
    width = terms_ref.shape[2] // 2
    seq = terms_ref.shape[0] // kvh
    for k in range(kvh):
        total = terms_ref[k].astype(jnp.float32)
        for s in range(1, seq):
            total = total + terms_ref[s * kvh + k].astype(jnp.float32)
        total = total.astype(jnp.bfloat16)
        key_ref[:, k * width : (k + 1) * width] = total[:, :width]
        value_ref[:, k * width : (k + 1) * width] = total[:, width:]


def attend_kernel(
    group,
    order_ref,
    me_ref,
    q_ref,
    do_ref,
    kv_ref,
    dq_ref,
    dkv_ref,
    slot_ref,
    qs_ref,
    ds_ref,
    kvs_ref,
    s_ref,
    dp_ref,
    m_ref,
    l_ref,
    d_ref,
    acc_ref,
    dq_acc_ref,
):
    slabs = order_ref.shape[0]
    total = kv_ref.shape[0]
    slab_rows = total // slabs
    heads = q_ref.shape[1] // HEAD
    kv_local = heads // group
    chunk_slabs = math.gcd(4, slabs)
    chunk = chunk_slabs * slab_rows
    chunks = slabs // chunk_slabs
    steps = chunks + 1
    columns = group * slab_rows
    width = kv_local * HEAD
    scale = HEAD ** (-0.5)
    exponent_scale = scale * math.log2(math.e)

    for slot in range(slabs):
        slot_ref[order_ref[slot]] = slot
    me = me_ref[0]
    first, second = order_ref[2 * me], order_ref[2 * me + 1]
    low_half = jnp.where(first < second, 0, 1)
    low_slab = jnp.minimum(first, second)
    high_slab = jnp.maximum(first, second)
    low_steps = low_slab // chunk_slabs + 1

    def sort_slab(slab):
        rows = pl.ds(pl.multiple_of(slot_ref[slab] * slab_rows, slab_rows), slab_rows)
        kvs_ref[pl.ds(pl.multiple_of(slab * slab_rows, slab_rows), slab_rows), :] = kv_ref[rows, :]

    for slab in range(slabs):
        sort_slab(slab)

    for g in range(kv_local):
        key_cols = slice(g * HEAD, (g + 1) * HEAD)
        value_cols = slice(width + g * HEAD, width + (g + 1) * HEAD)
        for half in range(2):
            side = low_half if half == 0 else 1 - low_half
            rows = pl.ds(pl.multiple_of(side * slab_rows, slab_rows), slab_rows)
            for h in range(group):
                cols = slice((g * group + h) * HEAD, (g * group + h + 1) * HEAD)
                qs_ref[half, h * slab_rows : (h + 1) * slab_rows, :] = q_ref[rows, cols]
                ds_ref[half, h * slab_rows : (h + 1) * slab_rows, :] = do_ref[rows, cols]
        m_ref[...] = jnp.full(m_ref.shape, -jnp.inf, jnp.float32)
        l_ref[...] = jnp.zeros(l_ref.shape, jnp.float32)
        d_ref[...] = jnp.zeros(d_ref.shape, jnp.float32)
        acc_ref[...] = jnp.zeros(acc_ref.shape, jnp.float32)
        dq_acc_ref[...] = jnp.zeros(dq_acc_ref.shape, jnp.float32)

        def place(step):
            is_high = jnp.where(step >= low_steps, 1, 0)
            at = jnp.where(step >= low_steps, step - low_steps, step)
            return is_high, at, pl.ds(pl.multiple_of(at * chunk, chunk), chunk)

        def score_step(step):
            half, at, rows = place(step)
            slab = jnp.where(half == 1, high_slab, low_slab)
            scores = lax.dot_general(
                kvs_ref[rows, key_cols],
                qs_ref[half],
                (((1,), (1,)), ((), ())),
                preferred_element_type=jnp.float32,
            )
            key_pos = at * chunk + lax.broadcasted_iota(jnp.int32, scores.shape, 0)
            query_pos = slab * slab_rows + lax.rem(
                lax.broadcasted_iota(jnp.int32, (1, columns), 1), slab_rows
            )
            scores = jnp.where(key_pos <= query_pos, scores, -jnp.inf)
            s_ref[step] = scores
            m_ref[half] = jnp.maximum(m_ref[half], jnp.max(scores, axis=0, keepdims=True))
            dp_ref[step] = lax.dot_general(
                kvs_ref[rows, value_cols],
                ds_ref[half],
                (((1,), (1,)), ((), ())),
                preferred_element_type=jnp.float32,
            )

        repeat(steps, score_step)

        def sum_step(step):
            half, at, rows = place(step)
            expon = jnp.exp2((s_ref[step] - m_ref[half]) * exponent_scale)
            s_ref[step] = expon
            l_ref[half] = l_ref[half] + jnp.sum(expon, axis=0, keepdims=True)
            d_ref[half] = d_ref[half] + jnp.sum(expon * dp_ref[step], axis=0, keepdims=True)

        repeat(steps, sum_step)
        inverse = 1.0 / l_ref[...]
        l_ref[...] = inverse
        d_ref[...] = d_ref[...] * inverse

        def grad_step(step):
            half, at, rows = place(step)
            probs = s_ref[step] * l_ref[half]
            score_grads = (probs * (dp_ref[step] - d_ref[half])).astype(jnp.bfloat16)
            acc_ref[rows, HEAD:] = acc_ref[rows, HEAD:] + jnp.dot(
                probs.astype(jnp.bfloat16), ds_ref[half], preferred_element_type=jnp.float32
            )
            acc_ref[rows, :HEAD] = acc_ref[rows, :HEAD] + jnp.dot(
                score_grads, qs_ref[half], preferred_element_type=jnp.float32
            )
            dq_acc_ref[half] = dq_acc_ref[half] + lax.dot_general(
                kvs_ref[rows, key_cols],
                score_grads,
                (((0,), (0,)), ((), ())),
                preferred_element_type=jnp.float32,
            )

        repeat(steps, grad_step)

        for half in range(2):
            side = low_half if half == 0 else 1 - low_half
            rows = pl.ds(pl.multiple_of(side * slab_rows, slab_rows), slab_rows)
            grads = (jnp.transpose(dq_acc_ref[half]) * scale).astype(jnp.bfloat16)
            for h in range(group):
                cols = slice((g * group + h) * HEAD, (g * group + h + 1) * HEAD)
                dq_ref[rows, cols] = grads[h * slab_rows : (h + 1) * slab_rows, :]

        def place_slab(slab):
            rows = pl.ds(pl.multiple_of(slot_ref[slab] * slab_rows, slab_rows), slab_rows)
            terms = acc_ref[pl.ds(pl.multiple_of(slab * slab_rows, slab_rows), slab_rows), :]
            dkv_ref[rows, key_cols] = (terms[:, :HEAD] * scale).astype(jnp.bfloat16)
            dkv_ref[rows, value_cols] = terms[:, HEAD:].astype(jnp.bfloat16)

        for slab in range(slabs):
            place_slab(slab)


def per_device(queries, keys, values, d_out, slab_order):
    axes = ("seq", "kvh")
    kvh = lax.axis_size("kvh")
    seq = lax.axis_size("seq")
    devices = seq * kvh
    kv_local = KV_HEADS // kvh
    group = HEADS // KV_HEADS
    local_rows, query_width = queries.shape
    cache_rows = keys.shape[0]
    slabs = slab_order.shape[0]
    slab_rows = local_rows // 2
    total = slab_rows * slabs
    width = kv_local * HEAD
    chunk_slabs = math.gcd(4, slabs)
    chunk = chunk_slabs * slab_rows
    steps = slabs // chunk_slabs + 1
    columns = group * slab_rows
    params = pltpu.CompilerParams(vmem_limit_bytes=VMEM_LIMIT)
    vmem = pl.BlockSpec(memory_space=pltpu.VMEM)
    smem = pl.BlockSpec(memory_space=pltpu.SMEM)

    packed = pl.pallas_call(
        functools.partial(pack_kernel, kvh),
        out_shape=jax.ShapeDtypeStruct((devices, cache_rows, 2 * width), keys.dtype),
        in_specs=[vmem, vmem],
        out_specs=vmem,
        compiler_params=params,
        name="pack",
    )(keys, values)
    gathered = lax.all_to_all(packed, axes, split_axis=0, concat_axis=0, tiled=True)
    gathered = gathered.reshape(total, 2 * width)

    me = lax.axis_index("seq").astype(jnp.int32).reshape(1)
    query_grads, terms = pl.pallas_call(
        functools.partial(attend_kernel, group),
        out_shape=(
            jax.ShapeDtypeStruct(queries.shape, jnp.bfloat16),
            jax.ShapeDtypeStruct((total, 2 * width), jnp.bfloat16),
        ),
        in_specs=[smem, smem, vmem, vmem, vmem],
        out_specs=(vmem, vmem),
        scratch_shapes=[
            pltpu.SMEM((slabs,), jnp.int32),
            pltpu.VMEM((2, columns, HEAD), jnp.bfloat16),
            pltpu.VMEM((2, columns, HEAD), jnp.bfloat16),
            pltpu.VMEM((total, 2 * width), jnp.bfloat16),
            pltpu.VMEM((steps, chunk, columns), jnp.float32),
            pltpu.VMEM((steps, chunk, columns), jnp.float32),
            pltpu.VMEM((2, 1, columns), jnp.float32),
            pltpu.VMEM((2, 1, columns), jnp.float32),
            pltpu.VMEM((2, 1, columns), jnp.float32),
            pltpu.VMEM((total, 2 * HEAD), jnp.float32),
            pltpu.VMEM((2, HEAD, columns), jnp.float32),
        ],
        compiler_params=params,
        name="attend",
    )(slab_order, me, queries, d_out, gathered)

    owned = lax.all_to_all(
        terms.reshape(devices, cache_rows, 2 * width), axes, split_axis=0, concat_axis=0, tiled=True
    )
    key_grads, value_grads = pl.pallas_call(
        functools.partial(combine_kernel, kvh),
        out_shape=(
            jax.ShapeDtypeStruct(keys.shape, jnp.bfloat16),
            jax.ShapeDtypeStruct(values.shape, jnp.bfloat16),
        ),
        in_specs=[vmem],
        out_specs=(vmem, vmem),
        compiler_params=params,
        name="combine",
    )(owned)
    return (query_grads, key_grads, value_grads)


def solution(mesh):
    placed = (
        P("seq", "kvh"),
        P(("seq", "kvh"), None),
        P(("seq", "kvh"), None),
        P("seq", "kvh"),
        P(),
    )
    return jax.shard_map(
        per_device,
        mesh=mesh,
        in_specs=placed,
        out_specs=(P("seq", "kvh"), P(("seq", "kvh"), None), P(("seq", "kvh"), None)),
        check_vma=False,
    )
```

```python
import functools
import math

import jax
import jax.numpy as jnp
from jax import lax
from jax.experimental import pallas as pl
from jax.experimental.pallas import tpu as pltpu
from jax.sharding import Mesh
from jax.sharding import PartitionSpec as P

HEADS = 20
KV_HEADS = 4
HEAD = 128
GROUP = HEADS // KV_HEADS
SCALE = HEAD ** (-0.5)
EXPONENT_SCALE = SCALE * math.log2(math.e)
LOWEST = -1e30
VMEM_LIMIT = 56 * 1024 * 1024
ROWS_DOT_ROWS = (((1,), (1,)), ((), ()))
COLS_DOT_COLS = (((0,), (0,)), ((), ()))


def repeat(count, body):
    if count <= 8:
        for step in range(count):
            body(step)
    else:
        pl.loop(0, count)(body)


def at_rows(start, size):
    return pl.ds(pl.multiple_of(start, size), size)


def pair_of(order_ref, index):
    first, second = order_ref[2 * index], order_ref[2 * index + 1]
    return jnp.minimum(first, second), jnp.where(first < second, 0, 1)


class Work:
    def __init__(self, order_ref, me_ref, kv_ref, ks_ref, q_refs, d_refs, qs_ref, ds_ref):
        self.slab_rows = q_refs[0].shape[0] // 2
        self.outer = kv_ref.shape[0] // (2 * self.slab_rows)
        self.order_ref = order_ref
        me = me_ref[0]
        self.at, self.side = me // 2, me % 2
        self.low = [pair_of(order_ref, me), pair_of(order_ref, me + 1 - 2 * self.side)]
        self.half_rows = self.outer * self.slab_rows
        self.chunk = math.gcd(256, self.half_rows)
        rows = self.slab_rows

        def stack_keys(j):
            _, place = pair_of(order_ref, 2 * j + self.side)
            for half in range(2):
                here = place if half == 0 else 1 - place
                ks_ref[half, at_rows(j * rows, rows), :] = kv_ref[at_rows((2 * j + here) * rows, rows), :]

        repeat(self.outer, stack_keys)
        for owner in range(2):
            for half in range(2):
                place = self.low[owner][1]
                source = at_rows((place if half == 0 else 1 - place) * rows, rows)
                for h in range(GROUP):
                    cols = slice(h * HEAD, (h + 1) * HEAD)
                    qs_ref[owner, half, h * rows : (h + 1) * rows, :] = q_refs[owner][source, cols]
                    ds_ref[owner, half, h * rows : (h + 1) * rows, :] = d_refs[owner][source, cols]

    def blocks(self, body):
        rows = self.slab_rows
        for owner in range(2):
            repeat(
                self.half_rows // self.chunk,
                lambda n: body(owner, 1, 0, n * self.chunk, self.chunk, n * self.chunk, None),
            )

            def pick(j):
                low, _ = pair_of(self.order_ref, 2 * j + self.side)
                half = jnp.where(self.low[owner][0] >= low, 0, 1)
                mask = None if owner == 1 else j == self.at
                body(owner, half, half, j * rows, rows, self.half_rows + j * rows, mask)

            repeat(self.outer, pick)
            if owner == 0:
                body(owner, 1, 1, self.at * rows, rows, 2 * self.half_rows, True)

    def scores(self, ks_ref, qs_ref, owner, q_half, k_half, first, size, mask):
        scores = lax.dot_general(
            ks_ref[k_half, at_rows(first, size), :HEAD],
            qs_ref[owner, q_half],
            ROWS_DOT_ROWS,
            preferred_element_type=jnp.float32,
        )
        if mask is not None:
            key = lax.broadcasted_iota(jnp.int32, scores.shape, 0)
            query = lax.rem(lax.broadcasted_iota(jnp.int32, (1, scores.shape[1]), 1), self.slab_rows)
            if mask is not True:
                query = query + jnp.where(mask, 0, self.slab_rows)
            scores = jnp.where(key <= query, scores, LOWEST)
        return scores

    def grads(self, ks_ref, ds_ref, owner, q_half, k_half, first, size):
        return lax.dot_general(
            ks_ref[k_half, at_rows(first, size), HEAD:],
            ds_ref[owner, q_half],
            ROWS_DOT_ROWS,
            preferred_element_type=jnp.float32,
        )


def pack_kernel(kvh, keys_ref, values_ref, out_ref):
    for k in range(kvh):
        cols = slice(k * HEAD, (k + 1) * HEAD)
        key_part = keys_ref[:, cols]
        value_part = values_ref[:, cols]
        for s in range(out_ref.shape[0] // kvh):
            out_ref[s * kvh + k, :, :HEAD] = key_part
            out_ref[s * kvh + k, :, HEAD:] = value_part


def stats_kernel(
    order_ref, me_ref, q_ref, do_ref, q2_ref, do2_ref, kv_ref, out_ref,
    ks_ref, qs_ref, ds_ref, s_ref, m_ref, l_ref, d_ref,
):
    work = Work(order_ref, me_ref, kv_ref, ks_ref, (q_ref, q2_ref), (do_ref, do2_ref), qs_ref, ds_ref)
    m_ref[...] = jnp.full(m_ref.shape, LOWEST, jnp.float32)
    l_ref[...] = jnp.zeros(l_ref.shape, jnp.float32)
    d_ref[...] = jnp.zeros(d_ref.shape, jnp.float32)

    def maximum(owner, q_half, k_half, first, size, place, mask):
        scores = work.scores(ks_ref, qs_ref, owner, q_half, k_half, first, size, mask)
        s_ref[owner, at_rows(place, size), :] = scores
        m_ref[owner, q_half] = jnp.maximum(
            m_ref[owner, q_half], jnp.max(scores, axis=0, keepdims=True)
        )

    work.blocks(maximum)

    def sums(owner, q_half, k_half, first, size, place, mask):
        grads = work.grads(ks_ref, ds_ref, owner, q_half, k_half, first, size)
        scores = s_ref[owner, at_rows(place, size), :]
        expon = jnp.exp2((scores - m_ref[owner, q_half]) * EXPONENT_SCALE)
        l_ref[owner, q_half] = l_ref[owner, q_half] + jnp.sum(expon, axis=0, keepdims=True)
        d_ref[owner, q_half] = d_ref[owner, q_half] + jnp.sum(expon * grads, axis=0, keepdims=True)

    work.blocks(sums)
    for owner in range(2):
        for half in range(2):
            base = (2 * owner + half) * 3
            out_ref[base : base + 1, :] = m_ref[owner, half]
            out_ref[base + 1 : base + 2, :] = l_ref[owner, half]
            out_ref[base + 2 : base + 3, :] = d_ref[owner, half]


def grads_kernel(
    order_ref, me_ref, q_ref, do_ref, q2_ref, do2_ref, kv_ref, mine_ref, theirs_ref,
    dq_ref, dq2_ref, dkv_ref,
    ks_ref, qs_ref, ds_ref, m_ref, d_ref, acc_ref, dq_acc_ref,
):
    work = Work(order_ref, me_ref, kv_ref, ks_ref, (q_ref, q2_ref), (do_ref, do2_ref), qs_ref, ds_ref)
    acc_ref[...] = jnp.zeros(acc_ref.shape, jnp.float32)
    dq_acc_ref[...] = jnp.zeros(dq_acc_ref.shape, jnp.float32)
    for owner in range(2):
        for half in range(2):
            base = (2 * owner + half) * 3
            base2 = (2 * (1 - owner) + half) * 3
            m1, m2 = mine_ref[base : base + 1, :], theirs_ref[base2 : base2 + 1, :]
            top = jnp.maximum(m1, m2)
            w1 = jnp.exp2((m1 - top) * EXPONENT_SCALE)
            w2 = jnp.exp2((m2 - top) * EXPONENT_SCALE)
            total = w1 * mine_ref[base + 1 : base + 2, :] + w2 * theirs_ref[base2 + 1 : base2 + 2, :]
            delta = w1 * mine_ref[base + 2 : base + 3, :] + w2 * theirs_ref[base2 + 2 : base2 + 3, :]
            m_ref[owner, half] = top * EXPONENT_SCALE + jnp.log2(total)
            d_ref[owner, half] = delta / total

    def gradients(owner, q_half, k_half, first, size, place, mask):
        scores = work.scores(ks_ref, qs_ref, owner, q_half, k_half, first, size, mask)
        grads = work.grads(ks_ref, ds_ref, owner, q_half, k_half, first, size)
        probs = jnp.exp2(scores * EXPONENT_SCALE - m_ref[owner, q_half])
        score_grads = (probs * (grads - d_ref[owner, q_half])).astype(jnp.bfloat16)
        rows = at_rows(first, size)
        acc_ref[k_half, rows, HEAD:] = acc_ref[k_half, rows, HEAD:] + jnp.dot(
            probs.astype(jnp.bfloat16), ds_ref[owner, q_half], preferred_element_type=jnp.float32
        )
        acc_ref[k_half, rows, :HEAD] = acc_ref[k_half, rows, :HEAD] + jnp.dot(
            score_grads, qs_ref[owner, q_half], preferred_element_type=jnp.float32
        )
        dq_acc_ref[owner, q_half] = dq_acc_ref[owner, q_half] + lax.dot_general(
            ks_ref[k_half, rows, :HEAD], score_grads, COLS_DOT_COLS, preferred_element_type=jnp.float32
        )

    work.blocks(gradients)
    rows = work.slab_rows
    for owner, target in ((0, dq_ref), (1, dq2_ref)):
        for half in range(2):
            place = work.low[owner][1]
            source = at_rows((place if half == 0 else 1 - place) * rows, rows)
            grads = (jnp.transpose(dq_acc_ref[owner, half]) * SCALE).astype(target.dtype)
            for h in range(GROUP):
                target[source, h * HEAD : (h + 1) * HEAD] = grads[h * rows : (h + 1) * rows, :]

    def write_terms(j):
        _, place = pair_of(order_ref, 2 * j + work.side)
        for half in range(2):
            here = place if half == 0 else 1 - place
            target = at_rows((2 * j + here) * rows, rows)
            source = at_rows(j * rows, rows)
            dkv_ref[target, :HEAD] = (acc_ref[half, source, :HEAD] * SCALE).astype(jnp.bfloat16)
            dkv_ref[target, HEAD:] = acc_ref[half, source, HEAD:].astype(jnp.bfloat16)

    repeat(work.outer, write_terms)


def combine_kernel(kvh, terms_ref, key_ref, value_ref):
    seq = terms_ref.shape[0] // kvh
    for k in range(kvh):
        total = terms_ref[k].astype(jnp.float32)
        for s in range(1, seq):
            total = total + terms_ref[s * kvh + k].astype(jnp.float32)
        total = total.astype(jnp.bfloat16)
        key_ref[:, k * HEAD : (k + 1) * HEAD] = total[:, :HEAD]
        value_ref[:, k * HEAD : (k + 1) * HEAD] = total[:, HEAD:]


def per_device(queries, keys, values, d_out, slab_order):
    axes = ("outer", "kvh")
    kvh = lax.axis_size("kvh")
    outer = lax.axis_size("outer")
    peers = outer * kvh
    local_rows, query_width = queries.shape
    cache_rows = keys.shape[0]
    slab_rows = local_rows // 2
    column_rows = outer * local_rows
    half_rows = outer * slab_rows
    columns = GROUP * slab_rows
    swap = [(0, 1), (1, 0)]
    params = pltpu.CompilerParams(vmem_limit_bytes=VMEM_LIMIT)
    vmem = pl.BlockSpec(memory_space=pltpu.VMEM)
    smem = pl.BlockSpec(memory_space=pltpu.SMEM)
    shape = jax.ShapeDtypeStruct

    queries2 = lax.ppermute(queries, "pair", swap)
    d_out2 = lax.ppermute(d_out, "pair", swap)
    packed = pl.pallas_call(
        functools.partial(pack_kernel, kvh),
        out_shape=shape((peers, cache_rows, 2 * HEAD), keys.dtype),
        in_specs=[vmem, vmem],
        out_specs=vmem,
        compiler_params=params,
        name="pack",
    )(keys, values)
    gathered = lax.all_to_all(packed, axes, split_axis=0, concat_axis=0, tiled=True)
    gathered = gathered.reshape(column_rows, 2 * HEAD)

    me = (lax.axis_index("outer") * 2 + lax.axis_index("pair")).astype(jnp.int32).reshape(1)
    stacks = [
        pltpu.VMEM((2, half_rows, 2 * HEAD), jnp.bfloat16),
        pltpu.VMEM((2, 2, columns, HEAD), jnp.bfloat16),
        pltpu.VMEM((2, 2, columns, HEAD), jnp.bfloat16),
    ]
    row_stat = pltpu.VMEM((2, 2, 1, columns), jnp.float32)
    operands = (slab_order, me, queries, d_out, queries2, d_out2, gathered)
    stats = pl.pallas_call(
        stats_kernel,
        out_shape=shape((12, columns), jnp.float32),
        in_specs=[smem, smem] + [vmem] * 5,
        out_specs=vmem,
        scratch_shapes=stacks
        + [pltpu.VMEM((2, 2 * half_rows + slab_rows, columns), jnp.float32), row_stat, row_stat, row_stat],
        compiler_params=params,
        name="stats",
    )(*operands)
    stats2 = lax.ppermute(stats, "pair", swap)
    own_grads, other_grads, terms = pl.pallas_call(
        grads_kernel,
        out_shape=(
            shape(queries.shape, jnp.float32),
            shape(queries.shape, jnp.bfloat16),
            shape((column_rows, 2 * HEAD), jnp.bfloat16),
        ),
        in_specs=[smem, smem] + [vmem] * 7,
        out_specs=(vmem, vmem, vmem),
        scratch_shapes=stacks
        + [
            row_stat,
            row_stat,
            pltpu.VMEM((2, half_rows, 2 * HEAD), jnp.float32),
            pltpu.VMEM((2, 2, HEAD, columns), jnp.float32),
        ],
        compiler_params=params,
        name="grads",
    )(*operands, stats, stats2)
    received_grads = lax.ppermute(other_grads, "pair", swap)
    owned = lax.all_to_all(
        terms.reshape(peers, cache_rows, 2 * HEAD), axes, split_axis=0, concat_axis=0, tiled=True
    )
    query_grads = (own_grads + received_grads.astype(jnp.float32)).astype(jnp.bfloat16)
    key_grads, value_grads = pl.pallas_call(
        functools.partial(combine_kernel, kvh),
        out_shape=(shape(keys.shape, jnp.bfloat16), shape(values.shape, jnp.bfloat16)),
        in_specs=[vmem],
        out_specs=(vmem, vmem),
        compiler_params=params,
        name="combine",
    )(owned)
    return (query_grads, key_grads, value_grads)


def solution(mesh):
    kvh = mesh.shape["kvh"]
    pairs = mesh.shape["seq"] // 2
    paired = Mesh(mesh.devices.reshape(pairs, 2, kvh), ("outer", "pair", "kvh"))
    seq = ("outer", "pair")
    cache = P(("outer", "pair", "kvh"), None)
    placed = (P(seq, "kvh"), cache, cache, P(seq, "kvh"), P())
    return jax.shard_map(
        per_device,
        mesh=paired,
        in_specs=placed,
        out_specs=(P(seq, "kvh"), cache, cache),
        check_vma=False,
    )
```

```python
import functools
import math

import jax
import jax.numpy as jnp
from jax import lax
from jax.experimental import pallas as pl
from jax.experimental.pallas import tpu as pltpu
from jax.sharding import Mesh
from jax.sharding import PartitionSpec as P

HEADS = 20
KV_HEADS = 4
HEAD = 128
GROUP = HEADS // KV_HEADS
SCALE = HEAD ** (-0.5)
EXPONENT_SCALE = SCALE * math.log2(math.e)
LOWEST = -1e30
ROWS_DOT_ROWS = (((1,), (1,)), ((), ()))
COLS_DOT_COLS = (((0,), (0,)), ((), ()))


def repeat(count, body):
    if count <= 8:
        for step in range(count):
            body(step)
    else:
        pl.loop(0, count)(body)


def at_rows(start, size):
    return pl.ds(pl.multiple_of(start, size), size)


def pair_of(order_ref, index):
    first, second = order_ref[2 * index], order_ref[2 * index + 1]
    return jnp.minimum(first, second), jnp.where(first < second, 0, 1)


def load(source_ref, target_ref, sem):
    copy = pltpu.make_async_copy(source_ref, target_ref, sem)
    copy.start()
    return copy


class Work:
    def __init__(self, order_ref, me_ref, kv_ref, ks_ref, sems):
        self.half_rows = ks_ref.shape[1]
        self.outer = order_ref.shape[0] // 4
        self.slab_rows = self.half_rows // self.outer
        self.order_ref = order_ref
        me = me_ref[0]
        self.at, self.side = me // 2, me % 2
        self.low = [pair_of(order_ref, me)[0], pair_of(order_ref, me + 1 - 2 * self.side)[0]]
        self.chunk = math.gcd(256, self.half_rows)
        rows = self.slab_rows

        def copies(j):
            _, place = pair_of(order_ref, 2 * j + self.side)
            for half in range(2):
                here = place if half == 0 else 1 - place
                yield pltpu.make_async_copy(
                    kv_ref.at[at_rows((2 * j + here) * rows, rows)],
                    ks_ref.at[half, at_rows(j * rows, rows)],
                    sems.at[2 * j + half],
                )

        def start(j):
            for copy in copies(j):
                copy.start()

        def wait(j):
            for copy in copies(j):
                copy.wait()

        repeat(self.outer, start)
        self.wait = lambda: repeat(self.outer, wait)

    def blocks(self, body):
        rows = self.slab_rows
        for owner in range(2):
            repeat(
                self.half_rows // self.chunk,
                lambda n: body(owner, 1, 0, n * self.chunk, self.chunk, n * self.chunk, None),
            )

            def pick(j):
                low, _ = pair_of(self.order_ref, 2 * j + self.side)
                half = jnp.where(self.low[owner] >= low, 0, 1)
                mask = None if owner == 1 else j == self.at
                body(owner, half, half, j * rows, rows, self.half_rows + j * rows, mask)

            repeat(self.outer, pick)
            if owner == 0:
                body(owner, 1, 1, self.at * rows, rows, 2 * self.half_rows, True)

    def scores(self, ks_ref, qs_ref, owner, q_half, k_half, first, size, mask):
        scores = lax.dot_general(
            ks_ref[k_half, at_rows(first, size), :HEAD],
            qs_ref[owner, q_half],
            ROWS_DOT_ROWS,
            preferred_element_type=jnp.float32,
        )
        if mask is not None:
            key = lax.broadcasted_iota(jnp.int32, scores.shape, 0)
            query = lax.rem(lax.broadcasted_iota(jnp.int32, (1, scores.shape[1]), 1), self.slab_rows)
            if mask is not True:
                query = query + jnp.where(mask, 0, self.slab_rows)
            scores = jnp.where(key <= query, scores, LOWEST)
        return scores

    def grads(self, ks_ref, ds_ref, owner, q_half, k_half, first, size):
        return lax.dot_general(
            ks_ref[k_half, at_rows(first, size), HEAD:],
            ds_ref[owner, q_half],
            ROWS_DOT_ROWS,
            preferred_element_type=jnp.float32,
        )


def pack_kernel(kvh, keys_ref, values_ref, out_ref):
    for k in range(kvh):
        cols = slice(k * HEAD, (k + 1) * HEAD)
        key_part = keys_ref[:, cols]
        value_part = values_ref[:, cols]
        for s in range(out_ref.shape[0] // kvh):
            out_ref[s * kvh + k, :, :HEAD] = key_part
            out_ref[s * kvh + k, :, HEAD:] = value_part


def stack_kernel(order_ref, me_ref, q_ref, do_ref, q2_ref, do2_ref, qs_ref, ds_ref):
    rows = q_ref.shape[0] // 2
    me = me_ref[0]
    for owner, index in ((0, me), (1, me + 1 - 2 * (me % 2))):
        _, place = pair_of(order_ref, index)
        for half in range(2):
            source = at_rows((place if half == 0 else 1 - place) * rows, rows)
            for target, parts in ((qs_ref, (q_ref, q2_ref)), (ds_ref, (do_ref, do2_ref))):
                for h in range(GROUP):
                    target[owner, half, h * rows : (h + 1) * rows, :] = parts[owner][
                        source, h * HEAD : (h + 1) * HEAD
                    ]


def stats_kernel(order_ref, me_ref, qs_ref, ds_ref, kv_ref, out_ref, ks_ref, s_ref, m_ref, l_ref, d_ref, sems):
    work = Work(order_ref, me_ref, kv_ref, ks_ref, sems)
    m_ref[...] = jnp.full(m_ref.shape, LOWEST, jnp.float32)
    l_ref[...] = jnp.zeros(l_ref.shape, jnp.float32)
    d_ref[...] = jnp.zeros(d_ref.shape, jnp.float32)
    work.wait()

    def maximum(owner, q_half, k_half, first, size, place, mask):
        scores = work.scores(ks_ref, qs_ref, owner, q_half, k_half, first, size, mask)
        s_ref[owner, at_rows(place, size), :] = scores
        m_ref[owner, q_half] = jnp.maximum(
            m_ref[owner, q_half], jnp.max(scores, axis=0, keepdims=True)
        )

    work.blocks(maximum)

    def sums(owner, q_half, k_half, first, size, place, mask):
        grads = work.grads(ks_ref, ds_ref, owner, q_half, k_half, first, size)
        scores = s_ref[owner, at_rows(place, size), :]
        expon = jnp.exp2((scores - m_ref[owner, q_half]) * EXPONENT_SCALE)
        l_ref[owner, q_half] = l_ref[owner, q_half] + jnp.sum(expon, axis=0, keepdims=True)
        d_ref[owner, q_half] = d_ref[owner, q_half] + jnp.sum(expon * grads, axis=0, keepdims=True)

    work.blocks(sums)
    for owner in range(2):
        for half in range(2):
            base = (2 * owner + half) * 3
            out_ref[base : base + 1, :] = m_ref[owner, half]
            out_ref[base + 1 : base + 2, :] = l_ref[owner, half]
            out_ref[base + 2 : base + 3, :] = d_ref[owner, half]


def grads_kernel(
    order_ref, me_ref, qs_ref, ds_ref, kv_ref, mine_any, theirs_any,
    dq_ref, dq2_ref, dkv_ref,
    ks_ref, mine_ref, theirs_ref, m_ref, d_ref, acc_ref, dq_acc_ref, sems, stat_sems,
):
    work = Work(order_ref, me_ref, kv_ref, ks_ref, sems)
    stat_copies = [
        load(mine_any, mine_ref, stat_sems.at[0]),
        load(theirs_any, theirs_ref, stat_sems.at[1]),
    ]
    acc_ref[...] = jnp.zeros(acc_ref.shape, jnp.float32)
    dq_acc_ref[...] = jnp.zeros(dq_acc_ref.shape, jnp.float32)
    for copy in stat_copies:
        copy.wait()
    for owner in range(2):
        for half in range(2):
            base = (2 * owner + half) * 3
            base2 = (2 * (1 - owner) + half) * 3
            m1, m2 = mine_ref[base : base + 1, :], theirs_ref[base2 : base2 + 1, :]
            top = jnp.maximum(m1, m2)
            w1 = jnp.exp2((m1 - top) * EXPONENT_SCALE)
            w2 = jnp.exp2((m2 - top) * EXPONENT_SCALE)
            total = w1 * mine_ref[base + 1 : base + 2, :] + w2 * theirs_ref[base2 + 1 : base2 + 2, :]
            delta = w1 * mine_ref[base + 2 : base + 3, :] + w2 * theirs_ref[base2 + 2 : base2 + 3, :]
            m_ref[owner, half] = top * EXPONENT_SCALE + jnp.log2(total)
            d_ref[owner, half] = delta / total
    work.wait()

    def gradients(owner, q_half, k_half, first, size, place, mask):
        scores = work.scores(ks_ref, qs_ref, owner, q_half, k_half, first, size, mask)
        grads = work.grads(ks_ref, ds_ref, owner, q_half, k_half, first, size)
        probs = jnp.exp2(scores * EXPONENT_SCALE - m_ref[owner, q_half])
        score_grads = (probs * (grads - d_ref[owner, q_half])).astype(jnp.bfloat16)
        rows = at_rows(first, size)
        acc_ref[k_half, rows, HEAD:] = acc_ref[k_half, rows, HEAD:] + jnp.dot(
            probs.astype(jnp.bfloat16), ds_ref[owner, q_half], preferred_element_type=jnp.float32
        )
        acc_ref[k_half, rows, :HEAD] = acc_ref[k_half, rows, :HEAD] + jnp.dot(
            score_grads, qs_ref[owner, q_half], preferred_element_type=jnp.float32
        )
        dq_acc_ref[owner, q_half] = dq_acc_ref[owner, q_half] + lax.dot_general(
            ks_ref[k_half, rows, :HEAD], score_grads, COLS_DOT_COLS, preferred_element_type=jnp.float32
        )

    work.blocks(gradients)
    rows = work.slab_rows
    me = me_ref[0]
    for owner, index, target in ((0, me, dq_ref), (1, me + 1 - 2 * work.side, dq2_ref)):
        _, place = pair_of(order_ref, index)
        for half in range(2):
            source = at_rows((place if half == 0 else 1 - place) * rows, rows)
            grads = (jnp.transpose(dq_acc_ref[owner, half]) * SCALE).astype(target.dtype)
            for h in range(GROUP):
                target[source, h * HEAD : (h + 1) * HEAD] = grads[h * rows : (h + 1) * rows, :]

    def write_terms(j):
        _, place = pair_of(order_ref, 2 * j + work.side)
        for half in range(2):
            here = place if half == 0 else 1 - place
            target = at_rows((2 * j + here) * rows, rows)
            source = at_rows(j * rows, rows)
            dkv_ref[target, :HEAD] = (acc_ref[half, source, :HEAD] * SCALE).astype(jnp.bfloat16)
            dkv_ref[target, HEAD:] = acc_ref[half, source, HEAD:].astype(jnp.bfloat16)

    repeat(work.outer, write_terms)


def combine_kernel(kvh, terms_any, key_ref, value_ref, terms_ref, sem):
    load(terms_any, terms_ref, sem).wait()
    seq = terms_ref.shape[0] // kvh
    for k in range(kvh):
        total = terms_ref[k].astype(jnp.float32)
        for s in range(1, seq):
            total = total + terms_ref[s * kvh + k].astype(jnp.float32)
        total = total.astype(jnp.bfloat16)
        key_ref[:, k * HEAD : (k + 1) * HEAD] = total[:, :HEAD]
        value_ref[:, k * HEAD : (k + 1) * HEAD] = total[:, HEAD:]


def finish_kernel(own_ref, received_ref, out_ref):
    out_ref[...] = (own_ref[...] + received_ref[...].astype(jnp.float32)).astype(jnp.bfloat16)


def per_device(queries, keys, values, d_out, slab_order):
    axes = ("outer", "kvh")
    kvh = lax.axis_size("kvh")
    outer = lax.axis_size("outer")
    peers = outer * kvh
    local_rows, query_width = queries.shape
    cache_rows = keys.shape[0]
    slab_rows = local_rows // 2
    column_rows = outer * local_rows
    half_rows = outer * slab_rows
    columns = GROUP * slab_rows
    swap = [(0, 1), (1, 0)]
    params = pltpu.CompilerParams(vmem_limit_bytes=(8 << 20) + (6 << 10) * column_rows)
    beside = pl.CostEstimate(flops=2 * 10**10, bytes_accessed=10**6, transcendentals=0)
    vmem = pl.BlockSpec(memory_space=pltpu.VMEM)
    smem = pl.BlockSpec(memory_space=pltpu.SMEM)
    anywhere = pl.BlockSpec(memory_space=pl.ANY)
    shape = jax.ShapeDtypeStruct

    queries2 = lax.ppermute(queries, "pair", swap)
    d_out2 = lax.ppermute(d_out, "pair", swap)
    packed = pl.pallas_call(
        functools.partial(pack_kernel, kvh),
        out_shape=shape((peers, cache_rows, 2 * HEAD), keys.dtype),
        in_specs=[vmem, vmem],
        out_specs=vmem,
        compiler_params=params,
        name="pack",
    )(keys, values)
    gathered = lax.all_to_all(packed, axes, split_axis=0, concat_axis=0, tiled=True)
    gathered = gathered.reshape(column_rows, 2 * HEAD)

    me = (lax.axis_index("outer") * 2 + lax.axis_index("pair")).astype(jnp.int32).reshape(1)
    stack = shape((2, 2, columns, HEAD), jnp.bfloat16)
    stacks = pl.pallas_call(
        stack_kernel,
        out_shape=(stack, stack),
        in_specs=[smem, smem] + [vmem] * 4,
        out_specs=(vmem, vmem),
        compiler_params=params,
        cost_estimate=beside,
        name="stack",
    )(slab_order, me, queries, d_out, queries2, d_out2)
    sorted_keys = pltpu.VMEM((2, half_rows, 2 * HEAD), jnp.bfloat16)
    key_sems = pltpu.SemaphoreType.DMA((2 * outer,))
    row_stat = pltpu.VMEM((2, 2, 1, columns), jnp.float32)
    stats = pl.pallas_call(
        stats_kernel,
        out_shape=shape((12, columns), jnp.float32),
        in_specs=[smem, smem, vmem, vmem, anywhere],
        out_specs=vmem,
        scratch_shapes=[
            sorted_keys,
            pltpu.VMEM((2, 2 * half_rows + slab_rows, columns), jnp.float32),
            row_stat,
            row_stat,
            row_stat,
            key_sems,
        ],
        compiler_params=params,
        name="stats",
    )(slab_order, me, *stacks, gathered)
    stats2 = lax.ppermute(stats, "pair", swap)
    own_grads, other_grads, terms = pl.pallas_call(
        grads_kernel,
        out_shape=(
            shape(queries.shape, jnp.float32),
            shape(queries.shape, jnp.bfloat16),
            shape((column_rows, 2 * HEAD), jnp.bfloat16),
        ),
        in_specs=[smem, smem, vmem, vmem] + [anywhere] * 3,
        out_specs=(vmem, vmem, vmem),
        scratch_shapes=[
            sorted_keys,
            pltpu.VMEM((12, columns), jnp.float32),
            pltpu.VMEM((12, columns), jnp.float32),
            row_stat,
            row_stat,
            pltpu.VMEM((2, half_rows, 2 * HEAD), jnp.float32),
            pltpu.VMEM((2, 2, HEAD, columns), jnp.float32),
            key_sems,
            pltpu.SemaphoreType.DMA((2,)),
        ],
        compiler_params=params,
        name="grads",
    )(slab_order, me, *stacks, gathered, stats, stats2)
    received_grads = lax.ppermute(other_grads, "pair", swap)
    owned = lax.all_to_all(
        terms.reshape(peers, cache_rows, 2 * HEAD), axes, split_axis=0, concat_axis=0, tiled=True
    )
    query_grads = pl.pallas_call(
        finish_kernel,
        out_shape=shape(queries.shape, jnp.bfloat16),
        in_specs=[vmem, vmem],
        out_specs=vmem,
        compiler_params=params,
        cost_estimate=beside,
        name="finish",
    )(own_grads, received_grads)
    key_grads, value_grads = pl.pallas_call(
        functools.partial(combine_kernel, kvh),
        out_shape=(shape(keys.shape, jnp.bfloat16), shape(values.shape, jnp.bfloat16)),
        in_specs=[anywhere],
        out_specs=(vmem, vmem),
        scratch_shapes=[pltpu.VMEM((peers, cache_rows, 2 * HEAD), jnp.bfloat16), pltpu.SemaphoreType.DMA],
        compiler_params=params,
        name="combine",
    )(owned)
    return (query_grads, key_grads, value_grads)


def solution(mesh):
    kvh = mesh.shape["kvh"]
    pairs = mesh.shape["seq"] // 2
    paired = Mesh(mesh.devices.reshape(pairs, 2, kvh), ("outer", "pair", "kvh"))
    seq = ("outer", "pair")
    cache = P(("outer", "pair", "kvh"), None)
    placed = (P(seq, "kvh"), cache, cache, P(seq, "kvh"), P())
    return jax.shard_map(
        per_device,
        mesh=paired,
        in_specs=placed,
        out_specs=(P(seq, "kvh"), cache, cache),
        check_vma=False,
    )
```

```python
import functools
import math

import jax
import jax.numpy as jnp
from jax import lax
from jax.experimental import pallas as pl
from jax.experimental.pallas import tpu as pltpu
from jax.sharding import Mesh
from jax.sharding import PartitionSpec as P

HEADS = 20
KV_HEADS = 4
HEAD = 128
GROUP = HEADS // KV_HEADS
SCALE = HEAD ** (-0.5)
EXPONENT_SCALE = SCALE * math.log2(math.e)
LOWEST = -1e30
ROWS_DOT_ROWS = (((1,), (1,)), ((), ()))
COLS_DOT_COLS = (((0,), (0,)), ((), ()))


def repeat(count, body):
    if count <= 8:
        for step in range(count):
            body(step)
    else:
        pl.loop(0, count)(body)


def at_rows(start, size):
    return pl.ds(pl.multiple_of(start, size), size)


def pair_of(order_ref, index):
    first, second = order_ref[2 * index], order_ref[2 * index + 1]
    return jnp.minimum(first, second), jnp.where(first < second, 0, 1)


def load(source_ref, target_ref, sem):
    copy = pltpu.make_async_copy(source_ref, target_ref, sem)
    copy.start()
    return copy


class Work:
    def __init__(self, order_ref, kv_refs, ks_ref, sems):
        self.half_rows = ks_ref.shape[1]
        self.outer = len(kv_refs)
        self.slab_rows = self.half_rows // self.outer
        self.chunk = math.gcd(256, self.half_rows)
        rows = self.slab_rows
        at, side = lax.axis_index("outer"), lax.axis_index("pair")
        self.low = [pair_of(order_ref, 2 * at + side)[0], pair_of(order_ref, 2 * at + 1 - side)[0]]
        self.pairs = [
            pair_of(order_ref, 2 * lax.rem(at + self.outer - d, self.outer) + side)
            for d in range(self.outer)
        ]
        self.copies = []
        for d, kv_ref in enumerate(kv_refs):
            for half in range(2):
                source = at_rows(self.here(d, half) * rows, rows)
                self.copies.append(
                    load(kv_ref.at[source], ks_ref.at[half, pl.ds(d * rows, rows)], sems.at[2 * d + half])
                )

    def here(self, d, half):
        place = self.pairs[d][1]
        return place if half == 0 else 1 - place

    def wait(self):
        for copy in self.copies:
            copy.wait()

    def blocks(self, body):
        rows = self.slab_rows
        for owner in range(2):
            repeat(
                self.half_rows // self.chunk,
                lambda n: body(owner, 1, 0, n * self.chunk, self.chunk, n * self.chunk, False),
            )
            for d in range(self.outer):
                if owner == 0 and d == 0:
                    body(owner, 0, 0, 0, rows, self.half_rows, True)
                    body(owner, 1, 1, 0, rows, 2 * self.half_rows, True)
                else:
                    half = jnp.where(self.low[owner] >= self.pairs[d][0], 0, 1)
                    body(owner, half, half, d * rows, rows, self.half_rows + d * rows, False)

    def scores(self, ks_ref, qs_ref, owner, q_half, k_half, first, size, mask):
        scores = lax.dot_general(
            ks_ref[k_half, at_rows(first, size), :HEAD],
            qs_ref[owner, q_half],
            ROWS_DOT_ROWS,
            preferred_element_type=jnp.float32,
        )
        if mask:
            key = lax.broadcasted_iota(jnp.int32, scores.shape, 0)
            query = lax.rem(lax.broadcasted_iota(jnp.int32, (1, scores.shape[1]), 1), self.slab_rows)
            scores = jnp.where(key <= query, scores, LOWEST)
        return scores

    def grads(self, ks_ref, ds_ref, owner, q_half, k_half, first, size):
        return lax.dot_general(
            ks_ref[k_half, at_rows(first, size), HEAD:],
            ds_ref[owner, q_half],
            ROWS_DOT_ROWS,
            preferred_element_type=jnp.float32,
        )


def split_kernel(keys_ref, values_ref, *refs):
    outs, sems = refs[:-1], refs[-1]
    kvh = len(outs)
    copies = []
    for e, out_ref in enumerate(outs):
        head = lax.rem(lax.axis_index("kvh") + e, kvh)
        cols = at_rows(head * HEAD, HEAD)
        copies.append(load(keys_ref.at[:, cols], out_ref.at[:, pl.ds(0, HEAD)], sems.at[2 * e]))
        copies.append(load(values_ref.at[:, cols], out_ref.at[:, pl.ds(HEAD, HEAD)], sems.at[2 * e + 1]))
    for copy in copies:
        copy.wait()


def join_kernel(*refs):
    parts, out_ref, sems = refs[:-2], refs[-2], refs[-1]
    kvh = len(parts)
    rows = parts[0].shape[0]
    copies = []
    for e, part_ref in enumerate(parts):
        source = lax.rem(lax.axis_index("kvh") + kvh - e, kvh)
        copies.append(load(part_ref, out_ref.at[at_rows(source * rows, rows)], sems.at[e]))
    for copy in copies:
        copy.wait()


def stack_kernel(order_ref, q_ref, do_ref, q2_ref, do2_ref, qs_ref, ds_ref):
    rows = q_ref.shape[0] // 2
    at, side = lax.axis_index("outer"), lax.axis_index("pair")
    for owner, index in ((0, 2 * at + side), (1, 2 * at + 1 - side)):
        _, place = pair_of(order_ref, index)
        for half in range(2):
            source = at_rows((place if half == 0 else 1 - place) * rows, rows)
            for target, parts in ((qs_ref, (q_ref, q2_ref)), (ds_ref, (do_ref, do2_ref))):
                for h in range(GROUP):
                    target[owner, half, h * rows : (h + 1) * rows, :] = parts[owner][
                        source, h * HEAD : (h + 1) * HEAD
                    ]


def stats_kernel(order_ref, qs_ref, ds_ref, *refs):
    kv_refs, (out_ref, ks_ref, s_ref, m_ref, l_ref, d_ref, sems) = refs[:-7], refs[-7:]
    work = Work(order_ref, kv_refs, ks_ref, sems)
    m_ref[...] = jnp.full(m_ref.shape, LOWEST, jnp.float32)
    l_ref[...] = jnp.zeros(l_ref.shape, jnp.float32)
    d_ref[...] = jnp.zeros(d_ref.shape, jnp.float32)
    work.wait()

    def maximum(owner, q_half, k_half, first, size, place, mask):
        scores = work.scores(ks_ref, qs_ref, owner, q_half, k_half, first, size, mask)
        s_ref[owner, at_rows(place, size), :] = scores
        m_ref[owner, q_half] = jnp.maximum(
            m_ref[owner, q_half], jnp.max(scores, axis=0, keepdims=True)
        )

    work.blocks(maximum)

    def sums(owner, q_half, k_half, first, size, place, mask):
        grads = work.grads(ks_ref, ds_ref, owner, q_half, k_half, first, size)
        scores = s_ref[owner, at_rows(place, size), :]
        expon = jnp.exp2((scores - m_ref[owner, q_half]) * EXPONENT_SCALE)
        l_ref[owner, q_half] = l_ref[owner, q_half] + jnp.sum(expon, axis=0, keepdims=True)
        d_ref[owner, q_half] = d_ref[owner, q_half] + jnp.sum(expon * grads, axis=0, keepdims=True)

    work.blocks(sums)
    for owner in range(2):
        for half in range(2):
            base = (2 * owner + half) * 3
            out_ref[base : base + 1, :] = m_ref[owner, half]
            out_ref[base + 1 : base + 2, :] = l_ref[owner, half]
            out_ref[base + 2 : base + 3, :] = d_ref[owner, half]


def grads_kernel(outer, order_ref, qs_ref, ds_ref, *refs):
    kv_refs, (mine_any, theirs_any, dq_ref, dq2_ref) = refs[:outer], refs[outer : outer + 4]
    term_refs = refs[outer + 4 : 2 * outer + 4]
    ks_ref, mine_ref, theirs_ref, m_ref, d_ref, acc_ref, dq_acc_ref, sems, stat_sems = refs[2 * outer + 4 :]
    work = Work(order_ref, kv_refs, ks_ref, sems)
    stat_copies = [
        load(mine_any, mine_ref, stat_sems.at[0]),
        load(theirs_any, theirs_ref, stat_sems.at[1]),
    ]
    acc_ref[...] = jnp.zeros(acc_ref.shape, jnp.float32)
    dq_acc_ref[...] = jnp.zeros(dq_acc_ref.shape, jnp.float32)
    for copy in stat_copies:
        copy.wait()
    for owner in range(2):
        for half in range(2):
            base = (2 * owner + half) * 3
            base2 = (2 * (1 - owner) + half) * 3
            m1, m2 = mine_ref[base : base + 1, :], theirs_ref[base2 : base2 + 1, :]
            top = jnp.maximum(m1, m2)
            w1 = jnp.exp2((m1 - top) * EXPONENT_SCALE)
            w2 = jnp.exp2((m2 - top) * EXPONENT_SCALE)
            total = w1 * mine_ref[base + 1 : base + 2, :] + w2 * theirs_ref[base2 + 1 : base2 + 2, :]
            delta = w1 * mine_ref[base + 2 : base + 3, :] + w2 * theirs_ref[base2 + 2 : base2 + 3, :]
            m_ref[owner, half] = top * EXPONENT_SCALE + jnp.log2(total)
            d_ref[owner, half] = delta / total
    work.wait()

    def gradients(owner, q_half, k_half, first, size, place, mask):
        scores = work.scores(ks_ref, qs_ref, owner, q_half, k_half, first, size, mask)
        grads = work.grads(ks_ref, ds_ref, owner, q_half, k_half, first, size)
        probs = jnp.exp2(scores * EXPONENT_SCALE - m_ref[owner, q_half])
        score_grads = (probs * (grads - d_ref[owner, q_half])).astype(jnp.bfloat16)
        rows = at_rows(first, size)
        acc_ref[k_half, rows, HEAD:] = acc_ref[k_half, rows, HEAD:] + jnp.dot(
            probs.astype(jnp.bfloat16), ds_ref[owner, q_half], preferred_element_type=jnp.float32
        )
        acc_ref[k_half, rows, :HEAD] = acc_ref[k_half, rows, :HEAD] + jnp.dot(
            score_grads, qs_ref[owner, q_half], preferred_element_type=jnp.float32
        )
        dq_acc_ref[owner, q_half] = dq_acc_ref[owner, q_half] + lax.dot_general(
            ks_ref[k_half, rows, :HEAD], score_grads, COLS_DOT_COLS, preferred_element_type=jnp.float32
        )

    work.blocks(gradients)
    rows = work.slab_rows
    at, side = lax.axis_index("outer"), lax.axis_index("pair")
    for owner, index, target in ((0, 2 * at + side, dq_ref), (1, 2 * at + 1 - side, dq2_ref)):
        _, place = pair_of(order_ref, index)
        for half in range(2):
            source = at_rows((place if half == 0 else 1 - place) * rows, rows)
            grads = (jnp.transpose(dq_acc_ref[owner, half]) * SCALE).astype(target.dtype)
            for h in range(GROUP):
                target[source, h * HEAD : (h + 1) * HEAD] = grads[h * rows : (h + 1) * rows, :]

    for d, term_ref in enumerate(term_refs):
        for half in range(2):
            target = at_rows(work.here(d, half) * rows, rows)
            source = slice(d * rows, (d + 1) * rows)
            term_ref[target, :HEAD] = (acc_ref[half, source, :HEAD] * SCALE).astype(term_ref.dtype)
            term_ref[target, HEAD:] = acc_ref[half, source, HEAD:].astype(term_ref.dtype)


def sum_kernel(outer, *refs):
    terms, outs, (total_ref,) = refs[:outer], refs[outer:-1], refs[-1:]
    total = terms[0][...]
    for term_ref in terms[1:]:
        total = total + term_ref[...].astype(jnp.float32)
    total_ref[...] = total
    kvh = len(outs)
    rows = outs[0].shape[0]
    for e, out_ref in enumerate(outs):
        target = lax.rem(lax.axis_index("kvh") + e, kvh)
        out_ref[...] = total_ref[at_rows(target * rows, rows), :].astype(jnp.bfloat16)


def place_kernel(*refs):
    parts, (key_ref, value_ref, sems) = refs[:-3], refs[-3:]
    kvh = len(parts)
    copies = []
    for e, part_ref in enumerate(parts):
        head = lax.rem(lax.axis_index("kvh") + kvh - e, kvh)
        cols = at_rows(head * HEAD, HEAD)
        copies.append(load(part_ref.at[:, pl.ds(0, HEAD)], key_ref.at[:, cols], sems.at[2 * e]))
        copies.append(load(part_ref.at[:, pl.ds(HEAD, HEAD)], value_ref.at[:, cols], sems.at[2 * e + 1]))
    for copy in copies:
        copy.wait()


def finish_kernel(own_ref, received_ref, out_ref):
    out_ref[...] = (own_ref[...] + received_ref[...].astype(jnp.float32)).astype(jnp.bfloat16)


def per_device(queries, keys, values, d_out, slab_order):
    kvh = lax.axis_size("kvh")
    outer = lax.axis_size("outer")
    local_rows, query_width = queries.shape
    cache_rows = keys.shape[0]
    slab_rows = local_rows // 2
    half_rows = outer * slab_rows
    columns = GROUP * slab_rows
    params = pltpu.CompilerParams(vmem_limit_bytes=(8 << 20) + (6 << 10) * 2 * half_rows)
    beside = pl.CostEstimate(flops=2 * 10**10, bytes_accessed=10**6, transcendentals=0)
    vmem = pl.BlockSpec(memory_space=pltpu.VMEM)
    smem = pl.BlockSpec(memory_space=pltpu.SMEM)
    anywhere = pl.BlockSpec(memory_space=pl.ANY)
    shape = jax.ShapeDtypeStruct
    dma = pltpu.SemaphoreType.DMA

    def shift(array, axis, by):
        size = lax.axis_size(axis)
        return lax.ppermute(array, axis, [(n, (n + by) % size) for n in range(size)])

    part = shape((cache_rows, 2 * HEAD), jnp.bfloat16)
    block = shape((local_rows, 2 * HEAD), jnp.bfloat16)
    parts = pl.pallas_call(
        split_kernel,
        out_shape=(part,) * kvh,
        in_specs=[anywhere, anywhere],
        out_specs=(vmem,) * kvh,
        scratch_shapes=[dma((2 * kvh,))],
        compiler_params=params,
        name="split",
    )(keys, values)
    parts = [parts[0]] + [shift(parts[e], "kvh", e) for e in range(1, kvh)]
    queries2 = shift(queries, "pair", 1)
    d_out2 = shift(d_out, "pair", 1)
    own_block = pl.pallas_call(
        join_kernel,
        out_shape=block,
        in_specs=[anywhere] * kvh,
        out_specs=vmem,
        scratch_shapes=[dma((kvh,))],
        compiler_params=params,
        name="join",
    )(*parts)
    blocks = [own_block] + [shift(own_block, "outer", d) for d in range(1, outer)]

    stack = shape((2, 2, columns, HEAD), jnp.bfloat16)
    stacks = pl.pallas_call(
        stack_kernel,
        out_shape=(stack, stack),
        in_specs=[smem] + [vmem] * 4,
        out_specs=(vmem, vmem),
        compiler_params=params,
        cost_estimate=beside,
        name="stack",
    )(slab_order, queries, d_out, queries2, d_out2)
    sorted_keys = pltpu.VMEM((2, half_rows, 2 * HEAD), jnp.bfloat16)
    key_sems = dma((2 * outer,))
    row_stat = pltpu.VMEM((2, 2, 1, columns), jnp.float32)
    all_stats = (12, columns)
    stats = pl.pallas_call(
        stats_kernel,
        out_shape=shape(all_stats, jnp.float32),
        in_specs=[smem, vmem, vmem] + [anywhere] * outer,
        out_specs=vmem,
        scratch_shapes=[
            sorted_keys,
            pltpu.VMEM((2, 2 * half_rows + slab_rows, columns), jnp.float32),
            row_stat,
            row_stat,
            row_stat,
            key_sems,
        ],
        compiler_params=params,
        name="stats",
    )(slab_order, *stacks, *blocks)
    stats2 = shift(stats, "pair", 1)
    own_grads, other_grads, *terms = pl.pallas_call(
        functools.partial(grads_kernel, outer),
        out_shape=(
            shape(queries.shape, jnp.float32),
            shape(queries.shape, jnp.bfloat16),
            shape(block.shape, jnp.float32),
        )
        + (block,) * (outer - 1),
        in_specs=[smem, vmem, vmem] + [anywhere] * (outer + 2),
        out_specs=(vmem,) * (outer + 2),
        scratch_shapes=[
            sorted_keys,
            pltpu.VMEM(all_stats, jnp.float32),
            pltpu.VMEM(all_stats, jnp.float32),
            row_stat,
            row_stat,
            pltpu.VMEM((2, half_rows, 2 * HEAD), jnp.float32),
            pltpu.VMEM((2, 2, HEAD, columns), jnp.float32),
            key_sems,
            dma((2,)),
        ],
        compiler_params=params,
        name="grads",
    )(slab_order, *stacks, *blocks, stats, stats2)
    terms = [terms[0]] + [shift(terms[d], "outer", -d) for d in range(1, outer)]
    received_grads = shift(other_grads, "pair", 1)
    query_grads = pl.pallas_call(
        finish_kernel,
        out_shape=shape(queries.shape, jnp.bfloat16),
        in_specs=[vmem, vmem],
        out_specs=vmem,
        compiler_params=params,
        cost_estimate=beside,
        name="finish",
    )(own_grads, received_grads)
    owned = pl.pallas_call(
        functools.partial(sum_kernel, outer),
        out_shape=(part,) * kvh,
        in_specs=[vmem] * outer,
        out_specs=(vmem,) * kvh,
        scratch_shapes=[pltpu.VMEM(block.shape, jnp.float32)],
        compiler_params=params,
        name="sum",
    )(*terms)
    owned = [owned[0]] + [shift(owned[e], "kvh", e) for e in range(1, kvh)]
    key_grads, value_grads = pl.pallas_call(
        place_kernel,
        out_shape=(shape(keys.shape, jnp.bfloat16), shape(values.shape, jnp.bfloat16)),
        in_specs=[anywhere] * kvh,
        out_specs=(anywhere, anywhere),
        scratch_shapes=[dma((2 * kvh,))],
        compiler_params=params,
        name="place",
    )(*owned)
    return (query_grads, key_grads, value_grads)


def solution(mesh):
    kvh = mesh.shape["kvh"]
    pairs = mesh.shape["seq"] // 2
    paired = Mesh(mesh.devices.reshape(pairs, 2, kvh), ("outer", "pair", "kvh"))
    seq = ("outer", "pair")
    cache = P(("outer", "pair", "kvh"), None)
    placed = (P(seq, "kvh"), cache, cache, P(seq, "kvh"), P())
    return jax.shard_map(
        per_device,
        mesh=paired,
        in_specs=placed,
        out_specs=(P(seq, "kvh"), cache, cache),
        check_vma=False,
    )
```

```python
import functools
import math

import jax
import jax.numpy as jnp
from jax import lax
from jax.experimental import pallas as pl
from jax.experimental.pallas import tpu as pltpu
from jax.sharding import Mesh
from jax.sharding import PartitionSpec as P

HEADS = 20
KV_HEADS = 4
HEAD = 128
GROUP = HEADS // KV_HEADS
SCALE = HEAD ** (-0.5)
EXPONENT_SCALE = SCALE * math.log2(math.e)
LOWEST = -1e30
ROWS_DOT_ROWS = (((1,), (1,)), ((), ()))
COLS_DOT_COLS = (((0,), (0,)), ((), ()))


def at_rows(start, size):
    return pl.ds(pl.multiple_of(start, size), size)


def load(source_ref, target_ref, sem):
    copy = pltpu.make_async_copy(source_ref, target_ref, sem)
    copy.start()
    return copy


def wait_all(copies):
    for copy in copies:
        copy.wait()


class Work:
    def __init__(self, order_ref, half_rows, outer):
        self.half_rows, self.outer = half_rows, outer
        self.slab_rows = half_rows // outer
        self.chunk = math.gcd(256, half_rows)
        at, side = lax.axis_index("outer"), lax.axis_index("pair")

        def pair_of(index):
            first, second = order_ref[2 * index], order_ref[2 * index + 1]
            return jnp.minimum(first, second), jnp.where(first < second, 0, 1)

        self.owners = [pair_of(2 * at + side), pair_of(2 * at + 1 - side)]
        self.pairs = [pair_of(2 * lax.rem(at + outer - d, outer) + side) for d in range(outer)]

    def query_slot(self, owner, half):
        place = self.owners[owner][1]
        return jnp.where(half == 0, place, 1 - place)

    def key_slot(self, d, half):
        place = self.pairs[d][1]
        return place if half == 0 else 1 - place

    def blocks(self, body):
        rows = self.slab_rows
        for owner in range(2):
            for first in range(0, self.half_rows, self.chunk):
                body(owner, 1, 0, first, self.chunk, first, False)
            for d in range(self.outer):
                if owner == 0 and d == 0:
                    body(owner, 0, 0, 0, rows, self.half_rows, True)
                    body(owner, 1, 1, 0, rows, 2 * self.half_rows, True)
                else:
                    half = jnp.where(self.owners[owner][0] >= self.pairs[d][0], 0, 1)
                    body(owner, half, half, d * rows, rows, self.half_rows + d * rows, False)


def split_kernel(keys_ref, values_ref, q_ref, do_ref, *refs):
    parts, (qd_ref, sems) = refs[:-2], refs[-2:]
    kvh = len(parts)
    copies = []
    for e, part_ref in enumerate(parts):
        head = lax.rem(lax.axis_index("kvh") + e, kvh)
        cols = at_rows(head * HEAD, HEAD)
        for n, source_ref in enumerate((keys_ref, values_ref)):
            copies.append((source_ref.at[:, cols], part_ref.at[:, pl.ds(n * HEAD, HEAD)]))
    rows = q_ref.shape[0] // 2
    for n, source_ref in enumerate((q_ref, do_ref)):
        for slot in range(2):
            for h in range(GROUP):
                copies.append((
                    source_ref.at[pl.ds(slot * rows, rows), pl.ds(h * HEAD, HEAD)],
                    qd_ref.at[n, slot, pl.ds(h * rows, rows)],
                ))
    wait_all([load(*copy, sems.at[n]) for n, copy in enumerate(copies)])


def join_kernel(*refs):
    parts, (out_ref, sems) = refs[:-2], refs[-2:]
    kvh = len(parts)
    rows = parts[0].shape[0]
    copies = []
    for e, part_ref in enumerate(parts):
        source = lax.rem(lax.axis_index("kvh") + kvh - e, kvh)
        copies.append(load(part_ref, out_ref.at[at_rows(source * rows, rows)], sems.at[e]))
    wait_all(copies)


def stats_kernel(order_ref, own_ref, other_ref, *refs):
    kv_refs, (out_ref, e_ref, dp_ref, ks_ref, m_ref, l_ref, d_ref, sems) = refs[:-8], refs[-8:]
    work = Work(order_ref, ks_ref.shape[1], len(kv_refs))
    rows = work.slab_rows
    copies = []
    for d, kv_ref in enumerate(kv_refs):
        for half in range(2):
            source = at_rows(work.key_slot(d, half) * rows, rows)
            copies.append(
                load(kv_ref.at[source], ks_ref.at[half, pl.ds(d * rows, rows)], sems.at[2 * d + half])
            )
    m_ref[...] = jnp.full(m_ref.shape, LOWEST, jnp.float32)
    l_ref[...] = jnp.zeros(l_ref.shape, jnp.float32)
    d_ref[...] = jnp.zeros(d_ref.shape, jnp.float32)
    wait_all(copies)
    qd_refs = (own_ref, other_ref)

    def maximum(owner, q_half, k_half, first, size, place, masked):
        slot = work.query_slot(owner, q_half)
        scores = lax.dot_general(
            ks_ref[k_half, pl.ds(first, size), :HEAD],
            qd_refs[owner][0, slot],
            ROWS_DOT_ROWS,
            preferred_element_type=jnp.float32,
        )
        if masked:
            key = lax.broadcasted_iota(jnp.int32, scores.shape, 0)
            query = lax.rem(lax.broadcasted_iota(jnp.int32, (1, scores.shape[1]), 1), rows)
            scores = jnp.where(key <= query, scores, LOWEST)
        e_ref[owner, pl.ds(place, size), :] = scores
        m_ref[owner, q_half] = jnp.maximum(
            m_ref[owner, q_half], jnp.max(scores, axis=0, keepdims=True)
        )
        dp_ref[owner, pl.ds(place, size), :] = lax.dot_general(
            ks_ref[k_half, pl.ds(first, size), HEAD:],
            qd_refs[owner][1, slot],
            ROWS_DOT_ROWS,
            preferred_element_type=jnp.float32,
        )

    work.blocks(maximum)

    def sums(owner, q_half, k_half, first, size, place, masked):
        scores = e_ref[owner, pl.ds(place, size), :]
        grads = dp_ref[owner, pl.ds(place, size), :]
        expon = jnp.exp2((scores - m_ref[owner, q_half]) * EXPONENT_SCALE)
        e_ref[owner, pl.ds(place, size), :] = expon
        l_ref[owner, q_half] = l_ref[owner, q_half] + jnp.sum(expon, axis=0, keepdims=True)
        d_ref[owner, q_half] = d_ref[owner, q_half] + jnp.sum(expon * grads, axis=0, keepdims=True)

    work.blocks(sums)
    for owner in range(2):
        for half in range(2):
            base = (2 * owner + half) * 3
            out_ref[base : base + 1, :] = m_ref[owner, half]
            out_ref[base + 1 : base + 2, :] = l_ref[owner, half]
            out_ref[base + 2 : base + 3, :] = d_ref[owner, half]


def grads_kernel(outer, order_ref, own_ref, other_ref, mine_ref, theirs_ref, e_ref, dp_ref, *refs):
    term_refs, (gs_ref, w_ref, d_ref, acc_ref) = refs[:outer], refs[outer:]
    work = Work(order_ref, acc_ref.shape[1], outer)
    rows = work.slab_rows
    acc_ref[...] = jnp.zeros(acc_ref.shape, jnp.float32)
    for owner in range(2):
        for half in range(2):
            base = (2 * owner + half) * 3
            base2 = (2 * (1 - owner) + half) * 3
            m1, m2 = mine_ref[base : base + 1, :], theirs_ref[base2 : base2 + 1, :]
            top = jnp.maximum(m1, m2)
            w1 = jnp.exp2((m1 - top) * EXPONENT_SCALE)
            w2 = jnp.exp2((m2 - top) * EXPONENT_SCALE)
            total = w1 * mine_ref[base + 1 : base + 2, :] + w2 * theirs_ref[base2 + 1 : base2 + 2, :]
            delta = w1 * mine_ref[base + 2 : base + 3, :] + w2 * theirs_ref[base2 + 2 : base2 + 3, :]
            w_ref[owner, half] = w1 / total
            d_ref[owner, half] = delta / total
    qd_refs = (own_ref, other_ref)

    def gradients(owner, q_half, k_half, first, size, place, masked):
        slot = work.query_slot(owner, q_half)
        here = pl.ds(place, size)
        probs = e_ref[owner, here, :] * w_ref[owner, q_half]
        score_grads = (probs * (dp_ref[owner, here, :] - d_ref[owner, q_half])).astype(jnp.bfloat16)
        gs_ref[owner, here, :] = score_grads
        keys = pl.ds(first, size)
        acc_ref[k_half, keys, HEAD:] = acc_ref[k_half, keys, HEAD:] + jnp.dot(
            probs.astype(jnp.bfloat16), qd_refs[owner][1, slot], preferred_element_type=jnp.float32
        )
        acc_ref[k_half, keys, :HEAD] = acc_ref[k_half, keys, :HEAD] + jnp.dot(
            score_grads, qd_refs[owner][0, slot], preferred_element_type=jnp.float32
        )

    work.blocks(gradients)
    for d, term_ref in enumerate(term_refs):
        for half in range(2):
            target = at_rows(work.key_slot(d, half) * rows, rows)
            source = slice(d * rows, (d + 1) * rows)
            term_ref[target, :HEAD] = (acc_ref[half, source, :HEAD] * SCALE).astype(term_ref.dtype)
            term_ref[target, HEAD:] = acc_ref[half, source, HEAD:].astype(term_ref.dtype)


def query_kernel(outer, order_ref, gs_ref, ks_ref, own_ref, other_ref, acc_ref):
    work = Work(order_ref, ks_ref.shape[1], outer)
    rows = work.slab_rows
    acc_ref[...] = jnp.zeros(acc_ref.shape, jnp.float32)

    def terms(owner, q_half, k_half, first, size, place, masked):
        acc_ref[owner, q_half] = acc_ref[owner, q_half] + lax.dot_general(
            ks_ref[k_half, pl.ds(first, size), :HEAD],
            gs_ref[owner, pl.ds(place, size), :],
            COLS_DOT_COLS,
            preferred_element_type=jnp.float32,
        )

    work.blocks(terms)
    for owner, target in ((0, own_ref), (1, other_ref)):
        for half in range(2):
            place = at_rows(work.query_slot(owner, half) * rows, rows)
            grads = (jnp.transpose(acc_ref[owner, half]) * SCALE).astype(target.dtype)
            for h in range(GROUP):
                target[place, h * HEAD : (h + 1) * HEAD] = grads[h * rows : (h + 1) * rows, :]


def sum_kernel(outer, *refs):
    terms, outs, total_ref = refs[:outer], refs[outer:-1], refs[-1]
    total = terms[0][...]
    for term_ref in terms[1:]:
        total = total + term_ref[...].astype(jnp.float32)
    total_ref[...] = total
    kvh = len(outs)
    rows = outs[0].shape[0]
    for e, out_ref in enumerate(outs):
        target = lax.rem(lax.axis_index("kvh") + e, kvh)
        out_ref[...] = total_ref[at_rows(target * rows, rows), :].astype(jnp.bfloat16)


def place_kernel(own_ref, received_ref, *refs):
    parts, (dq_out, key_out, value_out, dq_ref, sems) = refs[:-5], refs[-5:]
    kvh = len(parts)
    copies = []
    for e, part_ref in enumerate(parts):
        head = lax.rem(lax.axis_index("kvh") + kvh - e, kvh)
        cols = at_rows(head * HEAD, HEAD)
        copies.append(load(part_ref.at[:, pl.ds(0, HEAD)], key_out.at[:, cols], sems.at[2 * e]))
        copies.append(load(part_ref.at[:, pl.ds(HEAD, HEAD)], value_out.at[:, cols], sems.at[2 * e + 1]))
    dq_ref[...] = (own_ref[...] + received_ref[...].astype(jnp.float32)).astype(jnp.bfloat16)
    copies.append(load(dq_ref, dq_out, sems.at[2 * kvh]))
    wait_all(copies)


def per_device(queries, keys, values, d_out, slab_order):
    kvh = lax.axis_size("kvh")
    outer = lax.axis_size("outer")
    local_rows, query_width = queries.shape
    cache_rows = keys.shape[0]
    slab_rows = local_rows // 2
    half_rows = outer * slab_rows
    columns = GROUP * slab_rows
    params = pltpu.CompilerParams(vmem_limit_bytes=(8 << 20) + (10 << 10) * 2 * half_rows)
    beside = pl.CostEstimate(flops=2 * 10**10, bytes_accessed=10**6, transcendentals=0)
    vmem = pl.BlockSpec(memory_space=pltpu.VMEM)
    smem = pl.BlockSpec(memory_space=pltpu.SMEM)
    anywhere = pl.BlockSpec(memory_space=pl.ANY)
    shape = jax.ShapeDtypeStruct
    dma = pltpu.SemaphoreType.DMA
    low, full = jnp.bfloat16, jnp.float32

    def call(kernel, name, limit=params, **arguments):
        return pl.pallas_call(kernel, compiler_params=limit, name=name, **arguments)

    def shift(array, axis, by):
        size = lax.axis_size(axis)
        return lax.ppermute(array, axis, [(n, (n + by) % size) for n in range(size)])

    part = shape((cache_rows, 2 * HEAD), low)
    block = shape((local_rows, 2 * HEAD), low)
    *parts, own_qd = call(
        split_kernel,
        "split",
        out_shape=(part,) * kvh + (shape((2, 2, columns, HEAD), low),),
        limit=pltpu.CompilerParams(vmem_limit_bytes=56 << 20),
        in_specs=[anywhere] * 4,
        out_specs=(anywhere,) * (kvh + 1),
        scratch_shapes=[dma((2 * kvh + 4 * GROUP,))],
    )(keys, values, queries, d_out)
    parts = [parts[0]] + [shift(parts[e], "kvh", e) for e in range(1, kvh)]
    other_qd = shift(own_qd, "pair", 1)
    own_block = call(
        join_kernel,
        "join",
        out_shape=block,
        in_specs=[anywhere] * kvh,
        out_specs=vmem,
        scratch_shapes=[dma((kvh,))],
    )(*parts)
    blocks = [own_block] + [shift(own_block, "outer", d) for d in range(1, outer)]

    all_stats = shape((12, columns), full)
    score_rows = (2, 2 * half_rows + slab_rows, columns)
    row_stat = pltpu.VMEM((2, 2, 1, columns), full)
    stats, expon, grad_probs, sorted_keys = call(
        stats_kernel,
        "stats",
        out_shape=(
            all_stats,
            shape(score_rows, full),
            shape(score_rows, full),
            shape((2, half_rows, 2 * HEAD), low),
        ),
        in_specs=[smem, vmem, vmem] + [anywhere] * outer,
        out_specs=(vmem,) * 4,
        scratch_shapes=[row_stat, row_stat, row_stat, dma((2 * outer,))],
    )(slab_order, own_qd, other_qd, *blocks)
    stats2 = shift(stats, "pair", 1)
    *terms, score_grads = call(
        functools.partial(grads_kernel, outer),
        "grads",
        out_shape=(shape(block.shape, full),) + (block,) * (outer - 1) + (shape(score_rows, low),),
        in_specs=[smem] + [vmem] * 6,
        out_specs=(vmem,) * (outer + 1),
        scratch_shapes=[row_stat, row_stat, pltpu.VMEM((2, half_rows, 2 * HEAD), full)],
    )(slab_order, own_qd, other_qd, stats, stats2, expon, grad_probs)
    terms = [terms[0]] + [shift(terms[d], "outer", -d) for d in range(1, outer)]
    own_grads, other_grads = call(
        functools.partial(query_kernel, outer),
        "query_terms",
        out_shape=(shape(queries.shape, full), shape(queries.shape, low)),
        in_specs=[smem, vmem, vmem],
        out_specs=(vmem, vmem),
        scratch_shapes=[pltpu.VMEM((2, 2, HEAD, columns), full)],
        cost_estimate=beside,
    )(slab_order, score_grads, sorted_keys)
    received_grads = shift(other_grads, "pair", 1)
    owned = call(
        functools.partial(sum_kernel, outer),
        "sum",
        out_shape=(part,) * kvh,
        in_specs=[vmem] * outer,
        out_specs=(vmem,) * kvh,
        scratch_shapes=[pltpu.VMEM(block.shape, full)],
    )(*terms)
    owned = [owned[0]] + [shift(owned[e], "kvh", e) for e in range(1, kvh)]
    return call(
        place_kernel,
        "place",
        out_shape=(shape(queries.shape, low), shape(keys.shape, low), shape(values.shape, low)),
        in_specs=[vmem, vmem] + [anywhere] * kvh,
        out_specs=(anywhere,) * 3,
        scratch_shapes=[pltpu.VMEM(queries.shape, low), dma((2 * kvh + 1,))],
    )(own_grads, received_grads, *owned)


def solution(mesh):
    kvh = mesh.shape["kvh"]
    pairs = mesh.shape["seq"] // 2
    paired = Mesh(mesh.devices.reshape(pairs, 2, kvh), ("outer", "pair", "kvh"))
    seq = ("outer", "pair")
    cache = P(("outer", "pair", "kvh"), None)
    placed = (P(seq, "kvh"), cache, cache, P(seq, "kvh"), P())
    return jax.shard_map(
        per_device,
        mesh=paired,
        in_specs=placed,
        out_specs=(P(seq, "kvh"), cache, cache),
        check_vma=False,
    )
```

```python
import functools
import math

import jax
import jax.numpy as jnp
from jax import lax
from jax.experimental import pallas as pl
from jax.experimental.pallas import tpu as pltpu
from jax.sharding import Mesh
from jax.sharding import PartitionSpec as P

HEADS = 20
KV_HEADS = 4
HEAD = 128
GROUP = HEADS // KV_HEADS
SCALE = HEAD ** (-0.5)
EXPONENT_SCALE = SCALE * math.log2(math.e)
LOWEST = -1e30
ROWS_DOT_ROWS = (((1,), (1,)), ((), ()))
COLS_DOT_COLS = (((0,), (0,)), ((), ()))


def at_rows(start, size):
    return pl.ds(pl.multiple_of(start, size), size)


def load(source_ref, target_ref, sem):
    copy = pltpu.make_async_copy(source_ref, target_ref, sem)
    copy.start()
    return copy


def wait_all(copies):
    for copy in copies:
        copy.wait()


class Work:
    def __init__(self, order_ref, slab_rows, outer):
        self.slab_rows = slab_rows
        at, side = lax.axis_index("outer"), lax.axis_index("pair")

        def pair_of(index):
            first, second = order_ref[2 * index], order_ref[2 * index + 1]
            return jnp.minimum(first, second), jnp.where(first < second, 0, 1)

        self.owners = [pair_of(2 * at + side), pair_of(2 * at + 1 - side)]
        self.pairs = [pair_of(2 * lax.rem(at + outer - d, outer) + side) for d in range(outer)]

    def query_slot(self, owner, half):
        place = self.owners[owner][1]
        return jnp.where(half == 0, place, 1 - place)

    def key_slot(self, d, half):
        place = self.pairs[d][1]
        return place if half == 0 else 1 - place

    def blocks(self, members, body):
        rows = self.slab_rows
        half_rows = len(members) * rows
        chunk = math.gcd(256, half_rows)
        for owner in range(2):
            for first in range(0, half_rows, chunk):
                body(owner, 1, 0, first, chunk, first, False)
            for n, d in enumerate(members):
                if owner == 0 and d == 0:
                    body(owner, 0, 0, n * rows, rows, half_rows + n * rows, True)
                    body(owner, 1, 1, n * rows, rows, 2 * half_rows, True)
                else:
                    half = jnp.where(self.owners[owner][0] >= self.pairs[d][0], 0, 1)
                    body(owner, half, half, n * rows, rows, half_rows + n * rows, False)


def split_kernel(cache_ref, *refs):
    parts, sems = refs[:-1], refs[-1]
    kvh = len(parts)
    rows = parts[0].shape[0]
    copies = []
    for e, part_ref in enumerate(parts):
        head = lax.rem(lax.axis_index("kvh") + e, kvh)
        cols = at_rows(head * HEAD, HEAD)
        for n in range(2):
            source = cache_ref.at[pl.ds(n * rows, rows), cols]
            copies.append(load(source, part_ref.at[:, pl.ds(n * HEAD, HEAD)], sems.at[2 * e + n]))
    wait_all(copies)


def stack_kernel(q_ref, do_ref, after_ref, out_ref):
    rows = q_ref.shape[0] // 2
    for n, source_ref in enumerate((q_ref, do_ref)):
        for slot in range(2):
            for h in range(GROUP):
                out_ref[n, slot, h * rows : (h + 1) * rows, :] = source_ref[
                    slot * rows : (slot + 1) * rows, h * HEAD : (h + 1) * HEAD
                ]


def join_kernel(*refs):
    parts, (out_ref, sems) = refs[:-2], refs[-2:]
    kvh = len(parts)
    rows = parts[0].shape[0]
    copies = []
    for e, part_ref in enumerate(parts):
        source = lax.rem(lax.axis_index("kvh") + kvh - e, kvh)
        copies.append(load(part_ref, out_ref.at[at_rows(source * rows, rows)], sems.at[e]))
    wait_all(copies)


def stats_kernel(outer, members, order_ref, own_ref, other_ref, *refs):
    kv_refs, (out_ref, e_ref, dp_ref, ks_ref, m_ref, l_ref, d_ref, sems) = refs[:-8], refs[-8:]
    rows = ks_ref.shape[1] // len(members)
    work = Work(order_ref, rows, outer)
    copies = []
    for n, (d, kv_ref) in enumerate(zip(members, kv_refs)):
        for half in range(2):
            source = at_rows(work.key_slot(d, half) * rows, rows)
            copies.append(
                load(kv_ref.at[source], ks_ref.at[half, pl.ds(n * rows, rows)], sems.at[2 * n + half])
            )
    m_ref[...] = jnp.full(m_ref.shape, LOWEST, jnp.float32)
    l_ref[...] = jnp.zeros(l_ref.shape, jnp.float32)
    d_ref[...] = jnp.zeros(d_ref.shape, jnp.float32)
    wait_all(copies)
    qd_refs = (own_ref, other_ref)

    def maximum(owner, q_half, k_half, first, size, place, masked):
        slot = work.query_slot(owner, q_half)
        scores = lax.dot_general(
            ks_ref[k_half, pl.ds(first, size), :HEAD],
            qd_refs[owner][0, slot],
            ROWS_DOT_ROWS,
            preferred_element_type=jnp.float32,
        )
        if masked:
            key = lax.broadcasted_iota(jnp.int32, scores.shape, 0)
            query = lax.rem(lax.broadcasted_iota(jnp.int32, (1, scores.shape[1]), 1), rows)
            scores = jnp.where(key <= query, scores, LOWEST)
        e_ref[owner, pl.ds(place, size), :] = scores
        m_ref[owner, q_half] = jnp.maximum(
            m_ref[owner, q_half], jnp.max(scores, axis=0, keepdims=True)
        )
        dp_ref[owner, pl.ds(place, size), :] = lax.dot_general(
            ks_ref[k_half, pl.ds(first, size), HEAD:],
            qd_refs[owner][1, slot],
            ROWS_DOT_ROWS,
            preferred_element_type=jnp.float32,
        )

    work.blocks(members, maximum)

    def sums(owner, q_half, k_half, first, size, place, masked):
        scores = e_ref[owner, pl.ds(place, size), :]
        grads = dp_ref[owner, pl.ds(place, size), :]
        expon = jnp.exp2((scores - m_ref[owner, q_half]) * EXPONENT_SCALE)
        e_ref[owner, pl.ds(place, size), :] = expon
        l_ref[owner, q_half] = l_ref[owner, q_half] + jnp.sum(expon, axis=0, keepdims=True)
        d_ref[owner, q_half] = d_ref[owner, q_half] + jnp.sum(expon * grads, axis=0, keepdims=True)

    work.blocks(members, sums)
    for owner in range(2):
        for half in range(2):
            base = (2 * owner + half) * 3
            out_ref[base : base + 1, :] = m_ref[owner, half]
            out_ref[base + 1 : base + 2, :] = l_ref[owner, half]
            out_ref[base + 2 : base + 3, :] = d_ref[owner, half]


def merged(stats_refs, base):
    rows = [ref[base : base + 3, :] for ref in stats_refs]
    top = functools.reduce(jnp.maximum, [part[:1] for part in rows])
    weights = [jnp.exp2((part[:1] - top) * EXPONENT_SCALE) for part in rows]
    total = sum(weight * part[1:2] for weight, part in zip(weights, rows))
    delta = sum(weight * part[2:3] for weight, part in zip(weights, rows))
    return top, total, delta


def merge_kernel(first_ref, second_ref, out_ref):
    for base in range(0, 12, 3):
        for n, row in enumerate(merged((first_ref, second_ref), base)):
            out_ref[base + n : base + n + 1, :] = row


def grads_kernel(outer, groups, order_ref, own_ref, other_ref, *refs):
    count = len(groups)
    stats_refs, theirs_ref, refs = refs[:count], refs[count], refs[count + 1 :]
    e_refs, dp_refs, refs = refs[:count], refs[count : 2 * count], refs[2 * count :]
    term_refs, gs_refs, refs = refs[:outer], refs[outer : outer + count], refs[outer + count :]
    acc_refs, (w_ref, d_ref) = refs[:count], refs[count:]
    rows = term_refs[0].shape[0] // 2
    work = Work(order_ref, rows, outer)
    for owner in range(2):
        for half in range(2):
            base = (2 * owner + half) * 3
            base2 = (2 * (1 - owner) + half) * 3
            mine = merged(stats_refs, base)
            theirs = [theirs_ref[base2 + n : base2 + n + 1, :] for n in range(3)]
            top = jnp.maximum(mine[0], theirs[0])
            w1 = jnp.exp2((mine[0] - top) * EXPONENT_SCALE)
            w2 = jnp.exp2((theirs[0] - top) * EXPONENT_SCALE)
            total = w1 * mine[1] + w2 * theirs[1]
            d_ref[owner, half] = (w1 * mine[2] + w2 * theirs[2]) / total
            for n, stats_ref in enumerate(stats_refs):
                weight = jnp.exp2((stats_ref[base : base + 1, :] - top) * EXPONENT_SCALE)
                w_ref[n, owner, half] = weight / total
    qd_refs = (own_ref, other_ref)

    for n, members in enumerate(groups):
        acc_ref = acc_refs[n]
        acc_ref[...] = jnp.zeros(acc_ref.shape, jnp.float32)

        def gradients(owner, q_half, k_half, first, size, place, masked):
            slot = work.query_slot(owner, q_half)
            here = pl.ds(place, size)
            probs = e_refs[n][owner, here, :] * w_ref[n, owner, q_half]
            grads = (probs * (dp_refs[n][owner, here, :] - d_ref[owner, q_half])).astype(jnp.bfloat16)
            gs_refs[n][owner, here, :] = grads
            keys = pl.ds(first, size)
            acc_ref[k_half, keys, HEAD:] = acc_ref[k_half, keys, HEAD:] + jnp.dot(
                probs.astype(jnp.bfloat16), qd_refs[owner][1, slot], preferred_element_type=jnp.float32
            )
            acc_ref[k_half, keys, :HEAD] = acc_ref[k_half, keys, :HEAD] + jnp.dot(
                grads, qd_refs[owner][0, slot], preferred_element_type=jnp.float32
            )

        work.blocks(members, gradients)
        for at, d in enumerate(members):
            term_ref = term_refs[d]
            for half in range(2):
                target = at_rows(work.key_slot(d, half) * rows, rows)
                source = slice(at * rows, (at + 1) * rows)
                term_ref[target, :HEAD] = (acc_ref[half, source, :HEAD] * SCALE).astype(term_ref.dtype)
                term_ref[target, HEAD:] = acc_ref[half, source, HEAD:].astype(term_ref.dtype)


def query_kernel(outer, groups, order_ref, after_ref, *refs):
    count = len(groups)
    gs_refs, ks_refs, (own_ref, other_ref, acc_ref) = refs[:count], refs[count : 2 * count], refs[2 * count :]
    rows = own_ref.shape[0] // 2
    work = Work(order_ref, rows, outer)
    acc_ref[...] = jnp.zeros(acc_ref.shape, jnp.float32)

    for n, members in enumerate(groups):

        def terms(owner, q_half, k_half, first, size, place, masked):
            acc_ref[owner, q_half] = acc_ref[owner, q_half] + lax.dot_general(
                ks_refs[n][k_half, pl.ds(first, size), :HEAD],
                gs_refs[n][owner, pl.ds(place, size), :],
                COLS_DOT_COLS,
                preferred_element_type=jnp.float32,
            )

        work.blocks(members, terms)
    for owner, target in ((0, own_ref), (1, other_ref)):
        for half in range(2):
            place = at_rows(work.query_slot(owner, half) * rows, rows)
            grads = (jnp.transpose(acc_ref[owner, half]) * SCALE).astype(target.dtype)
            for h in range(GROUP):
                target[place, h * HEAD : (h + 1) * HEAD] = grads[h * rows : (h + 1) * rows, :]


def sum_kernel(outer, *refs):
    terms, outs, total_ref = refs[:outer], refs[outer:-1], refs[-1]
    total = terms[0][...]
    for term_ref in terms[1:]:
        total = total + term_ref[...].astype(jnp.float32)
    total_ref[...] = total
    kvh = len(outs)
    rows = outs[0].shape[0]
    for e, out_ref in enumerate(outs):
        target = lax.rem(lax.axis_index("kvh") + e, kvh)
        out_ref[...] = total_ref[at_rows(target * rows, rows), :].astype(jnp.bfloat16)


def place_kernel(own_ref, received_ref, *refs):
    parts, (dq_out, key_out, value_out, dq_ref, sems) = refs[:-5], refs[-5:]
    kvh = len(parts)
    copies = []
    for e, part_ref in enumerate(parts):
        head = lax.rem(lax.axis_index("kvh") + kvh - e, kvh)
        cols = at_rows(head * HEAD, HEAD)
        copies.append(load(part_ref.at[:, pl.ds(0, HEAD)], key_out.at[:, cols], sems.at[2 * e]))
        copies.append(load(part_ref.at[:, pl.ds(HEAD, HEAD)], value_out.at[:, cols], sems.at[2 * e + 1]))
    dq_ref[...] = (own_ref[...] + received_ref[...].astype(jnp.float32)).astype(jnp.bfloat16)
    copies.append(load(dq_ref, dq_out, sems.at[2 * kvh]))
    wait_all(copies)


def per_device(queries, keys, values, d_out, slab_order):
    kvh = lax.axis_size("kvh")
    outer = lax.axis_size("outer")
    local_rows, query_width = queries.shape
    cache_rows = keys.shape[0]
    slab_rows = local_rows // 2
    columns = GROUP * slab_rows
    params = pltpu.CompilerParams(vmem_limit_bytes=(8 << 20) + (10 << 10) * outer * local_rows)
    beside = pl.CostEstimate(flops=2 * 10**10, bytes_accessed=10**6, transcendentals=0)
    vmem = pl.BlockSpec(memory_space=pltpu.VMEM)
    smem = pl.BlockSpec(memory_space=pltpu.SMEM)
    anywhere = pl.BlockSpec(memory_space=pl.ANY)
    shape = jax.ShapeDtypeStruct
    dma = pltpu.SemaphoreType.DMA
    low, full = jnp.bfloat16, jnp.float32

    def call(kernel, name, **arguments):
        return pl.pallas_call(kernel, compiler_params=params, name=name, **arguments)

    def shift(array, axis, by):
        size = lax.axis_size(axis)
        return lax.ppermute(array, axis, [(n, (n + by) % size) for n in range(size)])

    part = shape((cache_rows, 2 * HEAD), low)
    block = shape((local_rows, 2 * HEAD), low)
    parts = call(
        split_kernel,
        "split",
        out_shape=(part,) * kvh,
        in_specs=[vmem],
        out_specs=(vmem,) * kvh,
        scratch_shapes=[dma((2 * kvh,))],
    )(jnp.concatenate([keys, values], axis=0))
    own_qd = call(
        stack_kernel,
        "stack",
        out_shape=shape((2, 2, columns, HEAD), low),
        in_specs=[vmem, vmem, anywhere],
        out_specs=vmem,
        cost_estimate=beside,
    )(queries, d_out, parts[0])
    parts = [parts[0]] + [shift(parts[e], "kvh", e) for e in range(1, kvh)]
    other_qd = shift(own_qd, "pair", 1)
    own_block = call(
        join_kernel,
        "join",
        out_shape=block,
        in_specs=[anywhere] * kvh,
        out_specs=vmem,
        scratch_shapes=[dma((kvh,))],
    )(*parts)
    blocks = [own_block] + [shift(own_block, "outer", d) for d in range(1, outer)]

    far = outer // 2 + 1
    groups = [[0, *range(far, outer)], list(range(1, far))]
    all_stats = shape((12, columns), full)
    row_stat = pltpu.VMEM((2, 2, 1, columns), full)
    results = []
    for n, members in enumerate(groups):
        half_rows = len(members) * slab_rows
        score_rows = (2, 2 * half_rows + slab_rows, columns)
        results.append(
            call(
                functools.partial(stats_kernel, outer, members),
                "stats",
                out_shape=(
                    all_stats,
                    shape(score_rows, full),
                    shape(score_rows, full),
                    shape((2, half_rows, 2 * HEAD), low),
                ),
                in_specs=[smem, vmem, vmem] + [anywhere] * len(members),
                out_specs=(vmem,) * 4,
                scratch_shapes=[row_stat, row_stat, row_stat, dma((2 * len(members),))],
                cost_estimate=beside if n == 0 else None,
            )(slab_order, own_qd, other_qd, *[blocks[d] for d in members])
        )
    stats, expon, grad_probs, sorted_keys = zip(*results)
    mine = call(
        merge_kernel, "merge", out_shape=all_stats, in_specs=[vmem, vmem], out_specs=vmem
    )(*stats)
    theirs = shift(mine, "pair", 1)
    count = len(groups)
    grads = call(
        functools.partial(grads_kernel, outer, groups),
        "grads",
        out_shape=(shape(block.shape, full),)
        + (block,) * (outer - 1)
        + tuple(shape(scores.shape, low) for scores in expon),
        in_specs=[smem] + [vmem] * (3 + 3 * count),
        out_specs=(vmem,) * (outer + count),
        scratch_shapes=[pltpu.VMEM(keys_low.shape, full) for keys_low in sorted_keys]
        + [pltpu.VMEM((count, 2, 2, 1, columns), full), row_stat],
    )(slab_order, own_qd, other_qd, *stats, theirs, *expon, *grad_probs)
    terms, score_grads = grads[:outer], grads[outer:]
    terms = [terms[0]] + [shift(terms[d], "outer", -d) for d in range(1, outer)]
    own_grads, other_grads = call(
        functools.partial(query_kernel, outer, groups),
        "query_terms",
        out_shape=(shape(queries.shape, full), shape(queries.shape, low)),
        in_specs=[smem, anywhere] + [vmem] * (2 * count),
        out_specs=(vmem, vmem),
        scratch_shapes=[pltpu.VMEM((2, 2, HEAD, columns), full)],
        cost_estimate=beside,
    )(slab_order, terms[1], *score_grads, *sorted_keys)
    received_grads = shift(other_grads, "pair", 1)
    owned = call(
        functools.partial(sum_kernel, outer),
        "sum",
        out_shape=(part,) * kvh,
        in_specs=[vmem] * outer,
        out_specs=(vmem,) * kvh,
        scratch_shapes=[pltpu.VMEM(block.shape, full)],
    )(*terms)
    owned = [owned[0]] + [shift(owned[e], "kvh", e) for e in range(1, kvh)]
    return call(
        place_kernel,
        "place",
        out_shape=(shape(queries.shape, low), shape(keys.shape, low), shape(values.shape, low)),
        in_specs=[vmem, vmem] + [anywhere] * kvh,
        out_specs=(anywhere,) * 3,
        scratch_shapes=[pltpu.VMEM(queries.shape, low), dma((2 * kvh + 1,))],
    )(own_grads, received_grads, *owned)


def solution(mesh):
    kvh = mesh.shape["kvh"]
    pairs = mesh.shape["seq"] // 2
    paired = Mesh(mesh.devices.reshape(pairs, 2, kvh), ("outer", "pair", "kvh"))
    seq = ("outer", "pair")
    cache = P(("outer", "pair", "kvh"), None)
    placed = (P(seq, "kvh"), cache, cache, P(seq, "kvh"), P())
    return jax.shard_map(
        per_device,
        mesh=paired,
        in_specs=placed,
        out_specs=(P(seq, "kvh"), cache, cache),
        check_vma=False,
    )
```

```python
import functools
import math

import jax
import jax.numpy as jnp
from jax import lax
from jax.experimental import pallas as pl
from jax.experimental.pallas import tpu as pltpu
from jax.sharding import Mesh
from jax.sharding import PartitionSpec as P

HEADS = 20
KV_HEADS = 4
HEAD = 128
GROUP = HEADS // KV_HEADS
SCALE = HEAD ** (-0.5)
EXPONENT_SCALE = SCALE * math.log2(math.e)
LOWEST = -1e30
ROWS_DOT_ROWS = (((1,), (1,)), ((), ()))
COLS_DOT_COLS = (((0,), (0,)), ((), ()))


def at_rows(start, size):
    return pl.ds(pl.multiple_of(start, size), size)


def load(source_ref, target_ref, sem):
    copy = pltpu.make_async_copy(source_ref, target_ref, sem)
    copy.start()
    return copy


def wait_all(copies):
    for copy in copies:
        copy.wait()


class Work:
    def __init__(self, order_ref, slab_rows, outer):
        self.slab_rows = slab_rows
        at, side = lax.axis_index("outer"), lax.axis_index("pair")

        def pair_of(index):
            first, second = order_ref[2 * index], order_ref[2 * index + 1]
            return jnp.minimum(first, second), jnp.where(first < second, 0, 1)

        self.owners = [pair_of(2 * at + side), pair_of(2 * at + 1 - side)]
        self.pairs = [pair_of(2 * lax.rem(at + outer - d, outer) + side) for d in range(outer)]

    def query_slot(self, owner, half):
        place = self.owners[owner][1]
        return jnp.where(half == 0, place, 1 - place)

    def key_slot(self, d, half):
        place = self.pairs[d][1]
        return place if half == 0 else 1 - place

    def blocks(self, members, body):
        rows = self.slab_rows
        half_rows = len(members) * rows
        chunk = math.gcd(256, half_rows)
        for owner in range(2):
            for first in range(0, half_rows, chunk):
                body(owner, 1, 0, first, chunk, first, False)
            for n, d in enumerate(members):
                if owner == 0 and d == 0:
                    body(owner, 0, 0, n * rows, rows, half_rows + n * rows, True)
                    body(owner, 1, 1, n * rows, rows, 2 * half_rows, True)
                else:
                    half = jnp.where(self.owners[owner][0] >= self.pairs[d][0], 0, 1)
                    body(owner, half, half, n * rows, rows, half_rows + n * rows, False)


def split_kernel(cache_ref, *refs):
    parts, sems = refs[:-1], refs[-1]
    kvh = len(parts)
    rows = parts[0].shape[0]
    copies = []
    for e, part_ref in enumerate(parts):
        head = lax.rem(lax.axis_index("kvh") + e, kvh)
        cols = at_rows(head * HEAD, HEAD)
        for n in range(2):
            source = cache_ref.at[pl.ds(n * rows, rows), cols]
            copies.append(load(source, part_ref.at[:, pl.ds(n * HEAD, HEAD)], sems.at[2 * e + n]))
    wait_all(copies)


def stack_kernel(q_ref, do_ref, after_ref, out_ref):
    rows = q_ref.shape[0] // 2
    for n, source_ref in enumerate((q_ref, do_ref)):
        for slot in range(2):
            for h in range(GROUP):
                out_ref[n, slot, h * rows : (h + 1) * rows, :] = source_ref[
                    slot * rows : (slot + 1) * rows, h * HEAD : (h + 1) * HEAD
                ]


def join_kernel(*refs):
    parts, (out_ref, sems) = refs[:-2], refs[-2:]
    kvh = len(parts)
    rows = parts[0].shape[0]
    copies = []
    for e, part_ref in enumerate(parts):
        source = lax.rem(lax.axis_index("kvh") + kvh - e, kvh)
        copies.append(load(part_ref, out_ref.at[at_rows(source * rows, rows)], sems.at[e]))
    wait_all(copies)


def stats_kernel(outer, members, order_ref, own_ref, other_ref, *refs):
    refs = refs[:len(members)] + refs[-8:]
    kv_refs, (out_ref, e_ref, dp_ref, ks_ref, m_ref, l_ref, d_ref, sems) = refs[:-8], refs[-8:]
    rows = ks_ref.shape[1] // len(members)
    work = Work(order_ref, rows, outer)
    copies = []
    for n, (d, kv_ref) in enumerate(zip(members, kv_refs)):
        for half in range(2):
            source = at_rows(work.key_slot(d, half) * rows, rows)
            copies.append(
                load(kv_ref.at[source], ks_ref.at[half, pl.ds(n * rows, rows)], sems.at[2 * n + half])
            )
    m_ref[...] = jnp.full(m_ref.shape, LOWEST, jnp.float32)
    l_ref[...] = jnp.zeros(l_ref.shape, jnp.float32)
    d_ref[...] = jnp.zeros(d_ref.shape, jnp.float32)
    wait_all(copies)
    qd_refs = (own_ref, other_ref)

    def maximum(owner, q_half, k_half, first, size, place, masked):
        slot = work.query_slot(owner, q_half)
        scores = lax.dot_general(
            ks_ref[k_half, pl.ds(first, size), :HEAD],
            qd_refs[owner][0, slot],
            ROWS_DOT_ROWS,
            preferred_element_type=jnp.float32,
        )
        if masked:
            key = lax.broadcasted_iota(jnp.int32, scores.shape, 0)
            query = lax.rem(lax.broadcasted_iota(jnp.int32, (1, scores.shape[1]), 1), rows)
            scores = jnp.where(key <= query, scores, LOWEST)
        e_ref[owner, pl.ds(place, size), :] = scores
        m_ref[owner, q_half] = jnp.maximum(
            m_ref[owner, q_half], jnp.max(scores, axis=0, keepdims=True)
        )
        dp_ref[owner, pl.ds(place, size), :] = lax.dot_general(
            ks_ref[k_half, pl.ds(first, size), HEAD:],
            qd_refs[owner][1, slot],
            ROWS_DOT_ROWS,
            preferred_element_type=jnp.float32,
        )

    work.blocks(members, maximum)

    def sums(owner, q_half, k_half, first, size, place, masked):
        scores = e_ref[owner, pl.ds(place, size), :]
        grads = dp_ref[owner, pl.ds(place, size), :]
        expon = jnp.exp2((scores - m_ref[owner, q_half]) * EXPONENT_SCALE)
        e_ref[owner, pl.ds(place, size), :] = expon
        l_ref[owner, q_half] = l_ref[owner, q_half] + jnp.sum(expon, axis=0, keepdims=True)
        d_ref[owner, q_half] = d_ref[owner, q_half] + jnp.sum(expon * grads, axis=0, keepdims=True)

    work.blocks(members, sums)
    for owner in range(2):
        for half in range(2):
            base = (2 * owner + half) * 3
            out_ref[base : base + 1, :] = m_ref[owner, half]
            out_ref[base + 1 : base + 2, :] = l_ref[owner, half]
            out_ref[base + 2 : base + 3, :] = d_ref[owner, half]


def merged(stats_refs, base):
    rows = [ref[base : base + 3, :] for ref in stats_refs]
    top = functools.reduce(jnp.maximum, [part[:1] for part in rows])
    weights = [jnp.exp2((part[:1] - top) * EXPONENT_SCALE) for part in rows]
    total = sum(weight * part[1:2] for weight, part in zip(weights, rows))
    delta = sum(weight * part[2:3] for weight, part in zip(weights, rows))
    return top, total, delta


def merge_kernel(*refs):
    stats_refs, out_ref = refs[:-1], refs[-1]
    for base in range(0, 12, 3):
        for n, row in enumerate(merged(stats_refs, base)):
            out_ref[base + n : base + n + 1, :] = row


def grads_kernel(outer, groups, order_ref, own_ref, other_ref, *refs):
    count = len(groups)
    stats_refs, theirs_ref, refs = refs[:count], refs[count], refs[count + 1 :]
    e_refs, dp_refs, refs = refs[:count], refs[count : 2 * count], refs[2 * count :]
    term_refs, gs_refs, refs = refs[:outer], refs[outer : outer + count], refs[outer + count :]
    acc_refs, (w_ref, d_ref) = refs[:count], refs[count:]
    rows = term_refs[0].shape[0] // 2
    work = Work(order_ref, rows, outer)
    for owner in range(2):
        for half in range(2):
            base = (2 * owner + half) * 3
            base2 = (2 * (1 - owner) + half) * 3
            mine = merged(stats_refs, base)
            theirs = [theirs_ref[base2 + n : base2 + n + 1, :] for n in range(3)]
            top = jnp.maximum(mine[0], theirs[0])
            w1 = jnp.exp2((mine[0] - top) * EXPONENT_SCALE)
            w2 = jnp.exp2((theirs[0] - top) * EXPONENT_SCALE)
            total = w1 * mine[1] + w2 * theirs[1]
            d_ref[owner, half] = (w1 * mine[2] + w2 * theirs[2]) / total
            for n, stats_ref in enumerate(stats_refs):
                weight = jnp.exp2((stats_ref[base : base + 1, :] - top) * EXPONENT_SCALE)
                w_ref[n, owner, half] = weight / total
    qd_refs = (own_ref, other_ref)

    for n, members in enumerate(groups):
        acc_ref = acc_refs[n]
        acc_ref[...] = jnp.zeros(acc_ref.shape, jnp.float32)

        def gradients(owner, q_half, k_half, first, size, place, masked):
            slot = work.query_slot(owner, q_half)
            here = pl.ds(place, size)
            probs = e_refs[n][owner, here, :] * w_ref[n, owner, q_half]
            grads = (probs * (dp_refs[n][owner, here, :] - d_ref[owner, q_half])).astype(jnp.bfloat16)
            gs_refs[n][owner, here, :] = grads
            keys = pl.ds(first, size)
            acc_ref[k_half, keys, HEAD:] = acc_ref[k_half, keys, HEAD:] + jnp.dot(
                probs.astype(jnp.bfloat16), qd_refs[owner][1, slot], preferred_element_type=jnp.float32
            )
            acc_ref[k_half, keys, :HEAD] = acc_ref[k_half, keys, :HEAD] + jnp.dot(
                grads, qd_refs[owner][0, slot], preferred_element_type=jnp.float32
            )

        work.blocks(members, gradients)
        for at, d in enumerate(members):
            term_ref = term_refs[d]
            for half in range(2):
                target = at_rows(work.key_slot(d, half) * rows, rows)
                source = slice(at * rows, (at + 1) * rows)
                term_ref[target, :HEAD] = (acc_ref[half, source, :HEAD] * SCALE).astype(term_ref.dtype)
                term_ref[target, HEAD:] = acc_ref[half, source, HEAD:].astype(term_ref.dtype)


def query_kernel(outer, groups, order_ref, *refs):
    count = len(groups)
    gs_refs, ks_refs, (own_ref, other_ref, acc_ref) = refs[:count], refs[count : 2 * count], refs[2 * count :]
    rows = own_ref.shape[0] // 2
    work = Work(order_ref, rows, outer)
    acc_ref[...] = jnp.zeros(acc_ref.shape, jnp.float32)

    for n, members in enumerate(groups):

        def terms(owner, q_half, k_half, first, size, place, masked):
            acc_ref[owner, q_half] = acc_ref[owner, q_half] + lax.dot_general(
                ks_refs[n][k_half, pl.ds(first, size), :HEAD],
                gs_refs[n][owner, pl.ds(place, size), :],
                COLS_DOT_COLS,
                preferred_element_type=jnp.float32,
            )

        work.blocks(members, terms)
    for owner, target in ((0, own_ref), (1, other_ref)):
        for half in range(2):
            place = at_rows(work.query_slot(owner, half) * rows, rows)
            grads = (jnp.transpose(acc_ref[owner, half]) * SCALE).astype(target.dtype)
            for h in range(GROUP):
                target[place, h * HEAD : (h + 1) * HEAD] = grads[h * rows : (h + 1) * rows, :]


def sum_kernel(outer, *refs):
    terms, outs, total_ref = refs[:outer], refs[outer:-1], refs[-1]
    total = terms[0][...]
    for term_ref in terms[1:]:
        total = total + term_ref[...].astype(jnp.float32)
    total_ref[...] = total
    kvh = len(outs)
    rows = outs[0].shape[0]
    for e, out_ref in enumerate(outs):
        target = lax.rem(lax.axis_index("kvh") + e, kvh)
        out_ref[...] = total_ref[at_rows(target * rows, rows), :].astype(jnp.bfloat16)


def place_kernel(own_ref, received_ref, *refs):
    parts, (dq_out, key_out, value_out, dq_ref, sems) = refs[:-5], refs[-5:]
    kvh = len(parts)
    copies = []
    for e, part_ref in enumerate(parts):
        head = lax.rem(lax.axis_index("kvh") + kvh - e, kvh)
        cols = at_rows(head * HEAD, HEAD)
        copies.append(load(part_ref.at[:, pl.ds(0, HEAD)], key_out.at[:, cols], sems.at[2 * e]))
        copies.append(load(part_ref.at[:, pl.ds(HEAD, HEAD)], value_out.at[:, cols], sems.at[2 * e + 1]))
    dq_ref[...] = (own_ref[...] + received_ref[...].astype(jnp.float32)).astype(jnp.bfloat16)
    copies.append(load(dq_ref, dq_out, sems.at[2 * kvh]))
    wait_all(copies)


def per_device(queries, keys, values, d_out, slab_order):
    kvh = lax.axis_size("kvh")
    outer = lax.axis_size("outer")
    local_rows, query_width = queries.shape
    cache_rows = keys.shape[0]
    slab_rows = local_rows // 2
    columns = GROUP * slab_rows
    params = pltpu.CompilerParams(vmem_limit_bytes=(8 << 20) + (10 << 10) * outer * local_rows)
    beside = pl.CostEstimate(flops=2 * 10**10, bytes_accessed=10**6, transcendentals=0)
    vmem = pl.BlockSpec(memory_space=pltpu.VMEM)
    smem = pl.BlockSpec(memory_space=pltpu.SMEM)
    anywhere = pl.BlockSpec(memory_space=pl.ANY)
    shape = jax.ShapeDtypeStruct
    dma = pltpu.SemaphoreType.DMA
    low, full = jnp.bfloat16, jnp.float32

    def call(kernel, name, **arguments):
        return pl.pallas_call(kernel, compiler_params=params, name=name, **arguments)

    def shift(array, axis, by):
        size = lax.axis_size(axis)
        return lax.ppermute(array, axis, [(n, (n + by) % size) for n in range(size)])

    part = shape((cache_rows, 2 * HEAD), low)
    block = shape((local_rows, 2 * HEAD), low)
    parts = call(
        split_kernel,
        "split",
        out_shape=(part,) * kvh,
        in_specs=[vmem],
        out_specs=(vmem,) * kvh,
        scratch_shapes=[dma((2 * kvh,))],
    )(jnp.concatenate([keys, values], axis=0))
    own_qd = call(
        stack_kernel,
        "stack",
        out_shape=shape((2, 2, columns, HEAD), low),
        in_specs=[vmem, vmem, anywhere],
        out_specs=vmem,
        cost_estimate=beside,
    )(queries, d_out, parts[0])
    parts = [parts[0]] + [shift(parts[e], "kvh", e) for e in range(1, kvh)]
    other_qd = shift(own_qd, "pair", 1)
    own_block = call(
        join_kernel,
        "join",
        out_shape=block,
        in_specs=[anywhere] * kvh,
        out_specs=vmem,
        scratch_shapes=[dma((kvh,))],
        cost_estimate=beside,
    )(*parts)
    blocks = [own_block] + [shift(own_block, "outer", d) for d in range(1, outer)]

    far = outer // 2 + 1
    groups = [[0, *range(far, outer)], list(range(2, far)), [1]]
    groups = [members for members in groups if members]
    all_stats = shape((12, columns), full)
    row_stat = pltpu.VMEM((2, 2, 1, columns), full)
    results = []
    for n, members in enumerate(groups):
        half_rows = len(members) * slab_rows
        score_rows = (2, 2 * half_rows + slab_rows, columns)
        results.append(
            call(
                functools.partial(stats_kernel, outer, members),
                "stats",
                out_shape=(
                    all_stats,
                    shape(score_rows, full),
                    shape(score_rows, full),
                    shape((2, half_rows, 2 * HEAD), low),
                ),
                in_specs=[smem, vmem, vmem] + [anywhere] * (len(members) + min(n, 1)),
                out_specs=(vmem,) * 4,
                scratch_shapes=[row_stat, row_stat, row_stat, dma((2 * len(members),))],
                cost_estimate=beside if n + 1 < len(groups) else None,
            )(slab_order, own_qd, other_qd, *[blocks[d] for d in members], *[done[0] for done in results[-1:]])
        )
    stats, expon, grad_probs, sorted_keys = zip(*results)
    mine = call(
        merge_kernel, "merge", out_shape=all_stats, in_specs=[vmem] * len(stats), out_specs=vmem
    )(*stats)
    theirs = shift(mine, "pair", 1)
    count = len(groups)
    grads = call(
        functools.partial(grads_kernel, outer, groups),
        "grads",
        out_shape=(shape(block.shape, full),)
        + (block,) * (outer - 1)
        + tuple(shape(scores.shape, low) for scores in expon),
        in_specs=[smem] + [vmem] * (3 + 3 * count),
        out_specs=(vmem,) * (outer + count),
        scratch_shapes=[pltpu.VMEM(keys_low.shape, full) for keys_low in sorted_keys]
        + [pltpu.VMEM((count, 2, 2, 1, columns), full), row_stat],
    )(slab_order, own_qd, other_qd, *stats, theirs, *expon, *grad_probs)
    terms, score_grads = grads[:outer], grads[outer:]
    terms = [terms[0]] + [shift(terms[d], "outer", -d) for d in range(1, outer)]
    own_grads, other_grads = call(
        functools.partial(query_kernel, outer, groups),
        "query_terms",
        out_shape=(shape(queries.shape, full), shape(queries.shape, low)),
        in_specs=[smem] + [vmem] * (2 * count),
        out_specs=(vmem, vmem),
        scratch_shapes=[pltpu.VMEM((2, 2, HEAD, columns), full)],
        cost_estimate=beside,
    )(slab_order, *score_grads, *sorted_keys)
    received_grads = shift(other_grads, "pair", 1)
    owned = call(
        functools.partial(sum_kernel, outer),
        "sum",
        out_shape=(part,) * kvh,
        in_specs=[vmem] * outer,
        out_specs=(vmem,) * kvh,
        scratch_shapes=[pltpu.VMEM(block.shape, full)],
        cost_estimate=beside,
    )(*terms)
    owned = [owned[0]] + [shift(owned[e], "kvh", e) for e in range(1, kvh)]
    return call(
        place_kernel,
        "place",
        out_shape=(shape(queries.shape, low), shape(keys.shape, low), shape(values.shape, low)),
        in_specs=[vmem, vmem] + [anywhere] * kvh,
        out_specs=(anywhere,) * 3,
        scratch_shapes=[pltpu.VMEM(queries.shape, low), dma((2 * kvh + 1,))],
    )(own_grads, received_grads, *owned)


def solution(mesh):
    kvh = mesh.shape["kvh"]
    pairs = mesh.shape["seq"] // 2
    paired = Mesh(mesh.devices.reshape(pairs, 2, kvh), ("outer", "pair", "kvh"))
    seq = ("outer", "pair")
    cache = P(("outer", "pair", "kvh"), None)
    placed = (P(seq, "kvh"), cache, cache, P(seq, "kvh"), P())
    return jax.shard_map(
        per_device,
        mesh=paired,
        in_specs=placed,
        out_specs=(P(seq, "kvh"), cache, cache),
        check_vma=False,
    )
```

```python
import functools
import math

import jax
import jax.numpy as jnp
from jax import lax
from jax.experimental import pallas as pl
from jax.experimental.pallas import tpu as pltpu
from jax.sharding import Mesh
from jax.sharding import PartitionSpec as P

HEADS = 20
KV_HEADS = 4
HEAD = 128
GROUP = HEADS // KV_HEADS
SCALE = HEAD ** (-0.5)
EXPONENT_SCALE = SCALE * math.log2(math.e)
LOWEST = -1e30
ROWS_DOT_ROWS = (((1,), (1,)), ((), ()))
COLS_DOT_COLS = (((0,), (0,)), ((), ()))


def at_rows(start, size):
    return pl.ds(pl.multiple_of(start, size), size)


def load(source_ref, target_ref, sem):
    copy = pltpu.make_async_copy(source_ref, target_ref, sem)
    copy.start()
    return copy


def wait_all(copies):
    for copy in copies:
        copy.wait()


def partner(index, distance, size):
    if size & (size - 1) == 0:
        return index ^ distance
    return (index + size - distance) % size


def target_of(index, distance, size):
    if size & (size - 1) == 0:
        return index ^ distance
    return (index + distance) % size


def pick(condition, chosen, other):
    return lax.select(condition, chosen, jnp.full_like(chosen, other))


class Work:
    def __init__(self, order_ref, rows, outer, members, block_refs):
        self.rows, self.members, self.block_refs = rows, members, block_refs
        self.low_rows = len(members) * rows
        at, side = lax.axis_index("outer"), lax.axis_index("pair")

        def pair_of(index):
            first, second = order_ref[2 * index], order_ref[2 * index + 1]
            return jnp.minimum(first, second), jnp.where(first < second, 0, 1)

        self.owners = [pair_of(2 * at + side), pair_of(2 * at + 1 - side)]
        self.pairs = [pair_of(2 * partner(at, d, outer) + side) for d in members]

    @staticmethod
    def slot(place, half):
        return jnp.where(half == 0, place, 1 - place)

    def query_slot(self, owner, half):
        return self.slot(self.owners[owner][1], half)

    def key_rows(self, n, half):
        return at_rows(self.slot(self.pairs[n][1], half) * self.rows, self.rows)

    def keys(self, n, half, cols):
        return self.block_refs[n][self.key_rows(n, half), cols]

    def low_keys(self, cols):
        return jnp.concatenate([self.keys(n, 0, cols) for n in range(len(self.members))], axis=0)

    def tiles(self, owner):
        found = []
        for n, d in enumerate(self.members):
            here = pl.ds(self.low_rows + n * self.rows, self.rows)
            if owner == 0 and d == 0:
                found.append((n, 0, here, True))
                found.append((n, 1, pl.ds(2 * self.low_rows, self.rows), True))
            else:
                half = jnp.where(self.owners[owner][0] >= self.pairs[n][0], 0, 1)
                found.append((n, half, here, False))
        return found


def split_kernel(cache_ref, *refs):
    parts, sems = refs[:-1], refs[-1]
    kvh = len(parts)
    rows = parts[0].shape[0]
    copies = []
    for e, part_ref in enumerate(parts):
        cols = at_rows(target_of(lax.axis_index("kvh"), e, kvh) * HEAD, HEAD)
        for n in range(2):
            source = cache_ref.at[pl.ds(n * rows, rows), cols]
            copies.append(load(source, part_ref.at[:, pl.ds(n * HEAD, HEAD)], sems.at[2 * e + n]))
    wait_all(copies)


def stack_kernel(q_ref, do_ref, after_ref, out_ref):
    rows = q_ref.shape[0] // 2
    for n, source_ref in enumerate((q_ref, do_ref)):
        for slot in range(2):
            for h in range(GROUP):
                out_ref[n, slot, h * rows : (h + 1) * rows, :] = source_ref[
                    slot * rows : (slot + 1) * rows, h * HEAD : (h + 1) * HEAD
                ]


def join_kernel(*refs):
    parts, (out_ref, sems) = refs[:-2], refs[-2:]
    kvh = len(parts)
    rows = parts[0].shape[0]
    copies = []
    for e, part_ref in enumerate(parts):
        source = partner(lax.axis_index("kvh"), e, kvh)
        copies.append(load(part_ref, out_ref.at[at_rows(source * rows, rows)], sems.at[e]))
    wait_all(copies)


def stats_kernel(outer, members, order_ref, own_ref, other_ref, *refs):
    block_refs, (out_ref, e_ref, dp_ref) = refs[: len(members)], refs[-3:]
    rows = block_refs[0].shape[0] // 2
    work = Work(order_ref, rows, outer, members, block_refs)
    low_part = pl.ds(0, work.low_rows)
    key_cols, value_cols = slice(0, HEAD), slice(HEAD, 2 * HEAD)

    def products(keys, queries):
        return lax.dot_general(keys, queries, ROWS_DOT_ROWS, preferred_element_type=jnp.float32)

    tops = []
    for owner, qd_ref in enumerate((own_ref, other_ref)):
        high = work.query_slot(owner, 1)
        scores = products(work.low_keys(key_cols), qd_ref[0, high])
        e_ref[owner, low_part, :] = scores
        dp_ref[owner, low_part, :] = products(work.low_keys(value_cols), qd_ref[1, high])
        top = [jnp.full((1, scores.shape[1]), LOWEST, jnp.float32), jnp.max(scores, axis=0, keepdims=True)]
        for n, half, here, masked in work.tiles(owner):
            slot = work.query_slot(owner, half)
            scores = products(work.keys(n, half, key_cols), qd_ref[0, slot])
            if masked:
                key = lax.broadcasted_iota(jnp.int32, scores.shape, 0)
                query = lax.rem(lax.broadcasted_iota(jnp.int32, (1, scores.shape[1]), 1), rows)
                scores = jnp.where(key <= query, scores, LOWEST)
            e_ref[owner, here, :] = scores
            dp_ref[owner, here, :] = products(work.keys(n, half, value_cols), qd_ref[1, slot])
            most = jnp.max(scores, axis=0, keepdims=True)
            for side in range(2):
                seen = most if masked else pick(half == side, most, LOWEST)
                if not masked or half == side:
                    top[side] = jnp.maximum(top[side], seen)
        tops.append(top)

    for owner, top in enumerate(tops):

        def sums(here, most):
            expon = jnp.exp2((e_ref[owner, here, :] - most) * EXPONENT_SCALE)
            e_ref[owner, here, :] = expon
            return [
                jnp.sum(expon, axis=0, keepdims=True),
                jnp.sum(expon * dp_ref[owner, here, :], axis=0, keepdims=True),
            ]

        zero = jnp.zeros_like(top[0])
        totals = [[zero, zero], sums(low_part, top[1])]
        for n, half, here, masked in work.tiles(owner):
            part = sums(here, top[half] if masked else lax.select(half == 0, top[0], top[1]))
            for side in range(2):
                if not masked or half == side:
                    seen = part if masked else [pick(half == side, one, 0) for one in part]
                    totals[side] = [total + one for total, one in zip(totals[side], seen)]
        for half in range(2):
            base = (2 * owner + half) * 3
            for n, row in enumerate((top[half], *totals[half])):
                out_ref[base + n : base + n + 1, :] = row


def merged(stats_refs, base):
    rows = [ref[base : base + 3, :] for ref in stats_refs]
    top = functools.reduce(jnp.maximum, [part[:1] for part in rows])
    weights = [jnp.exp2((part[:1] - top) * EXPONENT_SCALE) for part in rows]
    total = sum(weight * part[1:2] for weight, part in zip(weights, rows))
    delta = sum(weight * part[2:3] for weight, part in zip(weights, rows))
    return top, total, delta


def merge_kernel(*refs):
    stats_refs, out_ref = refs[:-1], refs[-1]
    for base in range(0, 12, 3):
        for n, row in enumerate(merged(stats_refs, base)):
            out_ref[base + n : base + n + 1, :] = row


def grads_kernel(outer, groups, order_ref, own_ref, other_ref, *refs):
    count = len(groups)
    stats_refs, theirs_ref, refs = refs[:count], refs[count], refs[count + 1 :]
    e_refs, dp_refs, refs = refs[:count], refs[count : 2 * count], refs[2 * count :]
    term_refs, gs_refs = refs[:outer], refs[outer:]
    rows = term_refs[0].shape[0] // 2
    weights, deltas = [[] for _ in groups], []
    for owner in range(2):
        delta = []
        group_weights = [[] for _ in groups]
        for half in range(2):
            base = (2 * owner + half) * 3
            base2 = (2 * (1 - owner) + half) * 3
            mine = merged(stats_refs, base)
            theirs = [theirs_ref[base2 + n : base2 + n + 1, :] for n in range(3)]
            top = jnp.maximum(mine[0], theirs[0])
            w1 = jnp.exp2((mine[0] - top) * EXPONENT_SCALE)
            w2 = jnp.exp2((theirs[0] - top) * EXPONENT_SCALE)
            total = w1 * mine[1] + w2 * theirs[1]
            delta.append((w1 * mine[2] + w2 * theirs[2]) / total)
            for n, stats_ref in enumerate(stats_refs):
                weight = jnp.exp2((stats_ref[base : base + 1, :] - top) * EXPONENT_SCALE)
                group_weights[n].append(weight / total)
        deltas.append(delta)
        for n in range(count):
            weights[n].append(group_weights[n])

    for n, members in enumerate(groups):
        work = Work(order_ref, rows, outer, members, None)
        terms = [[None] * len(members), [None] * len(members)]

        def add(half, at, pair):
            old = terms[half][at]
            terms[half][at] = pair if old is None else [one + more for one, more in zip(old, pair)]

        for owner, qd_ref in enumerate((own_ref, other_ref)):

            def gradients(here, slot, weight, delta):
                probs = e_refs[n][owner, here, :] * weight
                grads = (probs * (dp_refs[n][owner, here, :] - delta)).astype(jnp.bfloat16)
                gs_refs[n][owner, here, :] = grads
                return [
                    jnp.dot(grads, qd_ref[0, slot], preferred_element_type=jnp.float32),
                    jnp.dot(probs.astype(jnp.bfloat16), qd_ref[1, slot], preferred_element_type=jnp.float32),
                ]

            weight, delta = weights[n][owner], deltas[owner]
            low_part = pl.ds(0, work.low_rows)
            part = gradients(low_part, work.query_slot(owner, 1), weight[1], delta[1])
            for at in range(len(members)):
                add(0, at, [one[at * rows : (at + 1) * rows] for one in part])
            for at, half, here, masked in work.tiles(owner):
                slot = work.query_slot(owner, half)
                if masked:
                    add(half, at, gradients(here, slot, weight[half], delta[half]))
                else:
                    is_low = half == 0
                    part = gradients(here, slot, lax.select(is_low, *weight), lax.select(is_low, *delta))
                    for side in range(2):
                        add(side, at, [pick(half == side, one, 0) for one in part])
        for at, d in enumerate(members):
            term_ref = term_refs[d]
            for half in range(2):
                target = work.key_rows(at, half)
                of_keys, of_values = terms[half][at]
                term_ref[target, :HEAD] = (of_keys * SCALE).astype(term_ref.dtype)
                term_ref[target, HEAD:] = of_values.astype(term_ref.dtype)


def query_kernel(outer, groups, order_ref, *refs):
    count = len(groups)
    block_refs, gs_refs, (own_ref, other_ref) = refs[:outer], refs[outer : outer + count], refs[outer + count :]
    rows = own_ref.shape[0] // 2
    works = [
        Work(order_ref, rows, outer, members, [block_refs[d] for d in members]) for members in groups
    ]
    cols = slice(0, HEAD)
    for owner, target in ((0, own_ref), (1, other_ref)):
        totals = [None, None]

        def add(half, part):
            totals[half] = part if totals[half] is None else totals[half] + part

        for gs_ref, work in zip(gs_refs, works):

            def terms(keys, here):
                return lax.dot_general(
                    keys, gs_ref[owner, here, :], COLS_DOT_COLS, preferred_element_type=jnp.float32
                )

            add(1, terms(work.low_keys(cols), pl.ds(0, work.low_rows)))
            for n, half, here, masked in work.tiles(owner):
                part = terms(work.keys(n, half, cols), here)
                for side in range(2):
                    if not masked:
                        add(side, pick(half == side, part, 0))
                    elif half == side:
                        add(side, part)
        for half in range(2):
            place = at_rows(works[0].query_slot(owner, half) * rows, rows)
            grads = (jnp.transpose(totals[half]) * SCALE).astype(target.dtype)
            for h in range(GROUP):
                target[place, h * HEAD : (h + 1) * HEAD] = grads[h * rows : (h + 1) * rows, :]


def sum_kernel(outer, *refs):
    terms, outs, total_ref = refs[:outer], refs[outer:-1], refs[-1]
    total = terms[0][...]
    for term_ref in terms[1:]:
        total = total + term_ref[...].astype(jnp.float32)
    total_ref[...] = total
    kvh = len(outs)
    rows = outs[0].shape[0]
    for e, out_ref in enumerate(outs):
        target = target_of(lax.axis_index("kvh"), e, kvh)
        out_ref[...] = total_ref[at_rows(target * rows, rows), :].astype(jnp.bfloat16)


def place_kernel(own_ref, received_ref, *refs):
    parts, (dq_out, key_out, value_out, dq_ref, sems) = refs[:-5], refs[-5:]
    kvh = len(parts)
    copies = []
    for e, part_ref in enumerate(parts):
        cols = at_rows(partner(lax.axis_index("kvh"), e, kvh) * HEAD, HEAD)
        copies.append(load(part_ref.at[:, pl.ds(0, HEAD)], key_out.at[:, cols], sems.at[2 * e]))
        copies.append(load(part_ref.at[:, pl.ds(HEAD, HEAD)], value_out.at[:, cols], sems.at[2 * e + 1]))
    dq_ref[...] = (own_ref[...] + received_ref[...].astype(jnp.float32)).astype(jnp.bfloat16)
    copies.append(load(dq_ref, dq_out, sems.at[2 * kvh]))
    wait_all(copies)


def per_device(queries, keys, values, d_out, slab_order):
    kvh = lax.axis_size("kvh")
    outer = lax.axis_size("outer")
    local_rows, query_width = queries.shape
    cache_rows = keys.shape[0]
    slab_rows = local_rows // 2
    columns = GROUP * slab_rows
    params = pltpu.CompilerParams(vmem_limit_bytes=(8 << 20) + (10 << 10) * outer * local_rows)
    beside = pl.CostEstimate(flops=2 * 10**10, bytes_accessed=10**6, transcendentals=0)
    vmem = pl.BlockSpec(memory_space=pltpu.VMEM)
    smem = pl.BlockSpec(memory_space=pltpu.SMEM)
    anywhere = pl.BlockSpec(memory_space=pl.ANY)
    shape = jax.ShapeDtypeStruct
    dma = pltpu.SemaphoreType.DMA
    low, full = jnp.bfloat16, jnp.float32

    def call(kernel, name, **arguments):
        return pl.pallas_call(kernel, compiler_params=params, name=name, **arguments)

    def shift(array, axis, by):
        size = lax.axis_size(axis)
        if by > 0:
            return lax.ppermute(array, axis, [(n, target_of(n, by, size)) for n in range(size)])
        return lax.ppermute(array, axis, [(n, partner(n, -by, size)) for n in range(size)])

    part = shape((cache_rows, 2 * HEAD), low)
    block = shape((local_rows, 2 * HEAD), low)
    parts = call(
        split_kernel,
        "split",
        out_shape=(part,) * kvh,
        in_specs=[vmem],
        out_specs=(vmem,) * kvh,
        scratch_shapes=[dma((2 * kvh,))],
    )(jnp.concatenate([keys, values], axis=0))
    own_qd = call(
        stack_kernel,
        "stack",
        out_shape=shape((2, 2, columns, HEAD), low),
        in_specs=[vmem, vmem, anywhere],
        out_specs=vmem,
        cost_estimate=beside,
    )(queries, d_out, parts[0])
    parts = [parts[0]] + [shift(parts[e], "kvh", e) for e in range(1, kvh)]
    other_qd = shift(own_qd, "pair", 1)
    own_block = call(
        join_kernel,
        "join",
        out_shape=block,
        in_specs=[anywhere] * kvh,
        out_specs=vmem,
        scratch_shapes=[dma((kvh,))],
        cost_estimate=beside,
    )(*parts)
    blocks = [own_block] + [shift(own_block, "outer", d) for d in range(1, outer)]

    far = outer // 2 + 1
    groups = [[0, *range(far, outer)], list(range(1, far))]
    all_stats = shape((12, columns), full)
    results = []
    for n, members in enumerate(groups):
        score_rows = shape((2, (2 * len(members) + 1) * slab_rows, columns), full)
        results.append(
            call(
                functools.partial(stats_kernel, outer, members),
                "stats",
                out_shape=(all_stats, score_rows, score_rows),
                in_specs=[smem] + [vmem] * (2 + len(members)) + [anywhere] * min(n, 1),
                out_specs=(vmem,) * 3,
                cost_estimate=beside if n + 1 < len(groups) else None,
            )(slab_order, own_qd, other_qd, *[blocks[d] for d in members], *[done[0] for done in results[-1:]])
        )
    stats, expon, grad_probs = zip(*results)
    mine = call(
        merge_kernel, "merge", out_shape=all_stats, in_specs=[vmem] * len(stats), out_specs=vmem
    )(*stats)
    theirs = shift(mine, "pair", 1)
    count = len(groups)
    grads = call(
        functools.partial(grads_kernel, outer, groups),
        "grads",
        out_shape=(shape(block.shape, full),)
        + (block,) * (outer - 1)
        + tuple(shape(scores.shape, low) for scores in expon),
        in_specs=[smem] + [vmem] * (3 + 3 * count),
        out_specs=(vmem,) * (outer + count),
    )(slab_order, own_qd, other_qd, *stats, theirs, *expon, *grad_probs)
    terms, score_grads = grads[:outer], grads[outer:]
    terms = [terms[0]] + [shift(terms[d], "outer", -d) for d in range(outer - 1, 0, -1)]
    own_grads, other_grads = call(
        functools.partial(query_kernel, outer, groups),
        "query_terms",
        out_shape=(shape(queries.shape, full), shape(queries.shape, low)),
        in_specs=[smem] + [vmem] * (outer + count),
        out_specs=(vmem, vmem),
        cost_estimate=beside,
    )(slab_order, *blocks, *score_grads)
    received_grads = shift(other_grads, "pair", 1)
    owned = call(
        functools.partial(sum_kernel, outer),
        "sum",
        out_shape=(part,) * kvh,
        in_specs=[vmem] * outer,
        out_specs=(vmem,) * kvh,
        scratch_shapes=[pltpu.VMEM(block.shape, full)],
        cost_estimate=beside,
    )(*terms)
    owned = [owned[0]] + [shift(owned[e], "kvh", e) for e in range(1, kvh)]
    return call(
        place_kernel,
        "place",
        out_shape=(shape(queries.shape, low), shape(keys.shape, low), shape(values.shape, low)),
        in_specs=[vmem, vmem] + [anywhere] * kvh,
        out_specs=(anywhere,) * 3,
        scratch_shapes=[pltpu.VMEM(queries.shape, low), dma((2 * kvh + 1,))],
    )(own_grads, received_grads, *owned)


def solution(mesh):
    kvh = mesh.shape["kvh"]
    pairs = mesh.shape["seq"] // 2
    paired = Mesh(mesh.devices.reshape(pairs, 2, kvh), ("outer", "pair", "kvh"))
    seq = ("outer", "pair")
    cache = P(("outer", "pair", "kvh"), None)
    placed = (P(seq, "kvh"), cache, cache, P(seq, "kvh"), P())
    return jax.shard_map(
        per_device,
        mesh=paired,
        in_specs=placed,
        out_specs=(P(seq, "kvh"), cache, cache),
        check_vma=False,
    )
```

```python
import functools
import math

import jax
import jax.numpy as jnp
from jax import lax
from jax.experimental import pallas as pl
from jax.experimental.pallas import tpu as pltpu
from jax.sharding import Mesh
from jax.sharding import PartitionSpec as P

HEADS = 20
KV_HEADS = 4
HEAD = 128
GROUP = HEADS // KV_HEADS
SCALE = HEAD ** (-0.5)
EXPONENT_SCALE = SCALE * math.log2(math.e)
LOWEST = -1e30
ROWS_DOT_ROWS = (((1,), (1,)), ((), ()))
COLS_DOT_COLS = (((0,), (0,)), ((), ()))


def at_rows(start, size):
    return pl.ds(pl.multiple_of(start, size), size)


def load(source_ref, target_ref, sem):
    copy = pltpu.make_async_copy(source_ref, target_ref, sem)
    copy.start()
    return copy


def wait_all(copies):
    for copy in copies:
        copy.wait()


def partner(index, distance, size):
    if size & (size - 1) == 0:
        return index ^ distance
    return (index + size - distance) % size


def target_of(index, distance, size):
    if size & (size - 1) == 0:
        return index ^ distance
    return (index + distance) % size


def pick(condition, chosen, other):
    return lax.select(condition, chosen, jnp.full_like(chosen, other))


class Work:
    def __init__(self, table_ref, rows, members, block_refs):
        self.rows, self.members, self.block_refs = rows, members, block_refs
        self.low_rows = len(members) * rows

        def pair(at):
            return jnp.max(table_ref[2 * at : 2 * at + 1, :]), jnp.max(table_ref[2 * at + 1 : 2 * at + 2, :])

        self.pairs = [pair(d) for d in members]
        self.owners = [pair(table_ref.shape[0] // 2 - 2), pair(table_ref.shape[0] // 2 - 1)]

    @staticmethod
    def slot(place, half):
        return jnp.where(half == 0, place, 1 - place)

    def query_slot(self, owner, half):
        return self.slot(self.owners[owner][1], half)

    def key_rows(self, n, half):
        return at_rows(self.slot(self.pairs[n][1], half) * self.rows, self.rows)

    def keys(self, n, half, cols):
        return self.block_refs[n][self.key_rows(n, half), cols]

    def low_keys(self, cols):
        return jnp.concatenate([self.keys(n, 0, cols) for n in range(len(self.members))], axis=0)

    def tiles(self, owner):
        found = []
        for n, d in enumerate(self.members):
            here = pl.ds(self.low_rows + n * self.rows, self.rows)
            if owner == 0 and d == 0:
                found.append((n, 0, here, True))
                found.append((n, 1, pl.ds(2 * self.low_rows, self.rows), True))
            else:
                half = jnp.where(self.owners[owner][0] >= self.pairs[n][0], 0, 1)
                found.append((n, half, here, False))
        return found


def split_kernel(cache_ref, *refs):
    parts, sems = refs[:-1], refs[-1]
    kvh = len(parts)
    rows = parts[0].shape[0]
    copies = []
    for e, part_ref in enumerate(parts):
        cols = at_rows(target_of(lax.axis_index("kvh"), e, kvh) * HEAD, HEAD)
        for n in range(2):
            source = cache_ref.at[pl.ds(n * rows, rows), cols]
            copies.append(load(source, part_ref.at[:, pl.ds(n * HEAD, HEAD)], sems.at[2 * e + n]))
    wait_all(copies)


def table_kernel(outer, order_ref, after_ref, table_ref):
    at, side = lax.axis_index("outer"), lax.axis_index("pair")
    indices = [2 * partner(at, d, outer) + side for d in range(outer)]
    indices += [2 * at + side, 2 * at + 1 - side]
    for n, index in enumerate(indices):
        first, second = order_ref[2 * index], order_ref[2 * index + 1]
        row = table_ref.shape[1:]
        table_ref[2 * n : 2 * n + 1, :] = jnp.full((1, *row), jnp.minimum(first, second), jnp.int32)
        table_ref[2 * n + 1 : 2 * n + 2, :] = jnp.full((1, *row), jnp.where(first < second, 0, 1), jnp.int32)


def stack_kernel(*refs):
    sources, outs = refs[:4], refs[4:]
    rows = sources[0].shape[0] // 2
    for n, source_ref in enumerate(sources):
        for slot in range(2):
            for h in range(GROUP):
                outs[n // 2][n % 2, slot, h * rows : (h + 1) * rows, :] = source_ref[
                    slot * rows : (slot + 1) * rows, h * HEAD : (h + 1) * HEAD
                ]


def join_kernel(after_ref, *refs):
    parts, (out_ref, sems) = refs[:-2], refs[-2:]
    kvh = len(parts)
    rows = parts[0].shape[0]
    copies = []
    for e, part_ref in enumerate(parts):
        source = partner(lax.axis_index("kvh"), e, kvh)
        copies.append(load(part_ref, out_ref.at[at_rows(source * rows, rows)], sems.at[e]))
    wait_all(copies)


def stats_kernel(members, table_ref, own_ref, other_ref, *refs):
    block_refs, (out_ref, e_ref, dp_ref) = refs[: len(members)], refs[-3:]
    rows = block_refs[0].shape[0] // 2
    work = Work(table_ref, rows, members, block_refs)
    low_part = pl.ds(0, work.low_rows)
    key_cols, value_cols = slice(0, HEAD), slice(HEAD, 2 * HEAD)

    def products(keys, queries):
        return lax.dot_general(keys, queries, ROWS_DOT_ROWS, preferred_element_type=jnp.float32)

    tops = []
    for owner, qd_ref in enumerate((own_ref, other_ref)):
        high = work.query_slot(owner, 1)
        scores = products(work.low_keys(key_cols), qd_ref[0, high])
        e_ref[owner, low_part, :] = scores
        dp_ref[owner, low_part, :] = products(work.low_keys(value_cols), qd_ref[1, high])
        top = [jnp.full((1, scores.shape[1]), LOWEST, jnp.float32), jnp.max(scores, axis=0, keepdims=True)]
        for n, half, here, masked in work.tiles(owner):
            slot = work.query_slot(owner, half)
            scores = products(work.keys(n, half, key_cols), qd_ref[0, slot])
            if masked:
                key = lax.broadcasted_iota(jnp.int32, scores.shape, 0)
                query = lax.rem(lax.broadcasted_iota(jnp.int32, (1, scores.shape[1]), 1), rows)
                scores = jnp.where(key <= query, scores, LOWEST)
            e_ref[owner, here, :] = scores
            dp_ref[owner, here, :] = products(work.keys(n, half, value_cols), qd_ref[1, slot])
            most = jnp.max(scores, axis=0, keepdims=True)
            for side in range(2):
                seen = most if masked else pick(half == side, most, LOWEST)
                if not masked or half == side:
                    top[side] = jnp.maximum(top[side], seen)
        tops.append(top)

    for owner, top in enumerate(tops):

        def sums(here, most):
            expon = jnp.exp2((e_ref[owner, here, :] - most) * EXPONENT_SCALE)
            e_ref[owner, here, :] = expon
            return [
                jnp.sum(expon, axis=0, keepdims=True),
                jnp.sum(expon * dp_ref[owner, here, :], axis=0, keepdims=True),
            ]

        zero = jnp.zeros_like(top[0])
        totals = [[zero, zero], sums(low_part, top[1])]
        for n, half, here, masked in work.tiles(owner):
            part = sums(here, top[half] if masked else lax.select(half == 0, top[0], top[1]))
            for side in range(2):
                if not masked or half == side:
                    seen = part if masked else [pick(half == side, one, 0) for one in part]
                    totals[side] = [total + one for total, one in zip(totals[side], seen)]
        for half in range(2):
            base = (2 * owner + half) * 3
            for n, row in enumerate((top[half], *totals[half])):
                out_ref[base + n : base + n + 1, :] = row


def merged(stats_refs, base):
    rows = [ref[base : base + 3, :] for ref in stats_refs]
    top = functools.reduce(jnp.maximum, [part[:1] for part in rows])
    weights = [jnp.exp2((part[:1] - top) * EXPONENT_SCALE) for part in rows]
    total = sum(weight * part[1:2] for weight, part in zip(weights, rows))
    delta = sum(weight * part[2:3] for weight, part in zip(weights, rows))
    return top, total, delta


def merge_kernel(*refs):
    stats_refs, out_ref = refs[:-1], refs[-1]
    for base in range(0, 12, 3):
        for n, row in enumerate(merged(stats_refs, base)):
            out_ref[base + n : base + n + 1, :] = row


def grads_kernel(outer, groups, table_ref, own_ref, other_ref, *refs):
    count = len(groups)
    stats_refs, theirs_ref, refs = refs[:count], refs[count], refs[count + 1 :]
    e_refs, dp_refs, refs = refs[:count], refs[count : 2 * count], refs[2 * count :]
    term_refs, gs_refs = refs[:outer], refs[outer:]
    rows = term_refs[0].shape[0] // 2
    weights, deltas = [[] for _ in groups], []
    for owner in range(2):
        delta = []
        group_weights = [[] for _ in groups]
        for half in range(2):
            base = (2 * owner + half) * 3
            base2 = (2 * (1 - owner) + half) * 3
            mine = merged(stats_refs, base)
            theirs = [theirs_ref[base2 + n : base2 + n + 1, :] for n in range(3)]
            top = jnp.maximum(mine[0], theirs[0])
            w1 = jnp.exp2((mine[0] - top) * EXPONENT_SCALE)
            w2 = jnp.exp2((theirs[0] - top) * EXPONENT_SCALE)
            total = w1 * mine[1] + w2 * theirs[1]
            delta.append((w1 * mine[2] + w2 * theirs[2]) / total)
            for n, stats_ref in enumerate(stats_refs):
                weight = jnp.exp2((stats_ref[base : base + 1, :] - top) * EXPONENT_SCALE)
                group_weights[n].append(weight / total)
        deltas.append(delta)
        for n in range(count):
            weights[n].append(group_weights[n])

    for n, members in enumerate(groups):
        work = Work(table_ref, rows, members, None)
        terms = [[None] * len(members), [None] * len(members)]

        def add(half, at, pair):
            old = terms[half][at]
            terms[half][at] = pair if old is None else [one + more for one, more in zip(old, pair)]

        for owner, qd_ref in enumerate((own_ref, other_ref)):

            def gradients(here, slot, weight, delta):
                probs = e_refs[n][owner, here, :] * weight
                grads = (probs * (dp_refs[n][owner, here, :] - delta)).astype(jnp.bfloat16)
                gs_refs[n][owner, here, :] = grads
                return [
                    jnp.dot(grads, qd_ref[0, slot], preferred_element_type=jnp.float32),
                    jnp.dot(probs.astype(jnp.bfloat16), qd_ref[1, slot], preferred_element_type=jnp.float32),
                ]

            weight, delta = weights[n][owner], deltas[owner]
            low_part = pl.ds(0, work.low_rows)
            part = gradients(low_part, work.query_slot(owner, 1), weight[1], delta[1])
            for at in range(len(members)):
                add(0, at, [one[at * rows : (at + 1) * rows] for one in part])
            for at, half, here, masked in work.tiles(owner):
                slot = work.query_slot(owner, half)
                if masked:
                    add(half, at, gradients(here, slot, weight[half], delta[half]))
                else:
                    is_low = half == 0
                    part = gradients(here, slot, lax.select(is_low, *weight), lax.select(is_low, *delta))
                    for side in range(2):
                        add(side, at, [pick(half == side, one, 0) for one in part])
        for at, d in enumerate(members):
            term_ref = term_refs[d]
            for half in range(2):
                target = work.key_rows(at, half)
                of_keys, of_values = terms[half][at]
                term_ref[target, :HEAD] = (of_keys * SCALE).astype(term_ref.dtype)
                term_ref[target, HEAD:] = of_values.astype(term_ref.dtype)


def query_kernel(outer, groups, table_ref, *refs):
    count = len(groups)
    block_refs, gs_refs, (own_ref, other_ref) = refs[:outer], refs[outer : outer + count], refs[outer + count :]
    rows = own_ref.shape[0] // 2
    works = [Work(table_ref, rows, members, [block_refs[d] for d in members]) for members in groups]
    cols = slice(0, HEAD)
    for owner, target in ((0, own_ref), (1, other_ref)):
        totals = [None, None]

        def add(half, part):
            totals[half] = part if totals[half] is None else totals[half] + part

        for gs_ref, work in zip(gs_refs, works):

            def terms(keys, here):
                return lax.dot_general(
                    keys, gs_ref[owner, here, :], COLS_DOT_COLS, preferred_element_type=jnp.float32
                )

            add(1, terms(work.low_keys(cols), pl.ds(0, work.low_rows)))
            for n, half, here, masked in work.tiles(owner):
                part = terms(work.keys(n, half, cols), here)
                for side in range(2):
                    if not masked:
                        add(side, pick(half == side, part, 0))
                    elif half == side:
                        add(side, part)
        for half in range(2):
            place = at_rows(works[0].query_slot(owner, half) * rows, rows)
            grads = (jnp.transpose(totals[half]) * SCALE).astype(target.dtype)
            for h in range(GROUP):
                target[place, h * HEAD : (h + 1) * HEAD] = grads[h * rows : (h + 1) * rows, :]


def sum_kernel(outer, *refs):
    terms, outs, total_ref = refs[:outer], refs[outer:-1], refs[-1]
    total = terms[0][...]
    for term_ref in terms[1:]:
        total = total + term_ref[...].astype(jnp.float32)
    total_ref[...] = total
    kvh = len(outs)
    rows = outs[0].shape[0]
    for e, out_ref in enumerate(outs):
        target = target_of(lax.axis_index("kvh"), e, kvh)
        out_ref[...] = total_ref[at_rows(target * rows, rows), :].astype(jnp.bfloat16)


def place_kernel(own_ref, received_ref, *refs):
    parts, (dq_out, key_out, value_out, dq_ref, sems) = refs[:-5], refs[-5:]
    kvh = len(parts)
    copies = []
    for e, part_ref in enumerate(parts):
        cols = at_rows(partner(lax.axis_index("kvh"), e, kvh) * HEAD, HEAD)
        copies.append(load(part_ref.at[:, pl.ds(0, HEAD)], key_out.at[:, cols], sems.at[2 * e]))
        copies.append(load(part_ref.at[:, pl.ds(HEAD, HEAD)], value_out.at[:, cols], sems.at[2 * e + 1]))
    dq_ref[...] = (own_ref[...] + received_ref[...].astype(jnp.float32)).astype(jnp.bfloat16)
    copies.append(load(dq_ref, dq_out, sems.at[2 * kvh]))
    wait_all(copies)


def per_device(queries, keys, values, d_out, slab_order):
    kvh = lax.axis_size("kvh")
    outer = lax.axis_size("outer")
    local_rows, query_width = queries.shape
    cache_rows = keys.shape[0]
    slab_rows = local_rows // 2
    columns = GROUP * slab_rows
    params = pltpu.CompilerParams(vmem_limit_bytes=(8 << 20) + (10 << 10) * outer * local_rows)
    beside = pl.CostEstimate(flops=2 * 10**10, bytes_accessed=10**6, transcendentals=0)
    vmem = pl.BlockSpec(memory_space=pltpu.VMEM)
    smem = pl.BlockSpec(memory_space=pltpu.SMEM)
    anywhere = pl.BlockSpec(memory_space=pl.ANY)
    shape = jax.ShapeDtypeStruct
    dma = pltpu.SemaphoreType.DMA
    low, full = jnp.bfloat16, jnp.float32

    def call(kernel, name, **arguments):
        return pl.pallas_call(kernel, compiler_params=params, name=name, **arguments)

    def shift(array, axis, by):
        size = lax.axis_size(axis)
        if by > 0:
            return lax.ppermute(array, axis, [(n, target_of(n, by, size)) for n in range(size)])
        return lax.ppermute(array, axis, [(n, partner(n, -by, size)) for n in range(size)])

    part = shape((cache_rows, 2 * HEAD), low)
    block = shape((local_rows, 2 * HEAD), low)
    parts = call(
        split_kernel,
        "split",
        out_shape=(part,) * kvh,
        in_specs=[vmem],
        out_specs=(vmem,) * kvh,
        scratch_shapes=[dma((2 * kvh,))],
    )(jnp.concatenate([keys, values], axis=0))
    table = call(
        functools.partial(table_kernel, outer),
        "table",
        out_shape=shape((2 * outer + 4, HEAD), jnp.int32),
        in_specs=[smem, anywhere],
        out_specs=vmem,
        cost_estimate=beside,
    )(slab_order, parts[0])
    parts = [parts[0]] + [shift(parts[e], "kvh", e) for e in range(1, kvh)]
    stack = shape((2, 2, columns, HEAD), low)
    own_qd, other_qd = call(
        stack_kernel,
        "stack",
        out_shape=(stack, stack),
        in_specs=[vmem] * 4,
        out_specs=(vmem, vmem),
    )(queries, d_out, shift(queries, "pair", 1), shift(d_out, "pair", 1))
    own_block = call(
        join_kernel,
        "join",
        out_shape=block,
        in_specs=[anywhere] * (1 + kvh),
        out_specs=vmem,
        scratch_shapes=[dma((kvh,))],
        cost_estimate=beside,
    )(table, *parts)
    blocks = [own_block] + [shift(own_block, "outer", d) for d in range(1, outer)]

    far = outer // 2 + 1
    groups = [[0, *range(far, outer)], list(range(1, far))]
    all_stats = shape((12, columns), full)
    results = []
    for n, members in enumerate(groups):
        score_rows = shape((2, (2 * len(members) + 1) * slab_rows, columns), full)
        results.append(
            call(
                functools.partial(stats_kernel, members),
                "stats",
                out_shape=(all_stats, score_rows, score_rows),
                in_specs=[vmem] * (3 + len(members)) + [anywhere] * min(n, 1),
                out_specs=(vmem,) * 3,
                cost_estimate=beside if n + 1 < len(groups) else None,
            )(table, own_qd, other_qd, *[blocks[d] for d in members], *[done[0] for done in results[-1:]])
        )
    stats, expon, grad_probs = zip(*results)
    mine = call(
        merge_kernel, "merge", out_shape=all_stats, in_specs=[vmem] * len(stats), out_specs=vmem
    )(*stats)
    theirs = shift(mine, "pair", 1)
    count = len(groups)
    grads = call(
        functools.partial(grads_kernel, outer, groups),
        "grads",
        out_shape=(shape(block.shape, full),)
        + (block,) * (outer - 1)
        + tuple(shape(scores.shape, low) for scores in expon),
        in_specs=[vmem] * (4 + 3 * count),
        out_specs=(vmem,) * (outer + count),
    )(table, own_qd, other_qd, *stats, theirs, *expon, *grad_probs)
    terms, score_grads = grads[:outer], grads[outer:]
    terms = [terms[0]] + [shift(terms[d], "outer", -d) for d in range(outer - 1, 0, -1)]
    own_grads, other_grads = call(
        functools.partial(query_kernel, outer, groups),
        "query_terms",
        out_shape=(shape(queries.shape, full), shape(queries.shape, low)),
        in_specs=[vmem] * (1 + outer + count),
        out_specs=(vmem, vmem),
        cost_estimate=beside,
    )(table, *blocks, *score_grads)
    received_grads = shift(other_grads, "pair", 1)
    owned = call(
        functools.partial(sum_kernel, outer),
        "sum",
        out_shape=(part,) * kvh,
        in_specs=[vmem] * outer,
        out_specs=(vmem,) * kvh,
        scratch_shapes=[pltpu.VMEM(block.shape, full)],
        cost_estimate=beside,
    )(*terms)
    owned = [owned[0]] + [shift(owned[e], "kvh", e) for e in range(1, kvh)]
    return call(
        place_kernel,
        "place",
        out_shape=(shape(queries.shape, low), shape(keys.shape, low), shape(values.shape, low)),
        in_specs=[vmem, vmem] + [anywhere] * kvh,
        out_specs=(anywhere,) * 3,
        scratch_shapes=[pltpu.VMEM(queries.shape, low), dma((2 * kvh + 1,))],
    )(own_grads, received_grads, *owned)


def solution(mesh):
    kvh = mesh.shape["kvh"]
    pairs = mesh.shape["seq"] // 2
    paired = Mesh(mesh.devices.reshape(pairs, 2, kvh), ("outer", "pair", "kvh"))
    seq = ("outer", "pair")
    cache = P(("outer", "pair", "kvh"), None)
    placed = (P(seq, "kvh"), cache, cache, P(seq, "kvh"), P())
    return jax.shard_map(
        per_device,
        mesh=paired,
        in_specs=placed,
        out_specs=(P(seq, "kvh"), cache, cache),
        check_vma=False,
    )
```

```python
import functools
import math

import jax
import jax.numpy as jnp
from jax import lax
from jax.experimental import pallas as pl
from jax.experimental.pallas import tpu as pltpu
from jax.sharding import Mesh
from jax.sharding import PartitionSpec as P

HEADS = 20
KV_HEADS = 4
HEAD = 128
GROUP = HEADS // KV_HEADS
SCALE = HEAD ** (-0.5)
EXPONENT_SCALE = SCALE * math.log2(math.e)
LOWEST = -1e30
ROWS_DOT_ROWS = (((1,), (1,)), ((), ()))
COLS_DOT_COLS = (((0,), (0,)), ((), ()))


def at_rows(start, size):
    return pl.ds(pl.multiple_of(start, size), size)


def load(source_ref, target_ref, sem):
    copy = pltpu.make_async_copy(source_ref, target_ref, sem)
    copy.start()
    return copy


def wait_all(copies):
    for copy in copies:
        copy.wait()


def partner(index, distance, size):
    if size & (size - 1) == 0:
        return index ^ distance
    return (index + size - distance) % size


def target_of(index, distance, size):
    if size & (size - 1) == 0:
        return index ^ distance
    return (index + distance) % size


def pick(condition, chosen, other):
    return lax.select(condition, chosen, jnp.full_like(chosen, other))


class Work:
    def __init__(self, table_ref, rows, members, block_refs):
        self.rows, self.members, self.block_refs = rows, members, block_refs
        self.low_rows = len(members) * rows

        def pair(at):
            return jnp.max(table_ref[2 * at : 2 * at + 1, :]), jnp.max(table_ref[2 * at + 1 : 2 * at + 2, :])

        self.pairs = [pair(d) for d in members]
        self.owners = [pair(table_ref.shape[0] // 2 - 2), pair(table_ref.shape[0] // 2 - 1)]

    @staticmethod
    def slot(place, half):
        return jnp.where(half == 0, place, 1 - place)

    def query_slot(self, owner, half):
        return self.slot(self.owners[owner][1], half)

    def key_rows(self, n, half):
        return at_rows(self.slot(self.pairs[n][1], half) * self.rows, self.rows)

    def keys(self, n, half, cols):
        return self.block_refs[n][self.key_rows(n, half), cols]

    def low_keys(self, cols):
        return jnp.concatenate([self.keys(n, 0, cols) for n in range(len(self.members))], axis=0)

    def tiles(self, owner):
        found = []
        for n, d in enumerate(self.members):
            here = pl.ds(self.low_rows + n * self.rows, self.rows)
            if owner == 0 and d == 0:
                found.append((n, 0, here, True))
                found.append((n, 1, pl.ds(2 * self.low_rows, self.rows), True))
            else:
                half = jnp.where(self.owners[owner][0] >= self.pairs[n][0], 0, 1)
                found.append((n, half, here, False))
        return found


def split_kernel(cache_ref, *refs):
    parts, sems = refs[:-1], refs[-1]
    kvh = len(parts)
    rows = parts[0].shape[0]
    copies = []
    for e, part_ref in enumerate(parts):
        cols = at_rows(target_of(lax.axis_index("kvh"), e, kvh) * HEAD, HEAD)
        for n in range(2):
            source = cache_ref.at[pl.ds(n * rows, rows), cols]
            copies.append(load(source, part_ref.at[:, pl.ds(n * HEAD, HEAD)], sems.at[2 * e + n]))
    wait_all(copies)


def table_kernel(outer, order_ref, after_ref, table_ref):
    at, side = lax.axis_index("outer"), lax.axis_index("pair")
    indices = [2 * partner(at, d, outer) + side for d in range(outer)]
    indices += [2 * at + side, 2 * at + 1 - side]
    for n, index in enumerate(indices):
        first, second = order_ref[2 * index], order_ref[2 * index + 1]
        row = table_ref.shape[1:]
        table_ref[2 * n : 2 * n + 1, :] = jnp.full((1, *row), jnp.minimum(first, second), jnp.int32)
        table_ref[2 * n + 1 : 2 * n + 2, :] = jnp.full((1, *row), jnp.where(first < second, 0, 1), jnp.int32)


def stack_kernel(*refs):
    sources, outs = refs[:4], refs[4:]
    rows = sources[0].shape[0] // 2
    for n, source_ref in enumerate(sources):
        for slot in range(2):
            for h in range(GROUP):
                outs[n // 2][n % 2, slot, h * rows : (h + 1) * rows, :] = source_ref[
                    slot * rows : (slot + 1) * rows, h * HEAD : (h + 1) * HEAD
                ]


def join_kernel(*refs):
    parts, (out_ref, sems) = refs[:-2], refs[-2:]
    kvh = len(parts)
    rows = parts[0].shape[0]
    copies = []
    for e, part_ref in enumerate(parts):
        source = partner(lax.axis_index("kvh"), e, kvh)
        copies.append(load(part_ref, out_ref.at[at_rows(source * rows, rows)], sems.at[e]))
    wait_all(copies)


def stats_kernel(members, table_ref, own_ref, other_ref, *refs):
    block_refs, (out_ref, e_ref, dp_ref) = refs[: len(members)], refs[-3:]
    rows = block_refs[0].shape[0] // 2
    work = Work(table_ref, rows, members, block_refs)
    low_part = pl.ds(0, work.low_rows)
    key_cols, value_cols = slice(0, HEAD), slice(HEAD, 2 * HEAD)

    def products(keys, queries):
        return lax.dot_general(keys, queries, ROWS_DOT_ROWS, preferred_element_type=jnp.float32)

    tops = []
    for owner, qd_ref in enumerate((own_ref, other_ref)):
        tiles = work.tiles(owner)
        seen_by_low = [tile for tile in tiles if not (tile[3] and tile[1] == 1)]
        seen_by_high = [tile for tile in tiles if not (tile[3] and tile[1] == 0)]

        def both(kind, cols):
            low_keys, high_keys = [
                [work.keys(n, half, cols) for n, half, _, _ in found] for found in (seen_by_low, seen_by_high)
            ]
            low = products(jnp.concatenate(low_keys, axis=0), qd_ref[kind, work.query_slot(owner, 0)])
            high = products(
                jnp.concatenate([work.low_keys(cols), *high_keys], axis=0),
                qd_ref[kind, work.query_slot(owner, 1)],
            )
            found = {}
            for at, tile in enumerate(seen_by_low):
                found[tile[2].start] = low[at * rows : (at + 1) * rows]
            for at, (n, half, here, masked) in enumerate(seen_by_high):
                mine = high[work.low_rows + at * rows : work.low_rows + (at + 1) * rows]
                found[here.start] = mine if masked else lax.select(half == 0, found[here.start], mine)
            return high[: work.low_rows], found

        scores, tile_scores = both(0, key_cols)
        e_ref[owner, low_part, :] = scores
        low_grads, tile_grads = both(1, value_cols)
        dp_ref[owner, low_part, :] = low_grads
        top = [jnp.full((1, scores.shape[1]), LOWEST, jnp.float32), jnp.max(scores, axis=0, keepdims=True)]
        for n, half, here, masked in tiles:
            scores = tile_scores[here.start]
            if masked:
                key = lax.broadcasted_iota(jnp.int32, scores.shape, 0)
                query = lax.rem(lax.broadcasted_iota(jnp.int32, (1, scores.shape[1]), 1), rows)
                scores = jnp.where(key <= query, scores, LOWEST)
            e_ref[owner, here, :] = scores
            dp_ref[owner, here, :] = tile_grads[here.start]
            most = jnp.max(scores, axis=0, keepdims=True)
            for side in range(2):
                seen = most if masked else pick(half == side, most, LOWEST)
                if not masked or half == side:
                    top[side] = jnp.maximum(top[side], seen)
        tops.append(top)

    for owner, top in enumerate(tops):

        def sums(here, most):
            expon = jnp.exp2((e_ref[owner, here, :] - most) * EXPONENT_SCALE)
            e_ref[owner, here, :] = expon
            return [
                jnp.sum(expon, axis=0, keepdims=True),
                jnp.sum(expon * dp_ref[owner, here, :], axis=0, keepdims=True),
            ]

        zero = jnp.zeros_like(top[0])
        totals = [[zero, zero], sums(low_part, top[1])]
        for n, half, here, masked in work.tiles(owner):
            part = sums(here, top[half] if masked else lax.select(half == 0, top[0], top[1]))
            for side in range(2):
                if not masked or half == side:
                    seen = part if masked else [pick(half == side, one, 0) for one in part]
                    totals[side] = [total + one for total, one in zip(totals[side], seen)]
        for half in range(2):
            base = (2 * owner + half) * 3
            for n, row in enumerate((top[half], *totals[half])):
                out_ref[base + n : base + n + 1, :] = row


def merged(stats_refs, base):
    rows = [ref[base : base + 3, :] for ref in stats_refs]
    top = functools.reduce(jnp.maximum, [part[:1] for part in rows])
    weights = [jnp.exp2((part[:1] - top) * EXPONENT_SCALE) for part in rows]
    total = sum(weight * part[1:2] for weight, part in zip(weights, rows))
    delta = sum(weight * part[2:3] for weight, part in zip(weights, rows))
    return top, total, delta


def merge_kernel(*refs):
    stats_refs, out_ref = refs[:-1], refs[-1]
    for base in range(0, 12, 3):
        for n, row in enumerate(merged(stats_refs, base)):
            out_ref[base + n : base + n + 1, :] = row


def grads_kernel(outer, groups, table_ref, own_ref, other_ref, *refs):
    count = len(groups)
    stats_refs, theirs_ref, refs = refs[:count], refs[count], refs[count + 1 :]
    e_refs, dp_refs, refs = refs[:count], refs[count : 2 * count], refs[2 * count :]
    term_refs, (high_ref, low_ref, p_high_ref, p_low_ref) = refs[:outer], refs[outer:]
    rows = term_refs[0].shape[0] // 2
    weights, deltas = [[] for _ in groups], []
    for owner in range(2):
        delta = []
        group_weights = [[] for _ in groups]
        for half in range(2):
            base = (2 * owner + half) * 3
            base2 = (2 * (1 - owner) + half) * 3
            mine = merged(stats_refs, base)
            theirs = [theirs_ref[base2 + n : base2 + n + 1, :] for n in range(3)]
            top = jnp.maximum(mine[0], theirs[0])
            w1 = jnp.exp2((mine[0] - top) * EXPONENT_SCALE)
            w2 = jnp.exp2((theirs[0] - top) * EXPONENT_SCALE)
            total = w1 * mine[1] + w2 * theirs[1]
            delta.append((w1 * mine[2] + w2 * theirs[2]) / total)
            for n, stats_ref in enumerate(stats_refs):
                weight = jnp.exp2((stats_ref[base : base + 1, :] - top) * EXPONENT_SCALE)
                group_weights[n].append(weight / total)
        deltas.append(delta)
        for n in range(count):
            weights[n].append(group_weights[n])

    works = [Work(table_ref, rows, members, None) for members in groups]
    all_rows = outer * rows
    totals = None
    for owner, qd_ref in enumerate((own_ref, other_ref)):
        delta = deltas[owner]
        base = 0
        for n, work in enumerate(works):

            def gradients(here, weight, half, targets, target):
                probs = e_refs[n][owner, here, :] * weight
                grads = probs * (dp_refs[n][owner, here, :] - delta[half])
                targets[0][owner, target, :] = grads.astype(jnp.bfloat16)
                targets[1][owner, target, :] = probs.astype(jnp.bfloat16)

            weight = weights[n][owner]
            high_targets, low_targets = (high_ref, p_high_ref), (low_ref, p_low_ref)
            low_part = pl.ds(0, work.low_rows)
            gradients(low_part, weight[1], 1, high_targets, pl.ds(base, work.low_rows))
            for at, half, here, masked in work.tiles(owner):
                first = base + at * rows
                if not masked or half == 0:
                    seen = weight[0] if masked else pick(half == 0, weight[0], 0)
                    gradients(here, seen, 0, low_targets, pl.ds(first, rows))
                if not masked or half == 1:
                    seen = weight[1] if masked else pick(half == 1, weight[1], 0)
                    gradients(here, seen, 1, high_targets, pl.ds(all_rows + first, rows))
            base += work.low_rows
        slots = [works[0].query_slot(owner, half) for half in range(2)]
        part = [
            jnp.dot(target[owner], qd_ref[kind, slots[half]], preferred_element_type=jnp.float32)
            for half, targets in enumerate(((low_ref, p_low_ref), (high_ref, p_high_ref)))
            for kind, target in enumerate(targets)
        ]
        totals = part if totals is None else [one + more for one, more in zip(totals, part)]
    low_keys, low_values, high_keys, high_values = totals
    base = 0
    for work in works:
        for at, d in enumerate(work.members):
            here, above = slice(base, base + rows), slice(all_rows + base, all_rows + base + rows)
            term_ref = term_refs[d]
            for half, of_keys, of_values in (
                (0, low_keys[here] + high_keys[here], low_values[here] + high_values[here]),
                (1, high_keys[above], high_values[above]),
            ):
                target = work.key_rows(at, half)
                term_ref[target, :HEAD] = (of_keys * SCALE).astype(term_ref.dtype)
                term_ref[target, HEAD:] = of_values.astype(term_ref.dtype)
            base += rows


def query_kernel(outer, groups, table_ref, *refs):
    block_refs, (high_ref, low_ref, own_ref, other_ref) = refs[:outer], refs[outer:]
    rows = own_ref.shape[0] // 2
    members = sum(groups, [])
    work = Work(table_ref, rows, members, [block_refs[d] for d in members])
    low_keys, high_keys = [
        jnp.concatenate([work.keys(n, half, slice(0, HEAD)) for n in range(outer)], axis=0) for half in range(2)
    ]
    all_keys = jnp.concatenate([low_keys, high_keys], axis=0)
    for owner, target in ((0, own_ref), (1, other_ref)):
        for half, keys, grads_ref in ((0, low_keys, low_ref), (1, all_keys, high_ref)):
            total = lax.dot_general(
                keys, grads_ref[owner], COLS_DOT_COLS, preferred_element_type=jnp.float32
            )
            place = at_rows(work.query_slot(owner, half) * rows, rows)
            grads = (jnp.transpose(total) * SCALE).astype(target.dtype)
            for h in range(GROUP):
                target[place, h * HEAD : (h + 1) * HEAD] = grads[h * rows : (h + 1) * rows, :]


def sum_kernel(outer, *refs):
    terms, outs, total_ref = refs[:outer], refs[outer:-1], refs[-1]
    total = terms[0][...]
    for term_ref in terms[1:]:
        total = total + term_ref[...].astype(jnp.float32)
    total_ref[...] = total
    kvh = len(outs)
    rows = outs[0].shape[0]
    for e, out_ref in enumerate(outs):
        target = target_of(lax.axis_index("kvh"), e, kvh)
        out_ref[...] = total_ref[at_rows(target * rows, rows), :].astype(jnp.bfloat16)


def place_kernel(own_ref, received_ref, *refs):
    parts, (dq_out, key_out, value_out, dq_ref, sems) = refs[:-5], refs[-5:]
    kvh = len(parts)
    copies = []
    for e, part_ref in enumerate(parts):
        cols = at_rows(partner(lax.axis_index("kvh"), e, kvh) * HEAD, HEAD)
        copies.append(load(part_ref.at[:, pl.ds(0, HEAD)], key_out.at[:, cols], sems.at[2 * e]))
        copies.append(load(part_ref.at[:, pl.ds(HEAD, HEAD)], value_out.at[:, cols], sems.at[2 * e + 1]))
    dq_ref[...] = (own_ref[...] + received_ref[...].astype(jnp.float32)).astype(jnp.bfloat16)
    copies.append(load(dq_ref, dq_out, sems.at[2 * kvh]))
    wait_all(copies)


def per_device(queries, keys, values, d_out, slab_order):
    kvh = lax.axis_size("kvh")
    outer = lax.axis_size("outer")
    local_rows, query_width = queries.shape
    cache_rows = keys.shape[0]
    slab_rows = local_rows // 2
    columns = GROUP * slab_rows
    params = pltpu.CompilerParams(vmem_limit_bytes=(8 << 20) + (13 << 10) * outer * local_rows)
    beside = pl.CostEstimate(flops=2 * 10**10, bytes_accessed=10**6, transcendentals=0)
    vmem = pl.BlockSpec(memory_space=pltpu.VMEM)
    smem = pl.BlockSpec(memory_space=pltpu.SMEM)
    anywhere = pl.BlockSpec(memory_space=pl.ANY)
    shape = jax.ShapeDtypeStruct
    dma = pltpu.SemaphoreType.DMA
    low, full = jnp.bfloat16, jnp.float32

    def call(kernel, name, **arguments):
        return pl.pallas_call(kernel, compiler_params=params, name=name, **arguments)

    def shift(array, axis, by):
        size = lax.axis_size(axis)
        if by > 0:
            return lax.ppermute(array, axis, [(n, target_of(n, by, size)) for n in range(size)])
        return lax.ppermute(array, axis, [(n, partner(n, -by, size)) for n in range(size)])

    part = shape((cache_rows, 2 * HEAD), low)
    block = shape((local_rows, 2 * HEAD), low)
    parts = call(
        split_kernel,
        "split",
        out_shape=(part,) * kvh,
        in_specs=[vmem],
        out_specs=(vmem,) * kvh,
        scratch_shapes=[dma((2 * kvh,))],
    )(jnp.concatenate([keys, values], axis=0))
    parts = [parts[0]] + [shift(parts[e], "kvh", e) for e in range(1, kvh)]
    stack = shape((2, 2, columns, HEAD), low)
    own_qd, other_qd = call(
        stack_kernel,
        "stack",
        out_shape=(stack, stack),
        in_specs=[vmem] * 4,
        out_specs=(vmem, vmem),
    )(queries, d_out, shift(queries, "pair", 1), shift(d_out, "pair", 1))
    own_block = call(
        join_kernel,
        "join",
        out_shape=block,
        in_specs=[anywhere] * kvh,
        out_specs=vmem,
        scratch_shapes=[dma((kvh,))],
        cost_estimate=beside,
    )(*parts)
    blocks = [own_block] + [shift(own_block, "outer", d) for d in range(1, outer)]

    table = call(
        functools.partial(table_kernel, outer),
        "table",
        out_shape=shape((2 * outer + 4, HEAD), jnp.int32),
        in_specs=[smem, anywhere],
        out_specs=vmem,
    )(slab_order, blocks[outer - 1])
    far = outer // 2 + 1
    groups = [[0, *range(far, outer)], list(range(1, far))]
    all_stats = shape((12, columns), full)
    results = []
    for n, members in enumerate(groups):
        score_rows = shape((2, (2 * len(members) + 1) * slab_rows, columns), full)
        results.append(
            call(
                functools.partial(stats_kernel, members),
                "stats",
                out_shape=(all_stats, score_rows, score_rows),
                in_specs=[vmem] * (3 + len(members)) + [anywhere] * min(n, 1),
                out_specs=(vmem,) * 3,
                cost_estimate=beside if n + 1 < len(groups) else None,
            )(table, own_qd, other_qd, *[blocks[d] for d in members], *[done[0] for done in results[-1:]])
        )
    stats, expon, grad_probs = zip(*results)
    mine = call(
        merge_kernel, "merge", out_shape=all_stats, in_specs=[vmem] * len(stats), out_specs=vmem
    )(*stats)
    theirs = shift(mine, "pair", 1)
    count = len(groups)
    high_rows = shape((2, 2 * outer * slab_rows, columns), low)
    low_rows = shape((2, outer * slab_rows, columns), low)
    grads = call(
        functools.partial(grads_kernel, outer, groups),
        "grads",
        out_shape=(shape(block.shape, full),) + (block,) * (outer - 1) + (high_rows, low_rows),
        in_specs=[vmem] * (4 + 3 * count),
        out_specs=(vmem,) * (outer + 2),
        scratch_shapes=[pltpu.VMEM(high_rows.shape, low), pltpu.VMEM(low_rows.shape, low)],
    )(table, own_qd, other_qd, *stats, theirs, *expon, *grad_probs)
    terms, score_grads = grads[:outer], grads[outer:]
    terms = [terms[0]] + [shift(terms[d], "outer", -d) for d in range(outer - 1, 0, -1)]
    own_grads, other_grads = call(
        functools.partial(query_kernel, outer, groups),
        "query_terms",
        out_shape=(shape(queries.shape, full), shape(queries.shape, low)),
        in_specs=[vmem] * (3 + outer),
        out_specs=(vmem, vmem),
        cost_estimate=beside,
    )(table, *blocks, *score_grads)
    received_grads = shift(other_grads, "pair", 1)
    owned = call(
        functools.partial(sum_kernel, outer),
        "sum",
        out_shape=(part,) * kvh,
        in_specs=[vmem] * outer,
        out_specs=(vmem,) * kvh,
        scratch_shapes=[pltpu.VMEM(block.shape, full)],
        cost_estimate=beside,
    )(*terms)
    owned = [owned[0]] + [shift(owned[e], "kvh", e) for e in range(1, kvh)]
    return call(
        place_kernel,
        "place",
        out_shape=(shape(queries.shape, low), shape(keys.shape, low), shape(values.shape, low)),
        in_specs=[vmem, vmem] + [anywhere] * kvh,
        out_specs=(anywhere,) * 3,
        scratch_shapes=[pltpu.VMEM(queries.shape, low), dma((2 * kvh + 1,))],
    )(own_grads, received_grads, *owned)


def solution(mesh):
    kvh = mesh.shape["kvh"]
    pairs = mesh.shape["seq"] // 2
    paired = Mesh(mesh.devices.reshape(pairs, 2, kvh), ("outer", "pair", "kvh"))
    seq = ("outer", "pair")
    cache = P(("outer", "pair", "kvh"), None)
    placed = (P(seq, "kvh"), cache, cache, P(seq, "kvh"), P())
    return jax.shard_map(
        per_device,
        mesh=paired,
        in_specs=placed,
        out_specs=(P(seq, "kvh"), cache, cache),
        check_vma=False,
    )
```

```python
import functools
import math

import jax
import jax.numpy as jnp
from jax import lax
from jax.experimental import pallas as pl
from jax.experimental.pallas import tpu as pltpu
from jax.sharding import Mesh
from jax.sharding import PartitionSpec as P

HEADS = 20
KV_HEADS = 4
HEAD = 128
GROUP = HEADS // KV_HEADS
SCALE = HEAD ** (-0.5)
EXPONENT_SCALE = SCALE * math.log2(math.e)
LOWEST = -1e30
ROWS_DOT_ROWS = (((1,), (1,)), ((), ()))
COLS_DOT_COLS = (((0,), (0,)), ((), ()))


def at_rows(start, size):
    return pl.ds(pl.multiple_of(start, size), size)


def load(source_ref, target_ref, sem):
    copy = pltpu.make_async_copy(source_ref, target_ref, sem)
    copy.start()
    return copy


def wait_all(copies):
    for copy in copies:
        copy.wait()


def partner(index, distance, size):
    if size & (size - 1) == 0:
        return index ^ distance
    return (index + size - distance) % size


def target_of(index, distance, size):
    if size & (size - 1) == 0:
        return index ^ distance
    return (index + distance) % size


def pick(condition, chosen, other):
    return lax.select(condition, chosen, jnp.full_like(chosen, other))


class Work:
    def __init__(self, table_ref, rows, members, block_refs):
        self.rows, self.members, self.block_refs = rows, members, block_refs
        self.low_rows = len(members) * rows

        def pair(at):
            return jnp.max(table_ref[2 * at : 2 * at + 1, :]), jnp.max(table_ref[2 * at + 1 : 2 * at + 2, :])

        self.pairs = [pair(d) for d in members]
        self.owners = [pair(table_ref.shape[0] // 2 - 2), pair(table_ref.shape[0] // 2 - 1)]

    @staticmethod
    def slot(place, half):
        return jnp.where(half == 0, place, 1 - place)

    def query_slot(self, owner, half):
        return self.slot(self.owners[owner][1], half)

    def key_rows(self, n, half):
        return at_rows(self.slot(self.pairs[n][1], half) * self.rows, self.rows)

    def keys(self, n, half, cols):
        return self.block_refs[n][self.key_rows(n, half), cols]

    def low_keys(self, cols):
        return jnp.concatenate([self.keys(n, 0, cols) for n in range(len(self.members))], axis=0)

    def tiles(self, owner):
        found = []
        for n, d in enumerate(self.members):
            here = pl.ds(self.low_rows + n * self.rows, self.rows)
            if owner == 0 and d == 0:
                found.append((n, 0, here, True))
                found.append((n, 1, pl.ds(2 * self.low_rows, self.rows), True))
            else:
                half = jnp.where(self.owners[owner][0] >= self.pairs[n][0], 0, 1)
                found.append((n, half, here, False))
        return found


def split_kernel(cache_ref, *refs):
    parts, sems = refs[:-1], refs[-1]
    kvh = len(parts)
    rows = parts[0].shape[0]
    copies = []
    for e, part_ref in enumerate(parts):
        cols = at_rows(target_of(lax.axis_index("kvh"), e, kvh) * HEAD, HEAD)
        for n in range(2):
            source = cache_ref.at[pl.ds(n * rows, rows), cols]
            copies.append(load(source, part_ref.at[:, pl.ds(n * HEAD, HEAD)], sems.at[2 * e + n]))
    wait_all(copies)


def table_kernel(outer, order_ref, after_ref, table_ref):
    at, side = lax.axis_index("outer"), lax.axis_index("pair")
    indices = [2 * partner(at, d, outer) + side for d in range(outer)]
    indices += [2 * at + side, 2 * at + 1 - side]
    for n, index in enumerate(indices):
        first, second = order_ref[2 * index], order_ref[2 * index + 1]
        row = table_ref.shape[1:]
        table_ref[2 * n : 2 * n + 1, :] = jnp.full((1, *row), jnp.minimum(first, second), jnp.int32)
        table_ref[2 * n + 1 : 2 * n + 2, :] = jnp.full((1, *row), jnp.where(first < second, 0, 1), jnp.int32)


def stack_kernel(*refs):
    sources, outs = refs[:4], refs[4:]
    rows = sources[0].shape[0] // 2
    for n, source_ref in enumerate(sources):
        for slot in range(2):
            for h in range(GROUP):
                outs[n // 2][n % 2, slot, h * rows : (h + 1) * rows, :] = source_ref[
                    slot * rows : (slot + 1) * rows, h * HEAD : (h + 1) * HEAD
                ]


def join_kernel(order, *refs):
    parts, (out_ref, sems) = refs[:-2], refs[-2:]
    kvh = len(parts)
    rows = parts[0].shape[0]
    copies = []
    for e, part_ref in zip(order, parts):
        source = partner(lax.axis_index("kvh"), e, kvh)
        copies.append(load(part_ref, out_ref.at[at_rows(source * rows, rows)], sems.at[e]))
    wait_all(copies)


def stats_kernel(members, table_ref, own_ref, other_ref, *refs):
    block_refs, (out_ref, e_ref, dp_ref) = refs[: len(members)], refs[-3:]
    rows = block_refs[0].shape[0] // 2
    work = Work(table_ref, rows, members, block_refs)
    low_part = pl.ds(0, work.low_rows)
    key_cols, value_cols = slice(0, HEAD), slice(HEAD, 2 * HEAD)

    def products(keys, queries):
        return lax.dot_general(keys, queries, ROWS_DOT_ROWS, preferred_element_type=jnp.float32)

    tops = []
    for owner, qd_ref in enumerate((own_ref, other_ref)):
        high = work.query_slot(owner, 1)
        scores = products(work.low_keys(key_cols), qd_ref[0, high])
        e_ref[owner, low_part, :] = scores
        dp_ref[owner, low_part, :] = products(work.low_keys(value_cols), qd_ref[1, high])
        top = [jnp.full((1, scores.shape[1]), LOWEST, jnp.float32), jnp.max(scores, axis=0, keepdims=True)]
        for n, half, here, masked in work.tiles(owner):
            slot = work.query_slot(owner, half)
            scores = products(work.keys(n, half, key_cols), qd_ref[0, slot])
            if masked:
                key = lax.broadcasted_iota(jnp.int32, scores.shape, 0)
                query = lax.rem(lax.broadcasted_iota(jnp.int32, (1, scores.shape[1]), 1), rows)
                scores = jnp.where(key <= query, scores, LOWEST)
            e_ref[owner, here, :] = scores
            dp_ref[owner, here, :] = products(work.keys(n, half, value_cols), qd_ref[1, slot])
            most = jnp.max(scores, axis=0, keepdims=True)
            for side in range(2):
                seen = most if masked else pick(half == side, most, LOWEST)
                if not masked or half == side:
                    top[side] = jnp.maximum(top[side], seen)
        tops.append(top)

    for owner, top in enumerate(tops):

        def sums(here, most):
            expon = jnp.exp2((e_ref[owner, here, :] - most) * EXPONENT_SCALE)
            e_ref[owner, here, :] = expon
            return [
                jnp.sum(expon, axis=0, keepdims=True),
                jnp.sum(expon * dp_ref[owner, here, :], axis=0, keepdims=True),
            ]

        zero = jnp.zeros_like(top[0])
        totals = [[zero, zero], sums(low_part, top[1])]
        for n, half, here, masked in work.tiles(owner):
            part = sums(here, top[half] if masked else lax.select(half == 0, top[0], top[1]))
            for side in range(2):
                if not masked or half == side:
                    seen = part if masked else [pick(half == side, one, 0) for one in part]
                    totals[side] = [total + one for total, one in zip(totals[side], seen)]
        for half in range(2):
            base = (2 * owner + half) * 3
            for n, row in enumerate((top[half], *totals[half])):
                out_ref[base + n : base + n + 1, :] = row


def merged(stats_refs, base):
    rows = [ref[base : base + 3, :] for ref in stats_refs]
    top = functools.reduce(jnp.maximum, [part[:1] for part in rows])
    weights = [jnp.exp2((part[:1] - top) * EXPONENT_SCALE) for part in rows]
    total = sum(weight * part[1:2] for weight, part in zip(weights, rows))
    delta = sum(weight * part[2:3] for weight, part in zip(weights, rows))
    return top, total, delta


def merge_kernel(*refs):
    stats_refs, out_ref = refs[:-1], refs[-1]
    for base in range(0, 12, 3):
        for n, row in enumerate(merged(stats_refs, base)):
            out_ref[base + n : base + n + 1, :] = row


def grads_kernel(outer, groups, table_ref, own_ref, other_ref, *refs):
    count = len(groups)
    stats_refs, theirs_ref, refs = refs[:count], refs[count], refs[count + 1 :]
    e_refs, dp_refs, refs = refs[:count], refs[count : 2 * count], refs[2 * count :]
    term_refs, gs_refs = refs[:outer], refs[outer:]
    rows = term_refs[0].shape[0] // 2
    weights, deltas = [[] for _ in groups], []
    for owner in range(2):
        delta = []
        group_weights = [[] for _ in groups]
        for half in range(2):
            base = (2 * owner + half) * 3
            base2 = (2 * (1 - owner) + half) * 3
            mine = merged(stats_refs, base)
            theirs = [theirs_ref[base2 + n : base2 + n + 1, :] for n in range(3)]
            top = jnp.maximum(mine[0], theirs[0])
            w1 = jnp.exp2((mine[0] - top) * EXPONENT_SCALE)
            w2 = jnp.exp2((theirs[0] - top) * EXPONENT_SCALE)
            total = w1 * mine[1] + w2 * theirs[1]
            delta.append((w1 * mine[2] + w2 * theirs[2]) / total)
            for n, stats_ref in enumerate(stats_refs):
                weight = jnp.exp2((stats_ref[base : base + 1, :] - top) * EXPONENT_SCALE)
                group_weights[n].append(weight / total)
        deltas.append(delta)
        for n in range(count):
            weights[n].append(group_weights[n])

    for n, members in enumerate(groups):
        work = Work(table_ref, rows, members, None)
        terms = [[None] * len(members), [None] * len(members)]

        def add(half, at, pair):
            old = terms[half][at]
            terms[half][at] = pair if old is None else [one + more for one, more in zip(old, pair)]

        for owner, qd_ref in enumerate((own_ref, other_ref)):

            def gradients(here, slot, weight, delta):
                probs = e_refs[n][owner, here, :] * weight
                grads = (probs * (dp_refs[n][owner, here, :] - delta)).astype(jnp.bfloat16)
                gs_refs[n][owner, here, :] = grads
                return [
                    jnp.dot(grads, qd_ref[0, slot], preferred_element_type=jnp.float32),
                    jnp.dot(probs.astype(jnp.bfloat16), qd_ref[1, slot], preferred_element_type=jnp.float32),
                ]

            weight, delta = weights[n][owner], deltas[owner]
            low_part = pl.ds(0, work.low_rows)
            part = gradients(low_part, work.query_slot(owner, 1), weight[1], delta[1])
            for at in range(len(members)):
                add(0, at, [one[at * rows : (at + 1) * rows] for one in part])
            for at, half, here, masked in work.tiles(owner):
                slot = work.query_slot(owner, half)
                if masked:
                    add(half, at, gradients(here, slot, weight[half], delta[half]))
                else:
                    is_low = half == 0
                    part = gradients(here, slot, lax.select(is_low, *weight), lax.select(is_low, *delta))
                    for side in range(2):
                        add(side, at, [pick(half == side, one, 0) for one in part])
        for at, d in enumerate(members):
            term_ref = term_refs[d]
            for half in range(2):
                target = work.key_rows(at, half)
                of_keys, of_values = terms[half][at]
                term_ref[target, :HEAD] = (of_keys * SCALE).astype(term_ref.dtype)
                term_ref[target, HEAD:] = of_values.astype(term_ref.dtype)


def query_kernel(outer, groups, owner, table_ref, *refs):
    count = len(groups)
    block_refs, gs_refs, out_ref = refs[:outer], refs[outer : outer + count], refs[-1]
    rows = out_ref.shape[0] // 2
    works = [Work(table_ref, rows, members, [block_refs[d] for d in members]) for members in groups]
    cols = slice(0, HEAD)
    totals = [None, None]

    def add(half, part):
        totals[half] = part if totals[half] is None else totals[half] + part

    for gs_ref, work in zip(gs_refs, works):

        def terms(keys, here):
            return lax.dot_general(
                keys, gs_ref[owner, here, :], COLS_DOT_COLS, preferred_element_type=jnp.float32
            )

        add(1, terms(work.low_keys(cols), pl.ds(0, work.low_rows)))
        for n, half, here, masked in work.tiles(owner):
            part = terms(work.keys(n, half, cols), here)
            for side in range(2):
                if not masked:
                    add(side, pick(half == side, part, 0))
                elif half == side:
                    add(side, part)
    for half in range(2):
        place = at_rows(works[0].query_slot(owner, half) * rows, rows)
        grads = (jnp.transpose(totals[half]) * SCALE).astype(out_ref.dtype)
        for h in range(GROUP):
            out_ref[place, h * HEAD : (h + 1) * HEAD] = grads[h * rows : (h + 1) * rows, :]


def sum_kernel(outer, *refs):
    terms, outs, total_ref = refs[:outer], refs[outer:-1], refs[-1]
    total = terms[0][...]
    for term_ref in terms[1:]:
        total = total + term_ref[...].astype(jnp.float32)
    total_ref[...] = total
    kvh = len(outs)
    rows = outs[0].shape[0]
    for e, out_ref in enumerate(outs):
        target = target_of(lax.axis_index("kvh"), e, kvh)
        out_ref[...] = total_ref[at_rows(target * rows, rows), :].astype(jnp.bfloat16)


def place_kernel(order, own_ref, received_ref, *refs):
    parts, (dq_out, key_out, value_out, dq_ref, sems) = refs[:-5], refs[-5:]
    kvh = len(parts)
    copies = []
    for e, part_ref in zip(order, parts):
        cols = at_rows(partner(lax.axis_index("kvh"), e, kvh) * HEAD, HEAD)
        copies.append(load(part_ref.at[:, pl.ds(0, HEAD)], key_out.at[:, cols], sems.at[2 * e]))
        copies.append(load(part_ref.at[:, pl.ds(HEAD, HEAD)], value_out.at[:, cols], sems.at[2 * e + 1]))
    dq_ref[...] = (own_ref[...] + received_ref[...].astype(jnp.float32)).astype(jnp.bfloat16)
    copies.append(load(dq_ref, dq_out, sems.at[2 * kvh]))
    wait_all(copies)


def per_device(queries, keys, values, d_out, slab_order):
    kvh = lax.axis_size("kvh")
    outer = lax.axis_size("outer")
    local_rows, query_width = queries.shape
    cache_rows = keys.shape[0]
    slab_rows = local_rows // 2
    columns = GROUP * slab_rows
    params = pltpu.CompilerParams(vmem_limit_bytes=(8 << 20) + (10 << 10) * outer * local_rows)
    beside = pl.CostEstimate(flops=2 * 10**10, bytes_accessed=10**6, transcendentals=0)
    vmem = pl.BlockSpec(memory_space=pltpu.VMEM)
    smem = pl.BlockSpec(memory_space=pltpu.SMEM)
    anywhere = pl.BlockSpec(memory_space=pl.ANY)
    shape = jax.ShapeDtypeStruct
    dma = pltpu.SemaphoreType.DMA
    low, full = jnp.bfloat16, jnp.float32

    def call(kernel, name, **arguments):
        return pl.pallas_call(kernel, compiler_params=params, name=name, **arguments)

    def shift(array, axis, by):
        size = lax.axis_size(axis)
        if by > 0:
            return lax.ppermute(array, axis, [(n, target_of(n, by, size)) for n in range(size)])
        return lax.ppermute(array, axis, [(n, partner(n, -by, size)) for n in range(size)])

    order = (0, *range(2, kvh), *range(1, min(kvh, 2)))

    def exchange(parts):
        return [shift(parts[e], "kvh", e) if e > 0 else parts[e] for e in order]

    part = shape((cache_rows, 2 * HEAD), low)
    block = shape((local_rows, 2 * HEAD), low)
    parts = call(
        split_kernel,
        "split",
        out_shape=(part,) * kvh,
        in_specs=[vmem],
        out_specs=(vmem,) * kvh,
        scratch_shapes=[dma((2 * kvh,))],
    )(jnp.concatenate([keys, values], axis=0))
    parts = exchange(parts)
    stack = shape((2, 2, columns, HEAD), low)
    own_qd, other_qd = call(
        stack_kernel,
        "stack",
        out_shape=(stack, stack),
        in_specs=[vmem] * 4,
        out_specs=(vmem, vmem),
    )(queries, d_out, shift(queries, "pair", 1), shift(d_out, "pair", 1))
    own_block = call(
        functools.partial(join_kernel, order),
        "join",
        out_shape=block,
        in_specs=[anywhere] * kvh,
        out_specs=vmem,
        scratch_shapes=[dma((kvh,))],
        cost_estimate=beside,
    )(*parts)
    blocks = [own_block] + [shift(own_block, "outer", d) for d in range(1, outer)]

    table = call(
        functools.partial(table_kernel, outer),
        "table",
        out_shape=shape((2 * outer + 4, HEAD), jnp.int32),
        in_specs=[smem, anywhere],
        out_specs=vmem,
    )(slab_order, blocks[outer - 1])
    far = outer // 2 + 1
    groups = [[0, *range(far, outer)], list(range(1, far))]
    all_stats = shape((12, columns), full)
    results = []
    for n, members in enumerate(groups):
        score_rows = shape((2, (2 * len(members) + 1) * slab_rows, columns), full)
        results.append(
            call(
                functools.partial(stats_kernel, members),
                "stats",
                out_shape=(all_stats, score_rows, score_rows),
                in_specs=[vmem] * (3 + len(members)) + [anywhere] * min(n, 1),
                out_specs=(vmem,) * 3,
                cost_estimate=beside if n + 1 < len(groups) else None,
            )(table, own_qd, other_qd, *[blocks[d] for d in members], *[done[0] for done in results[-1:]])
        )
    stats, expon, grad_probs = zip(*results)
    mine = call(
        merge_kernel, "merge", out_shape=all_stats, in_specs=[vmem] * len(stats), out_specs=vmem
    )(*stats)
    theirs = shift(mine, "pair", 1)
    count = len(groups)
    grads = call(
        functools.partial(grads_kernel, outer, groups),
        "grads",
        out_shape=(shape(block.shape, full),)
        + (block,) * (outer - 1)
        + tuple(shape(scores.shape, low) for scores in expon),
        in_specs=[vmem] * (4 + 3 * count),
        out_specs=(vmem,) * (outer + count),
    )(table, own_qd, other_qd, *stats, theirs, *expon, *grad_probs)
    terms, score_grads = grads[:outer], grads[outer:]
    terms = [terms[0]] + [shift(terms[d], "outer", -d) for d in range(outer - 1, 0, -1)]
    def query_terms(owner, kind, *after):
        return call(
            functools.partial(query_kernel, outer, groups, owner),
            "query_terms",
            out_shape=shape(queries.shape, kind),
            in_specs=[vmem] * (1 + outer + count) + [anywhere] * len(after),
            out_specs=vmem,
            cost_estimate=beside,
        )(table, *blocks, *score_grads, *after)

    other_grads = query_terms(1, low)
    received_grads = shift(other_grads, "pair", 1)
    own_grads = query_terms(0, full, other_grads)
    owned = call(
        functools.partial(sum_kernel, outer),
        "sum",
        out_shape=(part,) * kvh,
        in_specs=[vmem] * outer,
        out_specs=(vmem,) * kvh,
        scratch_shapes=[pltpu.VMEM(block.shape, full)],
        cost_estimate=beside,
    )(*terms)
    owned = exchange(owned)
    return call(
        functools.partial(place_kernel, order),
        "place",
        out_shape=(shape(queries.shape, low), shape(keys.shape, low), shape(values.shape, low)),
        in_specs=[vmem, vmem] + [anywhere] * kvh,
        out_specs=(anywhere,) * 3,
        scratch_shapes=[pltpu.VMEM(queries.shape, low), dma((2 * kvh + 1,))],
    )(own_grads, received_grads, *owned)


def solution(mesh):
    kvh = mesh.shape["kvh"]
    pairs = mesh.shape["seq"] // 2
    paired = Mesh(mesh.devices.reshape(pairs, 2, kvh), ("outer", "pair", "kvh"))
    seq = ("outer", "pair")
    cache = P(("outer", "pair", "kvh"), None)
    placed = (P(seq, "kvh"), cache, cache, P(seq, "kvh"), P())
    return jax.shard_map(
        per_device,
        mesh=paired,
        in_specs=placed,
        out_specs=(P(seq, "kvh"), cache, cache),
        check_vma=False,
    )
```

```python
import functools
import math

import jax
import jax.numpy as jnp
from jax import lax
from jax.experimental import pallas as pl
from jax.experimental.pallas import tpu as pltpu
from jax.sharding import Mesh
from jax.sharding import PartitionSpec as P

HEADS = 20
KV_HEADS = 4
HEAD = 128
GROUP = HEADS // KV_HEADS
SCALE = HEAD ** (-0.5)
EXPONENT_SCALE = SCALE * math.log2(math.e)
LOWEST = -1e30
ROWS_DOT_ROWS = (((1,), (1,)), ((), ()))
COLS_DOT_COLS = (((0,), (0,)), ((), ()))


def at_rows(start, size):
    return pl.ds(pl.multiple_of(start, size), size)


def load(source_ref, target_ref, sem):
    copy = pltpu.make_async_copy(source_ref, target_ref, sem)
    copy.start()
    return copy


def wait_all(copies):
    for copy in copies:
        copy.wait()


def partner(index, distance, size):
    if size & (size - 1) == 0:
        return index ^ distance
    return (index + size - distance) % size


def target_of(index, distance, size):
    if size & (size - 1) == 0:
        return index ^ distance
    return (index + distance) % size


def pick(condition, chosen, other):
    return lax.select(condition, chosen, jnp.full_like(chosen, other))


class Work:
    def __init__(self, table_ref, rows, members, block_refs):
        self.rows, self.members, self.block_refs = rows, members, block_refs
        self.low_rows = len(members) * rows

        def pair(at):
            return jnp.max(table_ref[2 * at : 2 * at + 1, :]), jnp.max(table_ref[2 * at + 1 : 2 * at + 2, :])

        self.pairs = [pair(d) for d in members]
        self.owners = [pair(table_ref.shape[0] // 2 - 2), pair(table_ref.shape[0] // 2 - 1)]

    @staticmethod
    def slot(place, half):
        return jnp.where(half == 0, place, 1 - place)

    def query_slot(self, owner, half):
        return self.slot(self.owners[owner][1], half)

    def key_rows(self, n, half):
        return at_rows(self.slot(self.pairs[n][1], half) * self.rows, self.rows)

    def keys(self, n, half, cols):
        return self.block_refs[n][self.key_rows(n, half), cols]

    def low_keys(self, cols):
        return jnp.concatenate([self.keys(n, 0, cols) for n in range(len(self.members))], axis=0)

    def tiles(self, owner):
        found = []
        for n, d in enumerate(self.members):
            here = pl.ds(self.low_rows + n * self.rows, self.rows)
            if owner == 0 and d == 0:
                found.append((n, 0, here, True))
                found.append((n, 1, pl.ds(2 * self.low_rows, self.rows), True))
            else:
                half = jnp.where(self.owners[owner][0] >= self.pairs[n][0], 0, 1)
                found.append((n, half, here, False))
        return found


def split_kernel(cache_ref, *refs):
    parts, sems = refs[:-1], refs[-1]
    kvh = len(parts)
    rows = parts[0].shape[0]
    copies = []
    for e, part_ref in enumerate(parts):
        cols = at_rows(target_of(lax.axis_index("kvh"), e, kvh) * HEAD, HEAD)
        for n in range(2):
            source = cache_ref.at[pl.ds(n * rows, rows), cols]
            copies.append(load(source, part_ref.at[:, pl.ds(n * HEAD, HEAD)], sems.at[2 * e + n]))
    wait_all(copies)


def table_kernel(outer, order_ref, after_ref, table_ref):
    at, side = lax.axis_index("outer"), lax.axis_index("pair")
    indices = [2 * partner(at, d, outer) + side for d in range(outer)]
    indices += [2 * at + side, 2 * at + 1 - side]
    for n, index in enumerate(indices):
        first, second = order_ref[2 * index], order_ref[2 * index + 1]
        row = table_ref.shape[1:]
        table_ref[2 * n : 2 * n + 1, :] = jnp.full((1, *row), jnp.minimum(first, second), jnp.int32)
        table_ref[2 * n + 1 : 2 * n + 2, :] = jnp.full((1, *row), jnp.where(first < second, 0, 1), jnp.int32)


def stack_kernel(*refs):
    sources, outs = refs[:4], refs[4:]
    rows = sources[0].shape[0] // 2
    for n, source_ref in enumerate(sources):
        for slot in range(2):
            for h in range(GROUP):
                outs[n // 2][n % 2, slot, h * rows : (h + 1) * rows, :] = source_ref[
                    slot * rows : (slot + 1) * rows, h * HEAD : (h + 1) * HEAD
                ]


def join_kernel(order, *refs):
    parts, (out_ref, sems) = refs[:-2], refs[-2:]
    kvh = len(parts)
    rows = parts[0].shape[0]
    copies = []
    for e, part_ref in zip(order, parts):
        source = partner(lax.axis_index("kvh"), e, kvh)
        copies.append(load(part_ref, out_ref.at[at_rows(source * rows, rows)], sems.at[e]))
    wait_all(copies)


def stats_kernel(members, table_ref, own_ref, other_ref, *refs):
    block_refs, (out_ref, e_ref, dp_ref) = refs[: len(members)], refs[-3:]
    rows = block_refs[0].shape[0] // 2
    work = Work(table_ref, rows, members, block_refs)
    low_part = pl.ds(0, work.low_rows)
    key_cols, value_cols = slice(0, HEAD), slice(HEAD, 2 * HEAD)

    def products(keys, queries):
        return lax.dot_general(keys, queries, ROWS_DOT_ROWS, preferred_element_type=jnp.float32)

    tops = []
    for owner, qd_ref in enumerate((own_ref, other_ref)):
        high = work.query_slot(owner, 1)
        scores = products(work.low_keys(key_cols), qd_ref[0, high])
        e_ref[owner, low_part, :] = scores
        dp_ref[owner, low_part, :] = products(work.low_keys(value_cols), qd_ref[1, high])
        top = [jnp.full((1, scores.shape[1]), LOWEST, jnp.float32), jnp.max(scores, axis=0, keepdims=True)]
        for n, half, here, masked in work.tiles(owner):
            slot = work.query_slot(owner, half)
            scores = products(work.keys(n, half, key_cols), qd_ref[0, slot])
            if masked:
                key = lax.broadcasted_iota(jnp.int32, scores.shape, 0)
                query = lax.rem(lax.broadcasted_iota(jnp.int32, (1, scores.shape[1]), 1), rows)
                scores = jnp.where(key <= query, scores, LOWEST)
            e_ref[owner, here, :] = scores
            dp_ref[owner, here, :] = products(work.keys(n, half, value_cols), qd_ref[1, slot])
            most = jnp.max(scores, axis=0, keepdims=True)
            for side in range(2):
                seen = most if masked else pick(half == side, most, LOWEST)
                if not masked or half == side:
                    top[side] = jnp.maximum(top[side], seen)
        tops.append(top)

    for owner, top in enumerate(tops):

        def sums(here, most):
            expon = jnp.exp2((e_ref[owner, here, :] - most) * EXPONENT_SCALE)
            e_ref[owner, here, :] = expon
            return [
                jnp.sum(expon, axis=0, keepdims=True),
                jnp.sum(expon * dp_ref[owner, here, :], axis=0, keepdims=True),
            ]

        zero = jnp.zeros_like(top[0])
        totals = [[zero, zero], sums(low_part, top[1])]
        for n, half, here, masked in work.tiles(owner):
            part = sums(here, top[half] if masked else lax.select(half == 0, top[0], top[1]))
            for side in range(2):
                if not masked or half == side:
                    seen = part if masked else [pick(half == side, one, 0) for one in part]
                    totals[side] = [total + one for total, one in zip(totals[side], seen)]
        for half in range(2):
            base = (2 * owner + half) * 3
            for n, row in enumerate((top[half], *totals[half])):
                out_ref[base + n : base + n + 1, :] = row


def merged(stats_refs, base):
    rows = [ref[base : base + 3, :] for ref in stats_refs]
    top = functools.reduce(jnp.maximum, [part[:1] for part in rows])
    weights = [jnp.exp2((part[:1] - top) * EXPONENT_SCALE) for part in rows]
    total = sum(weight * part[1:2] for weight, part in zip(weights, rows))
    delta = sum(weight * part[2:3] for weight, part in zip(weights, rows))
    return top, total, delta


def merge_kernel(*refs):
    stats_refs, out_ref = refs[:-1], refs[-1]
    for base in range(0, 12, 3):
        for n, row in enumerate(merged(stats_refs, base)):
            out_ref[base + n : base + n + 1, :] = row


def grads_kernel(outer, groups, table_ref, own_ref, other_ref, *refs):
    count = len(groups)
    stats_refs, theirs_ref, refs = refs[:count], refs[count], refs[count + 1 :]
    e_refs, dp_refs, refs = refs[:count], refs[count : 2 * count], refs[2 * count :]
    term_refs, gs_refs = refs[:outer], refs[outer:]
    rows = term_refs[0].shape[0] // 2
    weights, deltas = [[] for _ in groups], []
    for owner in range(2):
        delta = []
        group_weights = [[] for _ in groups]
        for half in range(2):
            base = (2 * owner + half) * 3
            base2 = (2 * (1 - owner) + half) * 3
            mine = merged(stats_refs, base)
            theirs = [theirs_ref[base2 + n : base2 + n + 1, :] for n in range(3)]
            top = jnp.maximum(mine[0], theirs[0])
            w1 = jnp.exp2((mine[0] - top) * EXPONENT_SCALE)
            w2 = jnp.exp2((theirs[0] - top) * EXPONENT_SCALE)
            total = w1 * mine[1] + w2 * theirs[1]
            delta.append((w1 * mine[2] + w2 * theirs[2]) / total)
            for n, stats_ref in enumerate(stats_refs):
                weight = jnp.exp2((stats_ref[base : base + 1, :] - top) * EXPONENT_SCALE)
                group_weights[n].append(weight / total)
        deltas.append(delta)
        for n in range(count):
            weights[n].append(group_weights[n])

    for n, members in enumerate(groups):
        work = Work(table_ref, rows, members, None)
        terms = [[None] * len(members), [None] * len(members)]

        def add(half, at, pair):
            old = terms[half][at]
            terms[half][at] = pair if old is None else [one + more for one, more in zip(old, pair)]

        for owner, qd_ref in enumerate((own_ref, other_ref)):

            def gradients(here, slot, weight, delta):
                probs = e_refs[n][owner, here, :] * weight
                grads = (probs * (dp_refs[n][owner, here, :] - delta)).astype(jnp.bfloat16)
                gs_refs[n][owner, here, :] = grads
                return [
                    jnp.dot(grads, qd_ref[0, slot], preferred_element_type=jnp.float32),
                    jnp.dot(probs.astype(jnp.bfloat16), qd_ref[1, slot], preferred_element_type=jnp.float32),
                ]

            weight, delta = weights[n][owner], deltas[owner]
            low_part = pl.ds(0, work.low_rows)
            part = gradients(low_part, work.query_slot(owner, 1), weight[1], delta[1])
            for at in range(len(members)):
                add(0, at, [one[at * rows : (at + 1) * rows] for one in part])
            for at, half, here, masked in work.tiles(owner):
                slot = work.query_slot(owner, half)
                if masked:
                    add(half, at, gradients(here, slot, weight[half], delta[half]))
                else:
                    is_low = half == 0
                    part = gradients(here, slot, lax.select(is_low, *weight), lax.select(is_low, *delta))
                    for side in range(2):
                        add(side, at, [pick(half == side, one, 0) for one in part])
        for at, d in enumerate(members):
            term_ref = term_refs[d]
            for half in range(2):
                target = work.key_rows(at, half)
                of_keys, of_values = terms[half][at]
                term_ref[target, :HEAD] = (of_keys * SCALE).astype(term_ref.dtype)
                term_ref[target, HEAD:] = of_values.astype(term_ref.dtype)


def query_kernel(outer, groups, owner, table_ref, *refs):
    count = len(groups)
    block_refs, gs_refs, out_ref = refs[:outer], refs[outer : outer + count], refs[-1]
    rows = out_ref.shape[0] // 2
    works = [Work(table_ref, rows, members, [block_refs[d] for d in members]) for members in groups]
    cols = slice(0, HEAD)
    totals = [None, None]

    def add(half, part):
        totals[half] = part if totals[half] is None else totals[half] + part

    for gs_ref, work in zip(gs_refs, works):

        def terms(keys, here):
            return lax.dot_general(
                keys, gs_ref[owner, here, :], COLS_DOT_COLS, preferred_element_type=jnp.float32
            )

        add(1, terms(work.low_keys(cols), pl.ds(0, work.low_rows)))
        for n, half, here, masked in work.tiles(owner):
            part = terms(work.keys(n, half, cols), here)
            for side in range(2):
                if not masked:
                    add(side, pick(half == side, part, 0))
                elif half == side:
                    add(side, part)
    for half in range(2):
        place = at_rows(works[0].query_slot(owner, half) * rows, rows)
        grads = (jnp.transpose(totals[half]) * SCALE).astype(out_ref.dtype)
        for h in range(GROUP):
            out_ref[place, h * HEAD : (h + 1) * HEAD] = grads[h * rows : (h + 1) * rows, :]


def sum_kernel(outer, *refs):
    terms, outs, total_ref = refs[:outer], refs[outer:-1], refs[-1]
    total = terms[0][...]
    for term_ref in terms[1:]:
        total = total + term_ref[...].astype(jnp.float32)
    total_ref[...] = total
    kvh = len(outs)
    rows = outs[0].shape[0]
    for e, out_ref in enumerate(outs):
        target = target_of(lax.axis_index("kvh"), e, kvh)
        out_ref[...] = total_ref[at_rows(target * rows, rows), :].astype(jnp.bfloat16)


def place_kernel(order, own_ref, received_ref, *refs):
    parts, (dq_out, key_out, value_out, dq_ref, sems) = refs[:-5], refs[-5:]
    kvh = len(parts)
    copies = []
    for e, part_ref in zip(order, parts):
        cols = at_rows(partner(lax.axis_index("kvh"), e, kvh) * HEAD, HEAD)
        copies.append(load(part_ref.at[:, pl.ds(0, HEAD)], key_out.at[:, cols], sems.at[2 * e]))
        copies.append(load(part_ref.at[:, pl.ds(HEAD, HEAD)], value_out.at[:, cols], sems.at[2 * e + 1]))
    dq_ref[...] = (own_ref[...] + received_ref[...].astype(jnp.float32)).astype(jnp.bfloat16)
    copies.append(load(dq_ref, dq_out, sems.at[2 * kvh]))
    wait_all(copies)


def per_device(queries, keys, values, d_out, slab_order):
    kvh = lax.axis_size("kvh")
    outer = lax.axis_size("outer")
    local_rows, query_width = queries.shape
    cache_rows = keys.shape[0]
    slab_rows = local_rows // 2
    columns = GROUP * slab_rows
    params = pltpu.CompilerParams(vmem_limit_bytes=(8 << 20) + (10 << 10) * outer * local_rows)
    beside = pl.CostEstimate(flops=2 * 10**10, bytes_accessed=10**6, transcendentals=0)
    vmem = pl.BlockSpec(memory_space=pltpu.VMEM)
    smem = pl.BlockSpec(memory_space=pltpu.SMEM)
    anywhere = pl.BlockSpec(memory_space=pl.ANY)
    shape = jax.ShapeDtypeStruct
    dma = pltpu.SemaphoreType.DMA
    low, full = jnp.bfloat16, jnp.float32

    def call(kernel, name, **arguments):
        return pl.pallas_call(kernel, compiler_params=params, name=name, **arguments)

    def shift(array, axis, by):
        size = lax.axis_size(axis)
        if by > 0:
            return lax.ppermute(array, axis, [(n, target_of(n, by, size)) for n in range(size)])
        return lax.ppermute(array, axis, [(n, partner(n, -by, size)) for n in range(size)])

    order = (0, *range(2, kvh), *range(1, min(kvh, 2)))

    def exchange(parts):
        return [shift(parts[e], "kvh", e) if e > 0 else parts[e] for e in order]

    part = shape((cache_rows, 2 * HEAD), low)
    block = shape((local_rows, 2 * HEAD), low)
    parts = call(
        split_kernel,
        "split",
        out_shape=(part,) * kvh,
        in_specs=[vmem],
        out_specs=(vmem,) * kvh,
        scratch_shapes=[dma((2 * kvh,))],
    )(jnp.concatenate([keys, values], axis=0))
    parts = exchange(parts)
    stack = shape((2, 2, columns, HEAD), low)
    queries2 = shift(queries, "pair", 1)
    own_qd, other_qd = call(
        stack_kernel,
        "stack",
        out_shape=(stack, stack),
        in_specs=[vmem] * 4,
        out_specs=(vmem, vmem),
    )(queries, d_out, queries2, shift(d_out, "pair", 1))
    own_block = call(
        functools.partial(join_kernel, order),
        "join",
        out_shape=block,
        in_specs=[anywhere] * kvh,
        out_specs=vmem,
        scratch_shapes=[dma((kvh,))],
        cost_estimate=beside,
    )(*parts)
    blocks = [own_block] + [shift(own_block, "outer", d) for d in range(1, outer)]

    table = call(
        functools.partial(table_kernel, outer),
        "table",
        out_shape=shape((2 * outer + 4, HEAD), jnp.int32),
        in_specs=[smem, anywhere],
        out_specs=vmem,
    )(slab_order, queries2)
    groups = [[0, *range(outer - 1, 0, -1)]]
    all_stats = shape((12, columns), full)
    results = []
    for n, members in enumerate(groups):
        score_rows = shape((2, (2 * len(members) + 1) * slab_rows, columns), full)
        results.append(
            call(
                functools.partial(stats_kernel, members),
                "stats",
                out_shape=(all_stats, score_rows, score_rows),
                in_specs=[vmem] * (3 + len(members)) + [anywhere] * min(n, 1),
                out_specs=(vmem,) * 3,
                cost_estimate=beside if n + 1 < len(groups) else None,
            )(table, own_qd, other_qd, *[blocks[d] for d in members], *[done[0] for done in results[-1:]])
        )
    stats, expon, grad_probs = zip(*results)
    mine = stats[0]
    if len(stats) > 1:
        mine = call(
            merge_kernel, "merge", out_shape=all_stats, in_specs=[vmem] * len(stats), out_specs=vmem
        )(*stats)
    theirs = shift(mine, "pair", 1)
    count = len(groups)
    grads = call(
        functools.partial(grads_kernel, outer, groups),
        "grads",
        out_shape=(shape(block.shape, full),)
        + (block,) * (outer - 1)
        + tuple(shape(scores.shape, low) for scores in expon),
        in_specs=[vmem] * (4 + 3 * count),
        out_specs=(vmem,) * (outer + count),
    )(table, own_qd, other_qd, *stats, theirs, *expon, *grad_probs)
    terms, score_grads = grads[:outer], grads[outer:]
    terms = [terms[0]] + [shift(terms[d], "outer", -d) for d in range(outer - 1, 0, -1)]
    def query_terms(owner, kind, *after):
        return call(
            functools.partial(query_kernel, outer, groups, owner),
            "query_terms",
            out_shape=shape(queries.shape, kind),
            in_specs=[vmem] * (1 + outer + count) + [anywhere] * len(after),
            out_specs=vmem,
            cost_estimate=beside,
        )(table, *blocks, *score_grads, *after)

    other_grads = query_terms(1, low)
    received_grads = shift(other_grads, "pair", 1)
    own_grads = query_terms(0, full, other_grads)
    owned = call(
        functools.partial(sum_kernel, outer),
        "sum",
        out_shape=(part,) * kvh,
        in_specs=[vmem] * outer,
        out_specs=(vmem,) * kvh,
        scratch_shapes=[pltpu.VMEM(block.shape, full)],
        cost_estimate=beside,
    )(*terms)
    owned = exchange(owned)
    return call(
        functools.partial(place_kernel, order),
        "place",
        out_shape=(shape(queries.shape, low), shape(keys.shape, low), shape(values.shape, low)),
        in_specs=[vmem, vmem] + [anywhere] * kvh,
        out_specs=(anywhere,) * 3,
        scratch_shapes=[pltpu.VMEM(queries.shape, low), dma((2 * kvh + 1,))],
    )(own_grads, received_grads, *owned)


def solution(mesh):
    kvh = mesh.shape["kvh"]
    pairs = mesh.shape["seq"] // 2
    paired = Mesh(mesh.devices.reshape(pairs, 2, kvh), ("outer", "pair", "kvh"))
    seq = ("outer", "pair")
    cache = P(("outer", "pair", "kvh"), None)
    placed = (P(seq, "kvh"), cache, cache, P(seq, "kvh"), P())
    return jax.shard_map(
        per_device,
        mesh=paired,
        in_specs=placed,
        out_specs=(P(seq, "kvh"), cache, cache),
        check_vma=False,
    )
```

```python
import functools
import math

import jax
import jax.numpy as jnp
from jax import lax
from jax.experimental import pallas as pl
from jax.experimental.pallas import tpu as pltpu
from jax.sharding import Mesh
from jax.sharding import PartitionSpec as P

HEADS = 20
KV_HEADS = 4
HEAD = 128
GROUP = HEADS // KV_HEADS
SCALE = HEAD ** (-0.5)
EXPONENT_SCALE = SCALE * math.log2(math.e)
LOWEST = -1e30
ROWS_DOT_ROWS = (((1,), (1,)), ((), ()))
COLS_DOT_COLS = (((0,), (0,)), ((), ()))


def at_rows(start, size):
    return pl.ds(pl.multiple_of(start, size), size)


def load(source_ref, target_ref, sem):
    copy = pltpu.make_async_copy(source_ref, target_ref, sem)
    copy.start()
    return copy


def wait_all(copies):
    for copy in copies:
        copy.wait()


def partner(index, distance, size):
    if size & (size - 1) == 0:
        return index ^ distance
    return (index + size - distance) % size


def target_of(index, distance, size):
    if size & (size - 1) == 0:
        return index ^ distance
    return (index + distance) % size


def pick(condition, chosen, other):
    return lax.select(condition, chosen, jnp.full_like(chosen, other))


class Work:
    def __init__(self, table_ref, rows, members, block_refs):
        self.rows, self.members, self.block_refs = rows, members, block_refs
        self.low_rows = len(members) * rows

        def pair(at):
            return jnp.max(table_ref[2 * at : 2 * at + 1, :]), jnp.max(table_ref[2 * at + 1 : 2 * at + 2, :])

        self.pairs = [pair(d) for d in members]
        self.owners = [pair(table_ref.shape[0] // 2 - 2), pair(table_ref.shape[0] // 2 - 1)]

    @staticmethod
    def slot(place, half):
        return jnp.where(half == 0, place, 1 - place)

    def query_slot(self, owner, half):
        return self.slot(self.owners[owner][1], half)

    def key_rows(self, n, half):
        return at_rows(self.slot(self.pairs[n][1], half) * self.rows, self.rows)

    def keys(self, n, half, cols):
        return self.block_refs[n][self.key_rows(n, half), cols]

    def low_keys(self, cols):
        return jnp.concatenate([self.keys(n, 0, cols) for n in range(len(self.members))], axis=0)

    def tiles(self, owner):
        found = []
        for n, d in enumerate(self.members):
            here = pl.ds(self.low_rows + n * self.rows, self.rows)
            if owner == 0 and d == 0:
                found.append((n, 0, here, True))
                found.append((n, 1, pl.ds(2 * self.low_rows, self.rows), True))
            else:
                half = jnp.where(self.owners[owner][0] >= self.pairs[n][0], 0, 1)
                found.append((n, half, here, False))
        return found


def split_kernel(cache_ref, *refs):
    parts, sems = refs[:-1], refs[-1]
    kvh = len(parts)
    rows = parts[0].shape[0]
    copies = []
    for e, part_ref in enumerate(parts):
        cols = at_rows(target_of(lax.axis_index("kvh"), e, kvh) * HEAD, HEAD)
        for n in range(2):
            source = cache_ref.at[pl.ds(n * rows, rows), cols]
            copies.append(load(source, part_ref.at[:, pl.ds(n * HEAD, HEAD)], sems.at[2 * e + n]))
    wait_all(copies)


def table_kernel(outer, order_ref, after_ref, table_ref):
    at, side = lax.axis_index("outer"), lax.axis_index("pair")
    indices = [2 * partner(at, d, outer) + side for d in range(outer)]
    indices += [2 * at + side, 2 * at + 1 - side]
    for n, index in enumerate(indices):
        first, second = order_ref[2 * index], order_ref[2 * index + 1]
        row = table_ref.shape[1:]
        table_ref[2 * n : 2 * n + 1, :] = jnp.full((1, *row), jnp.minimum(first, second), jnp.int32)
        table_ref[2 * n + 1 : 2 * n + 2, :] = jnp.full((1, *row), jnp.where(first < second, 0, 1), jnp.int32)


def stack_kernel(*refs):
    sources, outs = refs[:4], refs[4:]
    rows = sources[0].shape[0] // 2
    for n, source_ref in enumerate(sources):
        for slot in range(2):
            for h in range(GROUP):
                outs[n // 2][n % 2, slot, h * rows : (h + 1) * rows, :] = source_ref[
                    slot * rows : (slot + 1) * rows, h * HEAD : (h + 1) * HEAD
                ]


def join_kernel(order, *refs):
    parts, (out_ref, sems) = refs[:-2], refs[-2:]
    kvh = len(parts)
    rows = parts[0].shape[0]
    copies = []
    for e, part_ref in zip(order, parts):
        source = partner(lax.axis_index("kvh"), e, kvh)
        copies.append(load(part_ref, out_ref.at[at_rows(source * rows, rows)], sems.at[e]))
    wait_all(copies)


def stats_kernel(members, table_ref, own_ref, other_ref, *refs):
    block_refs, (out_ref, e_ref, dp_ref) = refs[: len(members)], refs[-3:]
    rows = block_refs[0].shape[0] // 2
    work = Work(table_ref, rows, members, block_refs)
    low_part = pl.ds(0, work.low_rows)
    key_cols, value_cols = slice(0, HEAD), slice(HEAD, 2 * HEAD)

    def products(keys, queries):
        return lax.dot_general(keys, queries, ROWS_DOT_ROWS, preferred_element_type=jnp.float32)

    tops = []
    for owner, qd_ref in enumerate((own_ref, other_ref)):
        high = work.query_slot(owner, 1)
        scores = products(work.low_keys(key_cols), qd_ref[0, high])
        e_ref[owner, low_part, :] = scores
        dp_ref[owner, low_part, :] = products(work.low_keys(value_cols), qd_ref[1, high])
        top = [jnp.full((1, scores.shape[1]), LOWEST, jnp.float32), jnp.max(scores, axis=0, keepdims=True)]
        for n, half, here, masked in work.tiles(owner):
            slot = work.query_slot(owner, half)
            scores = products(work.keys(n, half, key_cols), qd_ref[0, slot])
            if masked:
                key = lax.broadcasted_iota(jnp.int32, scores.shape, 0)
                query = lax.rem(lax.broadcasted_iota(jnp.int32, (1, scores.shape[1]), 1), rows)
                scores = jnp.where(key <= query, scores, LOWEST)
            e_ref[owner, here, :] = scores
            dp_ref[owner, here, :] = products(work.keys(n, half, value_cols), qd_ref[1, slot])
            most = jnp.max(scores, axis=0, keepdims=True)
            for side in range(2):
                seen = most if masked else pick(half == side, most, LOWEST)
                if not masked or half == side:
                    top[side] = jnp.maximum(top[side], seen)
        tops.append(top)

    for owner, top in enumerate(tops):

        def sums(here, most):
            expon = jnp.exp2((e_ref[owner, here, :] - most) * EXPONENT_SCALE)
            e_ref[owner, here, :] = expon
            return [
                jnp.sum(expon, axis=0, keepdims=True),
                jnp.sum(expon * dp_ref[owner, here, :], axis=0, keepdims=True),
            ]

        zero = jnp.zeros_like(top[0])
        totals = [[zero, zero], sums(low_part, top[1])]
        for n, half, here, masked in work.tiles(owner):
            part = sums(here, top[half] if masked else lax.select(half == 0, top[0], top[1]))
            for side in range(2):
                if not masked or half == side:
                    seen = part if masked else [pick(half == side, one, 0) for one in part]
                    totals[side] = [total + one for total, one in zip(totals[side], seen)]
        for half in range(2):
            base = (2 * owner + half) * 3
            for n, row in enumerate((top[half], *totals[half])):
                out_ref[base + n : base + n + 1, :] = row


def merged(stats_refs, base):
    rows = [ref[base : base + 3, :] for ref in stats_refs]
    top = functools.reduce(jnp.maximum, [part[:1] for part in rows])
    weights = [jnp.exp2((part[:1] - top) * EXPONENT_SCALE) for part in rows]
    total = sum(weight * part[1:2] for weight, part in zip(weights, rows))
    delta = sum(weight * part[2:3] for weight, part in zip(weights, rows))
    return top, total, delta


def merge_kernel(*refs):
    stats_refs, out_ref = refs[:-1], refs[-1]
    for base in range(0, 12, 3):
        for n, row in enumerate(merged(stats_refs, base)):
            out_ref[base + n : base + n + 1, :] = row


def grads_kernel(outer, groups, table_ref, own_ref, other_ref, *refs):
    count = len(groups)
    stats_refs, theirs_ref, refs = refs[:count], refs[count], refs[count + 1 :]
    e_refs, dp_refs, refs = refs[:count], refs[count : 2 * count], refs[2 * count :]
    term_refs, gs_refs = refs[:outer], refs[outer:]
    rows = term_refs[0].shape[0] // 2
    weights, deltas = [[] for _ in groups], []
    for owner in range(2):
        delta = []
        group_weights = [[] for _ in groups]
        for half in range(2):
            base = (2 * owner + half) * 3
            base2 = (2 * (1 - owner) + half) * 3
            mine = merged(stats_refs, base)
            theirs = [theirs_ref[base2 + n : base2 + n + 1, :] for n in range(3)]
            top = jnp.maximum(mine[0], theirs[0])
            w1 = jnp.exp2((mine[0] - top) * EXPONENT_SCALE)
            w2 = jnp.exp2((theirs[0] - top) * EXPONENT_SCALE)
            total = w1 * mine[1] + w2 * theirs[1]
            delta.append((w1 * mine[2] + w2 * theirs[2]) / total)
            for n, stats_ref in enumerate(stats_refs):
                weight = jnp.exp2((stats_ref[base : base + 1, :] - top) * EXPONENT_SCALE)
                group_weights[n].append(weight / total)
        deltas.append(delta)
        for n in range(count):
            weights[n].append(group_weights[n])

    for n, members in enumerate(groups):
        work = Work(table_ref, rows, members, None)
        terms = [[None] * len(members), [None] * len(members)]

        def add(half, at, pair):
            old = terms[half][at]
            terms[half][at] = pair if old is None else [one + more for one, more in zip(old, pair)]

        for owner, qd_ref in enumerate((own_ref, other_ref)):

            def gradients(here, slot, weight, delta):
                probs = e_refs[n][owner, here, :] * weight
                grads = (probs * (dp_refs[n][owner, here, :] - delta)).astype(jnp.bfloat16)
                gs_refs[n][owner, here, :] = grads
                return [
                    jnp.dot(grads, qd_ref[0, slot], preferred_element_type=jnp.float32),
                    jnp.dot(probs.astype(jnp.bfloat16), qd_ref[1, slot], preferred_element_type=jnp.float32),
                ]

            weight, delta = weights[n][owner], deltas[owner]
            low_part = pl.ds(0, work.low_rows)
            part = gradients(low_part, work.query_slot(owner, 1), weight[1], delta[1])
            for at in range(len(members)):
                add(0, at, [one[at * rows : (at + 1) * rows] for one in part])
            for at, half, here, masked in work.tiles(owner):
                slot = work.query_slot(owner, half)
                if masked:
                    add(half, at, gradients(here, slot, weight[half], delta[half]))
                else:
                    is_low = half == 0
                    part = gradients(here, slot, lax.select(is_low, *weight), lax.select(is_low, *delta))
                    for side in range(2):
                        add(side, at, [pick(half == side, one, 0) for one in part])
        for at, d in enumerate(members):
            term_ref = term_refs[d]
            for half in range(2):
                target = work.key_rows(at, half)
                of_keys, of_values = terms[half][at]
                term_ref[target, :HEAD] = (of_keys * SCALE).astype(term_ref.dtype)
                term_ref[target, HEAD:] = of_values.astype(term_ref.dtype)


def query_kernel(outer, groups, owner, table_ref, *refs):
    count = len(groups)
    block_refs, gs_refs, out_ref = refs[:outer], refs[outer : outer + count], refs[-1]
    rows = out_ref.shape[0] // 2
    works = [Work(table_ref, rows, members, [block_refs[d] for d in members]) for members in groups]
    cols = slice(0, HEAD)
    totals = [None, None]

    def add(half, part):
        totals[half] = part if totals[half] is None else totals[half] + part

    for gs_ref, work in zip(gs_refs, works):

        def terms(keys, here):
            return lax.dot_general(
                keys, gs_ref[owner, here, :], COLS_DOT_COLS, preferred_element_type=jnp.float32
            )

        add(1, terms(work.low_keys(cols), pl.ds(0, work.low_rows)))
        for n, half, here, masked in work.tiles(owner):
            part = terms(work.keys(n, half, cols), here)
            for side in range(2):
                if not masked:
                    add(side, pick(half == side, part, 0))
                elif half == side:
                    add(side, part)
    for half in range(2):
        place = at_rows(works[0].query_slot(owner, half) * rows, rows)
        grads = (jnp.transpose(totals[half]) * SCALE).astype(out_ref.dtype)
        for h in range(GROUP):
            out_ref[place, h * HEAD : (h + 1) * HEAD] = grads[h * rows : (h + 1) * rows, :]


def sum_kernel(outer, *refs):
    terms, outs, total_ref = refs[:outer], refs[outer:-1], refs[-1]
    total = terms[0][...]
    for term_ref in terms[1:]:
        total = total + term_ref[...].astype(jnp.float32)
    total_ref[...] = total
    kvh = len(outs)
    rows = outs[0].shape[0]
    for e, out_ref in enumerate(outs):
        target = target_of(lax.axis_index("kvh"), e, kvh)
        out_ref[...] = total_ref[at_rows(target * rows, rows), :].astype(jnp.bfloat16)


def place_kernel(order, own_ref, received_ref, *refs):
    parts, (dq_out, key_out, value_out, dq_ref, sems) = refs[:-5], refs[-5:]
    kvh = len(parts)
    copies = []
    for e, part_ref in zip(order, parts):
        cols = at_rows(partner(lax.axis_index("kvh"), e, kvh) * HEAD, HEAD)
        copies.append(load(part_ref.at[:, pl.ds(0, HEAD)], key_out.at[:, cols], sems.at[2 * e]))
        copies.append(load(part_ref.at[:, pl.ds(HEAD, HEAD)], value_out.at[:, cols], sems.at[2 * e + 1]))
    dq_ref[...] = (own_ref[...] + received_ref[...].astype(jnp.float32)).astype(jnp.bfloat16)
    copies.append(load(dq_ref, dq_out, sems.at[2 * kvh]))
    wait_all(copies)


def per_device(queries, keys, values, d_out, slab_order):
    kvh = lax.axis_size("kvh")
    outer = lax.axis_size("outer")
    local_rows, query_width = queries.shape
    cache_rows = keys.shape[0]
    slab_rows = local_rows // 2
    columns = GROUP * slab_rows
    params = pltpu.CompilerParams(vmem_limit_bytes=(8 << 20) + (10 << 10) * outer * local_rows)
    beside = pl.CostEstimate(flops=2 * 10**10, bytes_accessed=10**6, transcendentals=0)
    vmem = pl.BlockSpec(memory_space=pltpu.VMEM)
    smem = pl.BlockSpec(memory_space=pltpu.SMEM)
    anywhere = pl.BlockSpec(memory_space=pl.ANY)
    shape = jax.ShapeDtypeStruct
    dma = pltpu.SemaphoreType.DMA
    low, full = jnp.bfloat16, jnp.float32

    def call(kernel, name, **arguments):
        return pl.pallas_call(kernel, compiler_params=params, name=name, **arguments)

    def shift(array, axis, by):
        size = lax.axis_size(axis)
        if by > 0:
            return lax.ppermute(array, axis, [(n, target_of(n, by, size)) for n in range(size)])
        return lax.ppermute(array, axis, [(n, partner(n, -by, size)) for n in range(size)])

    order = (0, *range(2, kvh), *range(1, min(kvh, 2)))

    def exchange(parts):
        return [shift(parts[e], "kvh", e) if e > 0 else parts[e] for e in order]

    part = shape((cache_rows, 2 * HEAD), low)
    block = shape((local_rows, 2 * HEAD), low)
    parts = call(
        split_kernel,
        "split",
        out_shape=(part,) * kvh,
        in_specs=[vmem],
        out_specs=(vmem,) * kvh,
        scratch_shapes=[dma((2 * kvh,))],
    )(jnp.concatenate([keys, values], axis=0))
    parts = exchange(parts)
    stack = shape((2, 2, columns, HEAD), low)
    queries2 = shift(queries, "pair", 1)
    own_qd, other_qd = call(
        stack_kernel,
        "stack",
        out_shape=(stack, stack),
        in_specs=[vmem] * 4,
        out_specs=(vmem, vmem),
    )(queries, d_out, queries2, shift(d_out, "pair", 1))
    own_block = call(
        functools.partial(join_kernel, order),
        "join",
        out_shape=block,
        in_specs=[anywhere] * kvh,
        out_specs=vmem,
        scratch_shapes=[dma((kvh,))],
        cost_estimate=beside,
    )(*parts)
    blocks = [own_block] + [shift(own_block, "outer", d) for d in range(1, outer)]

    table = call(
        functools.partial(table_kernel, outer),
        "table",
        out_shape=shape((2 * outer + 4, HEAD), jnp.int32),
        in_specs=[smem, anywhere],
        out_specs=vmem,
    )(slab_order, queries2)
    far = outer // 2 + 1
    groups = [[0, *range(far, outer)], list(range(far - 1, 0, -1))]
    all_stats = shape((12, columns), full)
    results = []
    for n, members in enumerate(groups):
        score_rows = shape((2, (2 * len(members) + 1) * slab_rows, columns), full)
        results.append(
            call(
                functools.partial(stats_kernel, members),
                "stats",
                out_shape=(all_stats, score_rows, score_rows),
                in_specs=[vmem] * (3 + len(members)) + [anywhere] * min(n, 1),
                out_specs=(vmem,) * 3,
                cost_estimate=beside if n + 1 < len(groups) else None,
            )(table, own_qd, other_qd, *[blocks[d] for d in members], *[done[0] for done in results[-1:]])
        )
    stats, expon, grad_probs = zip(*results)
    mine = stats[0]
    if len(stats) > 1:
        mine = call(
            merge_kernel, "merge", out_shape=all_stats, in_specs=[vmem] * len(stats), out_specs=vmem
        )(*stats)
    theirs = shift(mine, "pair", 1)
    count = len(groups)
    grads = call(
        functools.partial(grads_kernel, outer, groups),
        "grads",
        out_shape=(shape(block.shape, full),)
        + (block,) * (outer - 1)
        + tuple(shape(scores.shape, low) for scores in expon),
        in_specs=[vmem] * (4 + 3 * count),
        out_specs=(vmem,) * (outer + count),
    )(table, own_qd, other_qd, *stats, theirs, *expon, *grad_probs)
    terms, score_grads = grads[:outer], grads[outer:]
    terms = [terms[0]] + [shift(terms[d], "outer", -d) for d in range(outer - 1, 0, -1)]
    def query_terms(owner, kind, *after):
        return call(
            functools.partial(query_kernel, outer, groups, owner),
            "query_terms",
            out_shape=shape(queries.shape, kind),
            in_specs=[vmem] * (1 + outer + count) + [anywhere] * len(after),
            out_specs=vmem,
            cost_estimate=beside,
        )(table, *blocks, *score_grads, *after)

    other_grads = query_terms(1, low)
    received_grads = shift(other_grads, "pair", 1)
    own_grads = query_terms(0, full, other_grads)
    owned = call(
        functools.partial(sum_kernel, outer),
        "sum",
        out_shape=(part,) * kvh,
        in_specs=[vmem] * outer,
        out_specs=(vmem,) * kvh,
        scratch_shapes=[pltpu.VMEM(block.shape, full)],
        cost_estimate=beside,
    )(*terms)
    owned = exchange(owned)
    return call(
        functools.partial(place_kernel, order),
        "place",
        out_shape=(shape(queries.shape, low), shape(keys.shape, low), shape(values.shape, low)),
        in_specs=[vmem, vmem] + [anywhere] * kvh,
        out_specs=(anywhere,) * 3,
        scratch_shapes=[pltpu.VMEM(queries.shape, low), dma((2 * kvh + 1,))],
    )(own_grads, received_grads, *owned)


def solution(mesh):
    kvh = mesh.shape["kvh"]
    pairs = mesh.shape["seq"] // 2
    paired = Mesh(mesh.devices.reshape(pairs, 2, kvh), ("outer", "pair", "kvh"))
    seq = ("outer", "pair")
    cache = P(("outer", "pair", "kvh"), None)
    placed = (P(seq, "kvh"), cache, cache, P(seq, "kvh"), P())
    return jax.shard_map(
        per_device,
        mesh=paired,
        in_specs=placed,
        out_specs=(P(seq, "kvh"), cache, cache),
        check_vma=False,
    )
```

```python
import functools
import math

import jax
import jax.numpy as jnp
from jax import lax
from jax.experimental import pallas as pl
from jax.experimental.pallas import tpu as pltpu
from jax.sharding import Mesh
from jax.sharding import PartitionSpec as P

HEADS = 20
KV_HEADS = 4
HEAD = 128
GROUP = HEADS // KV_HEADS
SCALE = HEAD ** (-0.5)
EXPONENT_SCALE = SCALE * math.log2(math.e)
LOWEST = -1e30
ROWS_DOT_ROWS = (((1,), (1,)), ((), ()))
COLS_DOT_COLS = (((0,), (0,)), ((), ()))


def at_rows(start, size):
    return pl.ds(pl.multiple_of(start, size), size)


def load(source_ref, target_ref, sem):
    copy = pltpu.make_async_copy(source_ref, target_ref, sem)
    copy.start()
    return copy


def wait_all(copies):
    for copy in copies:
        copy.wait()


def partner(index, distance, size):
    if size & (size - 1) == 0:
        return index ^ distance
    return (index + size - distance) % size


def target_of(index, distance, size):
    if size & (size - 1) == 0:
        return index ^ distance
    return (index + distance) % size


def pick(condition, chosen, other):
    return lax.select(condition, chosen, jnp.full_like(chosen, other))


class Work:
    def __init__(self, table_ref, rows, members, block_refs):
        self.rows, self.members, self.block_refs = rows, members, block_refs
        self.low_rows = len(members) * rows

        def pair(at):
            return jnp.max(table_ref[2 * at : 2 * at + 1, :]), jnp.max(table_ref[2 * at + 1 : 2 * at + 2, :])

        self.pairs = [pair(d) for d in members]
        self.owners = [pair(table_ref.shape[0] // 2 - 2), pair(table_ref.shape[0] // 2 - 1)]

    @staticmethod
    def slot(place, half):
        return jnp.where(half == 0, place, 1 - place)

    def query_slot(self, owner, half):
        return self.slot(self.owners[owner][1], half)

    def key_rows(self, n, half):
        return at_rows(self.slot(self.pairs[n][1], half) * self.rows, self.rows)

    def keys(self, n, half, cols):
        return self.block_refs[n][self.key_rows(n, half), cols]

    def low_keys(self, cols):
        return jnp.concatenate([self.keys(n, 0, cols) for n in range(len(self.members))], axis=0)

    def tiles(self, owner):
        found = []
        for n, d in enumerate(self.members):
            here = pl.ds(self.low_rows + n * self.rows, self.rows)
            if owner == 0 and d == 0:
                found.append((n, 0, here, True))
                found.append((n, 1, pl.ds(2 * self.low_rows, self.rows), True))
            else:
                half = jnp.where(self.owners[owner][0] >= self.pairs[n][0], 0, 1)
                found.append((n, half, here, False))
        return found


def split_kernel(cache_ref, *refs):
    parts, sems = refs[:-1], refs[-1]
    kvh = len(parts)
    rows = parts[0].shape[0]
    copies = []
    for e, part_ref in enumerate(parts):
        cols = at_rows(target_of(lax.axis_index("kvh"), e, kvh) * HEAD, HEAD)
        for n in range(2):
            source = cache_ref.at[pl.ds(n * rows, rows), cols]
            copies.append(load(source, part_ref.at[:, pl.ds(n * HEAD, HEAD)], sems.at[2 * e + n]))
    wait_all(copies)


def table_kernel(outer, order_ref, after_ref, table_ref):
    at, side = lax.axis_index("outer"), lax.axis_index("pair")
    indices = [2 * partner(at, d, outer) + side for d in range(outer)]
    indices += [2 * at + side, 2 * at + 1 - side]
    for n, index in enumerate(indices):
        first, second = order_ref[2 * index], order_ref[2 * index + 1]
        row = table_ref.shape[1:]
        table_ref[2 * n : 2 * n + 1, :] = jnp.full((1, *row), jnp.minimum(first, second), jnp.int32)
        table_ref[2 * n + 1 : 2 * n + 2, :] = jnp.full((1, *row), jnp.where(first < second, 0, 1), jnp.int32)


def stack_kernel(*refs):
    sources, outs = refs[:4], refs[4:]
    rows = sources[0].shape[0] // 2
    for n, source_ref in enumerate(sources):
        for slot in range(2):
            for h in range(GROUP):
                outs[n // 2][n % 2, slot, h * rows : (h + 1) * rows, :] = source_ref[
                    slot * rows : (slot + 1) * rows, h * HEAD : (h + 1) * HEAD
                ]


def join_kernel(order, *refs):
    parts, (out_ref, sems) = refs[:-2], refs[-2:]
    kvh = len(parts)
    rows = parts[0].shape[0]
    copies = []
    for e, part_ref in zip(order, parts):
        source = partner(lax.axis_index("kvh"), e, kvh)
        copies.append(load(part_ref, out_ref.at[at_rows(source * rows, rows)], sems.at[e]))
    wait_all(copies)


def stats_kernel(members, table_ref, own_ref, other_ref, *refs):
    block_refs, (out_ref, e_ref, dp_ref) = refs[: len(members)], refs[-3:]
    rows = block_refs[0].shape[0] // 2
    work = Work(table_ref, rows, members, block_refs)
    low_part = pl.ds(0, work.low_rows)
    key_cols, value_cols = slice(0, HEAD), slice(HEAD, 2 * HEAD)

    def products(keys, queries):
        return lax.dot_general(keys, queries, ROWS_DOT_ROWS, preferred_element_type=jnp.float32)

    tops = []
    for owner, qd_ref in enumerate((own_ref, other_ref)):
        high = work.query_slot(owner, 1)
        scores = products(work.low_keys(key_cols), qd_ref[0, high])
        e_ref[owner, low_part, :] = scores
        dp_ref[owner, low_part, :] = products(work.low_keys(value_cols), qd_ref[1, high])
        top = [jnp.full((1, scores.shape[1]), LOWEST, jnp.float32), jnp.max(scores, axis=0, keepdims=True)]
        for n, half, here, masked in work.tiles(owner):
            slot = work.query_slot(owner, half)
            scores = products(work.keys(n, half, key_cols), qd_ref[0, slot])
            if masked:
                key = lax.broadcasted_iota(jnp.int32, scores.shape, 0)
                query = lax.rem(lax.broadcasted_iota(jnp.int32, (1, scores.shape[1]), 1), rows)
                scores = jnp.where(key <= query, scores, LOWEST)
            e_ref[owner, here, :] = scores
            dp_ref[owner, here, :] = products(work.keys(n, half, value_cols), qd_ref[1, slot])
            most = jnp.max(scores, axis=0, keepdims=True)
            for side in range(2):
                seen = most if masked else pick(half == side, most, LOWEST)
                if not masked or half == side:
                    top[side] = jnp.maximum(top[side], seen)
        tops.append(top)

    for owner, top in enumerate(tops):

        def sums(here, most):
            expon = jnp.exp2((e_ref[owner, here, :] - most) * EXPONENT_SCALE)
            e_ref[owner, here, :] = expon
            return [
                jnp.sum(expon, axis=0, keepdims=True),
                jnp.sum(expon * dp_ref[owner, here, :], axis=0, keepdims=True),
            ]

        zero = jnp.zeros_like(top[0])
        totals = [[zero, zero], sums(low_part, top[1])]
        for n, half, here, masked in work.tiles(owner):
            part = sums(here, top[half] if masked else lax.select(half == 0, top[0], top[1]))
            for side in range(2):
                if not masked or half == side:
                    seen = part if masked else [pick(half == side, one, 0) for one in part]
                    totals[side] = [total + one for total, one in zip(totals[side], seen)]
        for half in range(2):
            base = (2 * owner + half) * 3
            for n, row in enumerate((top[half], *totals[half])):
                out_ref[base + n : base + n + 1, :] = row


def merged(stats_refs, base):
    rows = [ref[base : base + 3, :] for ref in stats_refs]
    top = functools.reduce(jnp.maximum, [part[:1] for part in rows])
    weights = [jnp.exp2((part[:1] - top) * EXPONENT_SCALE) for part in rows]
    total = sum(weight * part[1:2] for weight, part in zip(weights, rows))
    delta = sum(weight * part[2:3] for weight, part in zip(weights, rows))
    return top, total, delta


def merge_kernel(*refs):
    stats_refs, out_ref = refs[:-1], refs[-1]
    for base in range(0, 12, 3):
        for n, row in enumerate(merged(stats_refs, base)):
            out_ref[base + n : base + n + 1, :] = row


def grads_kernel(outer, groups, table_ref, own_ref, other_ref, *refs):
    count = len(groups)
    stats_refs, theirs_ref, refs = refs[:count], refs[count], refs[count + 1 :]
    e_refs, dp_refs, refs = refs[:count], refs[count : 2 * count], refs[2 * count :]
    term_refs, gs_refs = refs[:outer], refs[outer:]
    rows = term_refs[0].shape[0] // 2
    weights, deltas = [[] for _ in groups], []
    for owner in range(2):
        delta = []
        group_weights = [[] for _ in groups]
        for half in range(2):
            base = (2 * owner + half) * 3
            base2 = (2 * (1 - owner) + half) * 3
            mine = merged(stats_refs, base)
            theirs = [theirs_ref[base2 + n : base2 + n + 1, :] for n in range(3)]
            top = jnp.maximum(mine[0], theirs[0])
            w1 = jnp.exp2((mine[0] - top) * EXPONENT_SCALE)
            w2 = jnp.exp2((theirs[0] - top) * EXPONENT_SCALE)
            total = w1 * mine[1] + w2 * theirs[1]
            delta.append((w1 * mine[2] + w2 * theirs[2]) / total)
            for n, stats_ref in enumerate(stats_refs):
                weight = jnp.exp2((stats_ref[base : base + 1, :] - top) * EXPONENT_SCALE)
                group_weights[n].append(weight / total)
        deltas.append(delta)
        for n in range(count):
            weights[n].append(group_weights[n])

    for n, members in enumerate(groups):
        work = Work(table_ref, rows, members, None)
        terms = [[None] * len(members), [None] * len(members)]

        def add(half, at, pair):
            old = terms[half][at]
            terms[half][at] = pair if old is None else [one + more for one, more in zip(old, pair)]

        for owner, qd_ref in enumerate((own_ref, other_ref)):

            def gradients(here, slot, weight, delta):
                probs = e_refs[n][owner, here, :] * weight
                grads = (probs * (dp_refs[n][owner, here, :] - delta)).astype(jnp.bfloat16)
                gs_refs[n][owner, here, :] = grads
                return [
                    jnp.dot(grads, qd_ref[0, slot], preferred_element_type=jnp.float32),
                    jnp.dot(probs.astype(jnp.bfloat16), qd_ref[1, slot], preferred_element_type=jnp.float32),
                ]

            weight, delta = weights[n][owner], deltas[owner]
            low_part = pl.ds(0, work.low_rows)
            part = gradients(low_part, work.query_slot(owner, 1), weight[1], delta[1])
            for at in range(len(members)):
                add(0, at, [one[at * rows : (at + 1) * rows] for one in part])
            for at, half, here, masked in work.tiles(owner):
                slot = work.query_slot(owner, half)
                if masked:
                    add(half, at, gradients(here, slot, weight[half], delta[half]))
                else:
                    is_low = half == 0
                    part = gradients(here, slot, lax.select(is_low, *weight), lax.select(is_low, *delta))
                    for side in range(2):
                        add(side, at, [pick(half == side, one, 0) for one in part])
        for at, d in enumerate(members):
            term_ref = term_refs[d]
            for half in range(2):
                target = work.key_rows(at, half)
                of_keys, of_values = terms[half][at]
                term_ref[target, :HEAD] = (of_keys * SCALE).astype(term_ref.dtype)
                term_ref[target, HEAD:] = of_values.astype(term_ref.dtype)


def query_kernel(outer, groups, owner, table_ref, *refs):
    count = len(groups)
    block_refs, gs_refs, out_ref = refs[:outer], refs[outer : outer + count], refs[-1]
    rows = out_ref.shape[0] // 2
    works = [Work(table_ref, rows, members, [block_refs[d] for d in members]) for members in groups]
    cols = slice(0, HEAD)
    totals = [None, None]

    def add(half, part):
        totals[half] = part if totals[half] is None else totals[half] + part

    for gs_ref, work in zip(gs_refs, works):

        def terms(keys, here):
            return lax.dot_general(
                keys, gs_ref[owner, here, :], COLS_DOT_COLS, preferred_element_type=jnp.float32
            )

        add(1, terms(work.low_keys(cols), pl.ds(0, work.low_rows)))
        for n, half, here, masked in work.tiles(owner):
            part = terms(work.keys(n, half, cols), here)
            for side in range(2):
                if not masked:
                    add(side, pick(half == side, part, 0))
                elif half == side:
                    add(side, part)
    for half in range(2):
        place = at_rows(works[0].query_slot(owner, half) * rows, rows)
        grads = (jnp.transpose(totals[half]) * SCALE).astype(out_ref.dtype)
        for h in range(GROUP):
            out_ref[place, h * HEAD : (h + 1) * HEAD] = grads[h * rows : (h + 1) * rows, :]


def sum_kernel(outer, *refs):
    terms, outs, total_ref = refs[:outer], refs[outer:-1], refs[-1]
    total = terms[0][...]
    for term_ref in terms[1:]:
        total = total + term_ref[...].astype(jnp.float32)
    total_ref[...] = total
    kvh = len(outs)
    rows = outs[0].shape[0]
    for e, out_ref in enumerate(outs):
        target = target_of(lax.axis_index("kvh"), e, kvh)
        out_ref[...] = total_ref[at_rows(target * rows, rows), :].astype(jnp.bfloat16)


def place_kernel(order, own_ref, received_ref, *refs):
    parts, (dq_out, key_out, value_out, dq_ref, sems) = refs[:-5], refs[-5:]
    kvh = len(parts)
    copies = []
    for e, part_ref in zip(order, parts):
        cols = at_rows(partner(lax.axis_index("kvh"), e, kvh) * HEAD, HEAD)
        copies.append(load(part_ref.at[:, pl.ds(0, HEAD)], key_out.at[:, cols], sems.at[2 * e]))
        copies.append(load(part_ref.at[:, pl.ds(HEAD, HEAD)], value_out.at[:, cols], sems.at[2 * e + 1]))
    dq_ref[...] = (own_ref[...] + received_ref[...].astype(jnp.float32)).astype(jnp.bfloat16)
    copies.append(load(dq_ref, dq_out, sems.at[2 * kvh]))
    wait_all(copies)


def per_device(queries, keys, values, d_out, slab_order):
    kvh = lax.axis_size("kvh")
    outer = lax.axis_size("outer")
    local_rows, query_width = queries.shape
    cache_rows = keys.shape[0]
    slab_rows = local_rows // 2
    columns = GROUP * slab_rows
    params = pltpu.CompilerParams(vmem_limit_bytes=(8 << 20) + (10 << 10) * outer * local_rows)
    beside = pl.CostEstimate(flops=2 * 10**10, bytes_accessed=10**6, transcendentals=0)
    vmem = pl.BlockSpec(memory_space=pltpu.VMEM)
    smem = pl.BlockSpec(memory_space=pltpu.SMEM)
    anywhere = pl.BlockSpec(memory_space=pl.ANY)
    shape = jax.ShapeDtypeStruct
    dma = pltpu.SemaphoreType.DMA
    low, full = jnp.bfloat16, jnp.float32

    def call(kernel, name, **arguments):
        return pl.pallas_call(kernel, compiler_params=params, name=name, **arguments)

    def shift(array, axis, by):
        size = lax.axis_size(axis)
        if by > 0:
            return lax.ppermute(array, axis, [(n, target_of(n, by, size)) for n in range(size)])
        return lax.ppermute(array, axis, [(n, partner(n, -by, size)) for n in range(size)])

    order = (0, *range(2, kvh), *range(1, min(kvh, 2)))

    def exchange(parts):
        return [shift(parts[e], "kvh", e) if e > 0 else parts[e] for e in order]

    part = shape((cache_rows, 2 * HEAD), low)
    block = shape((local_rows, 2 * HEAD), low)
    parts = call(
        split_kernel,
        "split",
        out_shape=(part,) * kvh,
        in_specs=[vmem],
        out_specs=(vmem,) * kvh,
        scratch_shapes=[dma((2 * kvh,))],
    )(jnp.concatenate([keys, values], axis=0))
    parts = exchange(parts)
    stack = shape((2, 2, columns, HEAD), low)
    queries2 = shift(queries, "pair", 1)
    own_block = call(
        functools.partial(join_kernel, order),
        "join",
        out_shape=block,
        in_specs=[anywhere] * kvh,
        out_specs=vmem,
        scratch_shapes=[dma((kvh,))],
        cost_estimate=beside,
    )(*parts)
    late_d_out, own_block = lax.optimization_barrier((d_out, own_block))
    own_qd, other_qd = call(
        stack_kernel,
        "stack",
        out_shape=(stack, stack),
        in_specs=[vmem] * 4,
        out_specs=(vmem, vmem),
    )(queries, d_out, queries2, shift(late_d_out, "pair", 1))
    blocks = [own_block] + [shift(own_block, "outer", d) for d in range(1, outer)]

    table = call(
        functools.partial(table_kernel, outer),
        "table",
        out_shape=shape((2 * outer + 4, HEAD), jnp.int32),
        in_specs=[smem, anywhere],
        out_specs=vmem,
    )(slab_order, queries2)
    far = outer // 2 + 1
    groups = [[0, *range(far, outer)], list(range(far - 1, 0, -1))]
    all_stats = shape((12, columns), full)
    results = []
    for n, members in enumerate(groups):
        score_rows = shape((2, (2 * len(members) + 1) * slab_rows, columns), full)
        results.append(
            call(
                functools.partial(stats_kernel, members),
                "stats",
                out_shape=(all_stats, score_rows, score_rows),
                in_specs=[vmem] * (3 + len(members)) + [anywhere] * min(n, 1),
                out_specs=(vmem,) * 3,
                cost_estimate=beside if n + 1 < len(groups) else None,
            )(table, own_qd, other_qd, *[blocks[d] for d in members], *[done[0] for done in results[-1:]])
        )
    stats, expon, grad_probs = zip(*results)
    mine = stats[0]
    if len(stats) > 1:
        mine = call(
            merge_kernel, "merge", out_shape=all_stats, in_specs=[vmem] * len(stats), out_specs=vmem
        )(*stats)
    theirs = shift(mine, "pair", 1)
    count = len(groups)
    grads = call(
        functools.partial(grads_kernel, outer, groups),
        "grads",
        out_shape=(shape(block.shape, full),)
        + (block,) * (outer - 1)
        + tuple(shape(scores.shape, low) for scores in expon),
        in_specs=[vmem] * (4 + 3 * count),
        out_specs=(vmem,) * (outer + count),
    )(table, own_qd, other_qd, *stats, theirs, *expon, *grad_probs)
    terms, score_grads = grads[:outer], grads[outer:]
    terms = [terms[0]] + [shift(terms[d], "outer", -d) for d in range(outer - 1, 0, -1)]
    def query_terms(owner, kind, *after):
        return call(
            functools.partial(query_kernel, outer, groups, owner),
            "query_terms",
            out_shape=shape(queries.shape, kind),
            in_specs=[vmem] * (1 + outer + count) + [anywhere] * len(after),
            out_specs=vmem,
            cost_estimate=beside,
        )(table, *blocks, *score_grads, *after)

    other_grads = query_terms(1, low)
    received_grads = shift(other_grads, "pair", 1)
    own_grads = query_terms(0, full, other_grads)
    owned = call(
        functools.partial(sum_kernel, outer),
        "sum",
        out_shape=(part,) * kvh,
        in_specs=[vmem] * outer,
        out_specs=(vmem,) * kvh,
        scratch_shapes=[pltpu.VMEM(block.shape, full)],
        cost_estimate=beside,
    )(*terms)
    owned = exchange(owned)
    return call(
        functools.partial(place_kernel, order),
        "place",
        out_shape=(shape(queries.shape, low), shape(keys.shape, low), shape(values.shape, low)),
        in_specs=[vmem, vmem] + [anywhere] * kvh,
        out_specs=(anywhere,) * 3,
        scratch_shapes=[pltpu.VMEM(queries.shape, low), dma((2 * kvh + 1,))],
    )(own_grads, received_grads, *owned)


def solution(mesh):
    kvh = mesh.shape["kvh"]
    pairs = mesh.shape["seq"] // 2
    paired = Mesh(mesh.devices.reshape(pairs, 2, kvh), ("outer", "pair", "kvh"))
    seq = ("outer", "pair")
    cache = P(("outer", "pair", "kvh"), None)
    placed = (P(seq, "kvh"), cache, cache, P(seq, "kvh"), P())
    return jax.shard_map(
        per_device,
        mesh=paired,
        in_specs=placed,
        out_specs=(P(seq, "kvh"), cache, cache),
        check_vma=False,
    )
```
